32 devices in a mesh: dp: 32 (over z, y, x, core).
Axes of the slice: x: 2, y: 2, z: 4, core: 2. Of those that a mesh axis runs over, the one named last changes fastest.
Arguments:
- tokens: bfloat16 [49152, 768], P('dp'), may hold values from -6 to 6
- lengths: int32 [192], P('dp'), may hold values from 64 to 256, as said below
- w_qkv: bfloat16 [768, 2304], P('dp'), may hold values from -0.21875 to 0.21875
- w_out: bfloat16 [768, 768], P('dp'), may hold values from -1.75 to 1.75
- w_in: bfloat16 [768, 3072], P('dp'), may hold values from -0.21875 to 0.21875
- w_down: bfloat16 [768, 3072], P('dp'), may hold values from -0.109375 to 0.109375
- vector: bfloat16 [9216], P('dp'), may hold values from -3 to 3
- key_qkv: float32 [768, 2304], P('dp'), may hold values from -0.21875 to 0.21875
- key_out: float32 [768, 768], P('dp'), may hold values from -1.75 to 1.75
- key_in: float32 [768, 3072], P('dp'), may hold values from -0.21875 to 0.21875
- key_down: float32 [768, 3072], P('dp'), may hold values from -0.109375 to 0.109375
- key_vector: float32 [9216], P('dp'), may hold values from -3 to 3
- cotangent: bfloat16 [49152, 768], P('dp'), may hold values from -6 to 6
Outputs:
- output: bfloat16 [49152, 768], P('dp')
- grad_tokens: float32 [49152, 768], P('dp')
- grad_qkv: float32 [768, 2304], P('dp')
- grad_out: float32 [768, 768], P('dp')
- grad_in: float32 [768, 3072], P('dp')
- grad_down: float32 [768, 3072], P('dp')
- grad_vector: float32 [9216], P('dp')
- key_delta_qkv: float32 [768, 2304], P('dp')
- key_delta_out: float32 [768, 768], P('dp')
- key_delta_in: float32 [768, 3072], P('dp')
- key_delta_down: float32 [768, 3072], P('dp')
- key_delta_vector: float32 [9216], P('dp')
The draws below stay inside these ranges and needn't reach their ends.
Inputs may be any that keep to these rules, and one draw needn't show every extreme that they name: `lengths`: each crop holds its tokens at the head of its 256 slots; some crop holds exactly 256.
All inputs are finite; a program needn't handle non-finite values.
Results may differ from the reference program's by a relative error of at most 0.012.
The reference program's roundings to bfloat16 on the way count: a program that leaves them out, or rounds other values in their place, can miss the bound.
Values may be sent and summed in bfloat16 or wider, within the bound.
No kernel may reach another device: no remote copies, remote signals or barrier semaphores. Data moves between devices by JAX's collectives and lax.ppermute only.
A program may use at most 192 MiB of HBM per device.

```python
import math
import jax
import jax.numpy as jnp
from jax import lax

D = 768
H = 12
FF = 3072
HD = 64
SLOT = 256
MIN_LEN = 64
CROPS = 192
TOKENS = 49152
VEC = 9216


def draw_lengths(key, part):
    key = jax.random.fold_in(key, 7)
    draw_key, pick_key = jax.random.split(key)
    lengths_drawn = jax.random.randint(draw_key, (CROPS,), MIN_LEN, SLOT + 1)
    chosen = jax.random.randint(pick_key, (), 0, CROPS)
    return jnp.where(jnp.arange(CROPS) == chosen, SLOT, lengths_drawn).astype(jnp.int32)


def with_spikes(values, stream_key, source, target, shards_of, factor):
    def block_of(dim):
        return (jnp.arange(values.shape[dim]) // (values.shape[dim] // shards_of)).reshape((-1,) + (1,) * (values.ndim - 1 - dim))

    first = jax.random.permutation(stream_key, shards_of)[block_of(target)]
    other_side = (block_of(target) + shards_of // 2) % shards_of
    return jnp.where((block_of(source) == first) | (block_of(source) == other_side), factor * values, values)


def levels(own_key, shape, shards, least, high):
    def one(dim, blocks):
        draws = jax.random.uniform(jax.random.fold_in(jax.random.fold_in(own_key, 6), dim), (blocks,), jnp.float32, least / len(shards), high / len(shards))
        return jnp.repeat(jnp.exp(draws), shape[dim] // blocks).reshape((-1,) + (1,) * (len(shape) - dim - 1))

    gain = one(*shards[0])
    for cut in shards[1:]:
        gain = gain * one(*cut)
    return gain


def scatter_about(stream_key, shape, width, most, cuts=(), kind=jnp.bfloat16):
    loudness = levels(stream_key, shape, cuts, -0.22, 0.18) if cuts else 1.0
    drawn = jax.random.normal(stream_key, shape, jnp.float32) * width * loudness
    return jnp.minimum(jnp.maximum(drawn, -most), most).astype(kind)


def noise_with(stream_key, dims, width, most, shards, heavy, kind=jnp.bfloat16):
    array = width * jax.random.normal(stream_key, dims, jnp.float32)
    if shards:
        array = array * levels(stream_key, dims, shards, -0.22, 0.18)
    return jnp.clip(with_spikes(array, jax.random.fold_in(stream_key, 3), *heavy), -most, most).astype(kind)


def setup_inputs(seed: int = 0) -> dict:
    streams_of = jax.random.split(jax.random.key(seed), 14)
    return {
        "tokens": noise_with(streams_of[0], (TOKENS, D), 1.0, 6.0, ((0, 32),), (0, 1, 32, 2.75)),
        "lengths": draw_lengths(jax.random.fold_in(streams_of[13], 71), 0),
        "w_qkv": scatter_about(streams_of[2], (D, 3 * D), D ** -0.5, 0.21875, ((0, 32),)),
        "w_out": scatter_about(streams_of[3], (D, D), (D // 64) ** -0.5, 1.75, ((0, 32),)),
        "w_in": scatter_about(streams_of[4], (D, FF), D ** -0.5, 0.21875, ((0, 32),)),
        "w_down": scatter_about(streams_of[5], (D, FF), FF ** -0.5, 0.109375, ((0, 32),)),
        "vector": scatter_about(streams_of[6], (VEC,), 0.3, 3.0, ((0, 32),)),
        "key_qkv": scatter_about(streams_of[7], (D, 3 * D), D ** -0.5, 0.21875, ((0, 32),), jnp.float32),
        "key_out": scatter_about(streams_of[8], (D, D), (D // 64) ** -0.5, 1.75, ((0, 32),), jnp.float32),
        "key_in": scatter_about(streams_of[9], (D, FF), D ** -0.5, 0.21875, ((0, 32),), jnp.float32),
        "key_down": scatter_about(streams_of[10], (D, FF), FF ** -0.5, 0.109375, ((0, 32),), jnp.float32),
        "key_vector": scatter_about(streams_of[11], (VEC,), 0.3, 3.0, ((0, 32),), jnp.float32),
        "cotangent": noise_with(streams_of[12], (TOKENS, D), 1.0, 6.0, ((0, 32),), (0, 1, 32, 2.75)),
    }


@jax.custom_vjp
def low(v):
    return lax.optimization_barrier(v.astype(jnp.bfloat16)).astype(jnp.float32)

@jax.custom_vjp
def low_back(v):
    return v

def low_keep(v):
    return (low(v), None)

def low_pass(kept, grad):
    return (grad,)

def back_keep(v):
    return (v, None)

def back_low(kept, grad):
    return (low(grad),)
low.defvjp(low_keep, low_pass)
low_back.defvjp(back_keep, back_low)
epsilon = 1e-12
highest = lax.Precision.HIGHEST

def product(left_side, right_side):
    return jnp.dot(left_side, right_side, precision=highest)

def vector_piece(vector, number):
    return vector[number * D:(number + 1) * D]

def layer_norm(residual, gain_row, offset):
    center = residual - lax.optimization_barrier(jnp.mean(residual, axis=-1, keepdims=True))
    variance = lax.optimization_barrier(jnp.mean(center * center, axis=-1, keepdims=True))
    return center * lax.rsqrt(variance + epsilon) * gain_row + offset

def block_layer(inputs, crop_len, w_qkv, w_out, w_in, w_down, vector):
    crop_total = inputs.shape[0]
    flat_rows = inputs.reshape(crop_total * SLOT, D)
    bias_qkv = jnp.concatenate([vector_piece(vector, 0), jnp.zeros((D,), vector.dtype), vector_piece(vector, 1)])
    qkv = low(low_back(product(flat_rows, w_qkv) + bias_qkv))
    split_qkv = qkv.reshape(crop_total, SLOT, 3, H, HD)
    queries = split_qkv[:, :, 0]
    key_rows = split_qkv[:, :, 1]
    value_rows = split_qkv[:, :, 2]
    raw_scores = jnp.einsum('cqhd,ckhd->chqk', queries, key_rows, precision=highest) * HD ** (-0.5)
    scores = low_back(raw_scores)
    usable = jnp.arange(SLOT)[None, :] < crop_len[:, None]
    scores = jnp.where(usable[:, None, None, :], scores, -1e+30)
    weights = low(jax.nn.softmax(scores, axis=-1))
    attended = jnp.einsum('chqk,ckhd->cqhd', weights, value_rows, precision=highest).reshape(crop_total * SLOT, D)
    attended = low(low_back(attended))
    branch = low_back(product(attended, w_out) + vector_piece(vector, 2))
    normed = layer_norm(flat_rows + branch, 1.0 + vector_piece(vector, 3), vector_piece(vector, 4))
    hidden = low_back(product(low(normed), w_in) + vector[8 * D:])
    active = low(jax.nn.gelu(hidden, approximate=False))
    feed_out = low_back(product(active, w_down.T) + vector_piece(vector, 7))
    output = layer_norm(normed + feed_out, 1.0 + vector_piece(vector, 5), vector_piece(vector, 6))
    return output.reshape(crop_total, SLOT, D)

def reference(tokens, lengths, w_qkv, w_out, w_in, w_down, vector, key_qkv, key_out, key_in, key_down, key_vector, cotangent):
    group_size = math.gcd(CROPS, max(1, 4096 // SLOT))
    block_count = CROPS // group_size
    params = tuple((matrix.astype(jnp.float32) for matrix in (w_qkv, w_out, w_in, w_down, vector)))

    def forward(inputs, p_qkv, p_out, p_in, p_down, p_vector):
        blocks = inputs.reshape(block_count, group_size, SLOT, D)
        crop_blocks = lengths.reshape(block_count, group_size)

        def run_block(couple):
            return block_layer(couple[0], couple[1], p_qkv, p_out, p_in, p_down, p_vector)
        result = lax.map(jax.checkpoint(run_block), (blocks, crop_blocks))
        return result.reshape(CROPS * SLOT, D)
    output, pullback = jax.vjp(forward, tokens.astype(jnp.float32), *params)
    gradients = pullback(cotangent.astype(jnp.float32))
    deltas = tuple(((matrix - key_arr) * 0.0005 for key_arr, matrix in zip((key_qkv, key_out, key_in, key_down, key_vector), params)))
    return (output.astype(jnp.bfloat16), gradients[0], gradients[1], gradients[2], gradients[3], gradients[4], gradients[5], deltas[0], deltas[1], deltas[2], deltas[3], deltas[4])
```

```python
import functools

import jax
import jax.numpy as jnp
import numpy as np
from jax import lax
from jax.experimental import pallas as pl
from jax.experimental.pallas import tpu as pltpu
from jax.sharding import PartitionSpec as P

H = 12
EPS = 1e-12
EXT = 128
bf16 = jnp.bfloat16
f32 = jnp.float32
VMEM_LIMIT = 60 * 1024 * 1024
ANY = pl.BlockSpec(memory_space=pl.ANY)

NT = (((1,), (1,)), ((), ()))
TN = (((0,), (0,)), ((), ()))


def mm(a, b):
    return jnp.dot(a, b, preferred_element_type=f32)


def mm_nt(a, b):
    return lax.dot_general(a, b, NT, preferred_element_type=f32)


def mm_tn(a, b):
    return lax.dot_general(a, b, TN, preferred_element_type=f32)


def row_mean(v):
    return jnp.mean(v, axis=-1, keepdims=True)


def fold_rows(v):
    return jnp.sum(v.reshape(v.shape[0] // 8, 8, v.shape[1]), axis=0)


def chip_row(info, a, k, sign):
    x, y, z = info[1], info[2], info[3]
    xx = x ^ (a & 1)
    yy = y ^ (a >> 1)
    zz = (z + sign * k + 4) & 3
    return pl.multiple_of(((zz * 2 + yy) * 2 + xx) * 48, 16)


def weight_copies(info, refs, w, sems):
    if len(refs) == 1:
        return [pltpu.make_async_copy(refs[0], w, sems.at[0])]
    out = []
    places = (
        [(0, k) for k in range(4)],
        [(1, k) for k in range(4)],
        [(2, k) for k in range(4)],
        [(3, 0), (3, 1)],
        [(3, 2), (3, 3)],
    )
    for source in range(2):
        half = info[0] if source == 0 else 1 - info[0]
        for number, slots in enumerate(places):
            ref = refs[source * 5 + number]
            for j, (a, k) in enumerate(slots):
                row = chip_row(info, a, k, -1)
                out.append(
                    pltpu.make_async_copy(
                        ref.at[pl.ds(48 * j, 48)],
                        w.at[half, pl.ds(row, 48)],
                        sems.at[len(out)],
                    )
                )
    return out


def sem_count(pieces):
    return 1 if len(pieces) == 1 else 32


def attention_forward(n_src, has_ext, pairs, info, x_ref, *refs):
    src = refs[:n_src]
    if has_ext:
        spread_ref, pick_ref = refs[n_src : n_src + 2]
        refs = refs[n_src + 2 :]
    else:
        vec_in = refs[n_src]
        refs = refs[n_src + 1 :]
    vec_ref, qkv_ref, p_ref, a_ref, w, bias, sems = refs
    crop = pl.program_id(0)
    half_width = pairs * 128

    @pl.when(crop == 0)
    def _():
        copies = weight_copies(info, src, w, sems)
        for copy in copies:
            copy.start()
        for copy in copies:
            copy.wait()
        if has_ext:
            spread = mm(w[0, :, 3 * half_width :], spread_ref[...])
            groups = spread.shape[0] // 64
            picked = spread.reshape(groups, 64, spread.shape[1]) * pick_ref[...][None]
            vec_ref[0:groups, :] = jnp.sum(picked, axis=1)
        else:
            vec_ref[...] = vec_in[...]
        for h in range(2):
            for part, row in ((0, 0), (2, 1)):
                bias[h, :, part * half_width : (part + 1) * half_width] = vec_ref[
                    row : row + 1, h * half_width : (h + 1) * half_width
                ]
            bias[h, :, half_width : 2 * half_width] = jnp.zeros((1, half_width), f32)

    x = x_ref[...]
    slots = x.shape[0]
    length = info[4 + crop]
    usable = lax.broadcasted_iota(jnp.int32, (1, slots), 1) < length
    mask_row = jnp.where(usable, 0.0, -1e30).astype(f32)
    lane = lax.broadcasted_iota(jnp.int32, (1, 128), 1)
    sides = (
        jnp.where(lane < 64, 1.0, 0.0).astype(bf16),
        jnp.where(lane < 64, 0.0, 1.0).astype(bf16),
    )
    for h in range(2):
        qkv = (mm(x, w[h, :, : 3 * half_width]) + bias[h]).astype(bf16)
        qkv_ref[h] = qkv
        for p in range(pairs):
            q2 = qkv[:, p * 128 : (p + 1) * 128] * jnp.asarray(0.125, bf16)
            k2 = qkv[:, half_width + p * 128 : half_width + (p + 1) * 128]
            v2 = qkv[:, 2 * half_width + p * 128 : 2 * half_width + (p + 1) * 128]
            total = None
            for side in range(2):
                scores = mm_nt(q2, k2 * sides[side]) + mask_row
                top = jnp.max(scores, axis=1, keepdims=True)
                terms = jnp.exp(scores - top)
                mass = jnp.sum(terms, axis=1, keepdims=True)
                probs = (terms * (1.0 / mass)).astype(bf16)
                p_ref[h, 0, p * 2 + side] = probs
                part = mm(probs, v2 * sides[side])
                total = part if total is None else total + part
            a_ref[:, h * half_width + p * 128 : h * half_width + (p + 1) * 128] = (
                total.astype(bf16)
            )


def attention_backward(pairs, info, qkv_ref, da_ref, p_ref, out_ref, sums_ref):
    half_width = pairs * 128
    lane = lax.broadcasted_iota(jnp.int32, (1, 128), 1)
    sides = (
        jnp.where(lane < 64, 1.0, 0.0).astype(bf16),
        jnp.where(lane < 64, 0.0, 1.0).astype(bf16),
    )
    scale = jnp.asarray(0.125, f32)

    @pl.when(pl.program_id(0) == 0)
    def _():
        sums_ref[...] = jnp.zeros_like(sums_ref)

    for p in range(pairs):
        at = [part * half_width + p * 128 for part in range(3)]
        q2, k2, v2 = [qkv_ref[0, :, lo : lo + 128] for lo in at]
        da2 = da_ref[:, p * 128 : (p + 1) * 128]
        dq = dk = dv = None
        for side in range(2):
            probs_b = p_ref[0, 0, p * 2 + side]
            probs = probs_b.astype(f32)
            d_probs = mm_nt(da2, v2 * sides[side])
            inner = jnp.sum(probs * d_probs, axis=1, keepdims=True)
            d_scores = (probs * (d_probs - inner)).astype(bf16)
            part_v = mm_tn(probs_b, da2 * sides[side])
            part_q = mm(d_scores, k2 * sides[side])
            part_k = mm_tn(d_scores, q2 * sides[side])
            dv = part_v if dv is None else dv + part_v
            dq = part_q if dq is None else dq + part_q
            dk = part_k if dk is None else dk + part_k
        for lo, value in zip(at, (dq * scale, dk * scale, dv)):
            rounded = value.astype(bf16)
            out_ref[0, :, lo : lo + 128] = rounded
            sums_ref[:, lo : lo + 128] += fold_rows(rounded.astype(f32))


def gelu_parts(u):
    size = jnp.abs(u)
    t = 1.0 / (1.0 + size * (0.3275911 * 0.7071067811865476))
    bell = jnp.exp(u * u * -0.5)
    poly = t * (
        0.127414796
        + t * (-0.142248368 + t * (0.7107068705 + t * (-0.7265760135 + t * 0.5307027145)))
    )
    tail = poly * bell
    cdf = jnp.where(u < 0.0, tail, 1.0 - tail)
    return u * cdf, cdf + u * (bell * 0.3989422804014327)


def feed_forward(n_a, n_b, info, vec_ref, x_ref, a_ref, cot_ref, *refs):
    src_a = refs[:n_a]
    src_b = refs[n_a : n_a + n_b]
    (
        out_ref,
        g_ref,
        slope_ref,
        n1_ref,
        z1_ref,
        rstd_ref,
        dr2_ref,
        df_ref,
        sums_ref,
        wa,
        wb,
        sems_a,
        sems_b,
    ) = refs[n_a + n_b :]
    step = pl.program_id(0)
    width = x_ref.shape[1]
    half = width // 2
    copies_a = weight_copies(info, src_a, wa, sems_a)
    copies_b = weight_copies(info, src_b, wb, sems_b)

    @pl.when(step == 0)
    def _():
        for copy in copies_a + copies_b:
            copy.start()
        sums_ref[...] = jnp.zeros_like(sums_ref)
        for copy in copies_a:
            copy.wait()

    attended = a_ref[...]
    branch = jnp.concatenate(
        [mm(attended, wa[h, :, :half]) for h in range(2)], axis=1
    ) + vec_ref[2:3, :]
    resid = x_ref[...].astype(f32) + branch
    center = resid - row_mean(resid)
    rstd = lax.rsqrt(row_mean(center * center) + EPS)
    z1 = center * rstd
    z1_ref[...] = z1
    rstd_ref[...] = rstd
    n1 = z1 * (1.0 + vec_ref[3:4, :]) + vec_ref[4:5, :]
    n1b = n1.astype(bf16)
    n1_ref[...] = n1b

    @pl.when(step == 0)
    def _():
        for copy in copies_b:
            copy.wait()

    feed = None
    for j in range(4):
        h, lo = j // 2, (j % 2) * width
        u = mm(n1b, wa[h, :, half + lo : half + lo + width]) + vec_ref[8 + j : 9 + j, :]
        active, slope = gelu_parts(u)
        active = active.astype(bf16)
        g_ref[:, j * width : (j + 1) * width] = active
        slope_ref[:, j * width : (j + 1) * width] = slope.astype(bf16)
        part = mm_nt(active, wb[h, :, lo : lo + width])
        feed = part if feed is None else feed + part
    resid2 = n1 + feed + vec_ref[7:8, :]
    center2 = resid2 - row_mean(resid2)
    rstd2 = lax.rsqrt(row_mean(center2 * center2) + EPS)
    z2 = center2 * rstd2
    gain2 = 1.0 + vec_ref[5:6, :]
    out_ref[...] = (z2 * gain2 + vec_ref[6:7, :]).astype(bf16)
    dy = cot_ref[...].astype(f32)
    s = dy * gain2
    dr2 = rstd2 * (s - row_mean(s) - z2 * row_mean(s * z2))
    dr2_ref[...] = dr2
    df = dr2.astype(bf16)
    df_ref[...] = df
    sums_ref[0] += fold_rows(dy * z2)
    sums_ref[1] += fold_rows(dy)
    sums_ref[2] += fold_rows(df.astype(f32))


def feed_backward(n_a, n_b, info, vec_ref, df_ref, slope_ref, dr2_ref, z1_ref, rstd_ref, *refs):
    src_a = refs[:n_a]
    src_b = refs[n_a : n_a + n_b]
    (
        du_ref,
        dr1_ref,
        db_ref,
        da_ref,
        sums_ref,
        sums_b1_ref,
        wa,
        wb,
        sems_a,
        sems_b,
    ) = refs[n_a + n_b :]
    step = pl.program_id(0)
    width = df_ref.shape[1]
    half = width // 2
    copies_a = weight_copies(info, src_a, wa, sems_a)
    copies_b = weight_copies(info, src_b, wb, sems_b)

    @pl.when(step == 0)
    def _():
        for copy in copies_b + copies_a:
            copy.start()
        sums_ref[...] = jnp.zeros_like(sums_ref)
        sums_b1_ref[...] = jnp.zeros_like(sums_b1_ref)
        for copy in copies_b + copies_a:
            copy.wait()

    df = df_ref[...]
    dn1 = dr2_ref[...]
    for j in range(4):
        h, lo = j // 2, (j % 2) * width
        cut = slice(j * width, (j + 1) * width)
        d_active = mm(df, wb[h, :, lo : lo + width])
        du = (d_active * slope_ref[:, cut].astype(f32)).astype(bf16)
        du_ref[:, cut] = du
        sums_b1_ref[j] += fold_rows(du.astype(f32))
        dn1 = dn1 + mm_nt(du, wa[h, :, half + lo : half + lo + width])
    z1 = z1_ref[...]
    sums_ref[0] += fold_rows(dn1 * z1)
    sums_ref[1] += fold_rows(dn1)
    s = dn1 * (1.0 + vec_ref[3:4, :])
    dr1 = rstd_ref[...] * (s - row_mean(s) - z1 * row_mean(s * z1))
    dr1_ref[...] = dr1
    db = dr1.astype(bf16)
    db_ref[...] = db
    sums_ref[2] += fold_rows(db.astype(f32))
    da = mm_nt(db[:, :half], wa[0, :, :half]) + mm_nt(db[:, half:], wa[1, :, :half])
    da_ref[...] = da.astype(bf16)


def token_gradient(n_src, info, dqkv_ref, dr1_ref, *refs):
    src = refs[:n_src]
    out_ref, w, sems = refs[n_src:]
    used = dqkv_ref.shape[2]

    @pl.when(pl.program_id(0) == 0)
    def _():
        copies = weight_copies(info, src, w, sems)
        for copy in copies:
            copy.start()
        for copy in copies:
            copy.wait()

    out_ref[...] = (
        dr1_ref[...]
        + mm_nt(dqkv_ref[0], w[0, :, :used])
        + mm_nt(dqkv_ref[1], w[1, :, :used])
    )


def weight_gradient(starts, block, has_recv, n_out, ext_at, info, *refs):
    count = len(starts)
    lhs = refs[:count]
    rhs = refs[count : 2 * count]
    at = 2 * count
    recv = None
    ext = None
    if has_recv:
        recv = refs[at]
        at += 1
    if ext_at is not None:
        ext = refs[at]
        at += 1
    outs = refs[at : at + n_out]
    left, acc = refs[at + n_out :]
    step = pl.program_id(0)

    def store(value, lo, size):
        if n_out == 1:
            outs[0][:, pl.ds(lo, size)] = value.astype(outs[0].dtype)
            return
        acc[:, :size] = value
        for a in range(4):
            for k in range(4):
                row = chip_row(info, a, k, 1)
                mine = acc[pl.ds(row, 48), :size]
                theirs = recv[pl.ds(row, 48), pl.ds(lo, size)].astype(f32)
                outs[a][k, :, pl.ds(lo, size)] = (mine + theirs).astype(bf16)

    for number, start in enumerate(starts):
        stop = starts[number + 1] if number + 1 < count else None

        @pl.when(step == start)
        def _(number=number):
            left[...] = lhs[number][...].T

        here = step >= start
        if stop is not None:
            here = here & (step < stop)

        @pl.when(here)
        def _(number=number):
            right = rhs[number]
            right = right[0] if len(right.shape) == 3 else right[...]
            store(mm(left[...], right), pl.multiple_of(step * block, 128), block)

    if ext_at is not None:

        @pl.when(step == pl.num_programs(0) - 1)
        def _():
            store(ext[...].astype(f32), ext_at, EXT)


def params():
    return pltpu.CompilerParams(
        dimension_semantics=("arbitrary",), vmem_limit_bytes=VMEM_LIMIT
    )


def call(kernel, grid, in_specs, out_specs, out_shape, scratch, flops, nbytes, name):
    return pl.pallas_call(
        kernel,
        grid_spec=pltpu.PrefetchScalarGridSpec(
            num_scalar_prefetch=1,
            grid=grid,
            in_specs=in_specs,
            out_specs=out_specs,
            scratch_shapes=scratch,
        ),
        out_shape=out_shape,
        compiler_params=params(),
        cost_estimate=pl.CostEstimate(
            flops=int(flops), bytes_accessed=int(nbytes), transcendentals=0
        ),
        name=name,
    )


def struct(shape, dtype):
    return jax.ShapeDtypeStruct(shape, dtype)


def whole_block(shape):
    return pl.BlockSpec(shape, lambda i, info: (0,) * len(shape))


def rows_block(rows, columns):
    return pl.BlockSpec((rows, columns), lambda i, info: (i, 0))


def spread_tables(width):
    per = width // 64
    e = np.arange(width)
    spread = (np.arange(EXT)[:, None] == (e % per)[None, :]).astype(np.float32)
    pick = (np.arange(64)[:, None] == (e // per)[None, :]).astype(np.float32)
    return spread, pick


def run_attention_forward(info, x, pieces, vec, crops):
    rows, width = x.shape
    slots = rows // crops
    half = width // 2
    w_columns = pieces[0].shape[-1]
    has_ext = vec is None
    pairs = half // 128
    if has_ext:
        spread, pick = spread_tables(width)
        extra = [jnp.asarray(spread, bf16), jnp.asarray(pick, f32)]
    else:
        extra = [vec]
    extra_specs = [whole_block(e.shape) for e in extra]
    kernel = functools.partial(attention_forward, len(pieces), has_ext, pairs)
    return call(
        kernel,
        (crops,),
        [rows_block(slots, width)] + [ANY] * len(pieces) + extra_specs,
        [
            whole_block((16, width)),
            pl.BlockSpec((2, slots, 3 * half), lambda i, info: (0, i, 0)),
            pl.BlockSpec((2, 1, H // 2, slots, slots), lambda i, info: (0, i, 0, 0, 0)),
            rows_block(slots, width),
        ],
        [
            struct((16, width), f32),
            struct((2, rows, 3 * half), bf16),
            struct((2, crops, H // 2, slots, slots), bf16),
            struct((rows, width), bf16),
        ],
        [
            pltpu.VMEM((2, width, w_columns), bf16),
            pltpu.VMEM((2, 1, 3 * half), f32),
            pltpu.SemaphoreType.DMA((sem_count(pieces),)),
        ],
        2 * rows * width * 3 * width + 8 * rows * slots * width,
        30e6,
        "attention_forward",
    )(info, x, *pieces, *extra)


def run_attention_backward(info, qkv, da, probs, crops, which):
    _, rows, columns = qkv.shape
    slots = rows // crops
    half = columns // 3

    def pick(info):
        return info[0] if which else 1 - info[0]

    kernel = functools.partial(attention_backward, half // 128)
    return call(
        kernel,
        (crops,),
        [
            pl.BlockSpec((1, slots, columns), lambda i, info: (pick(info), i, 0)),
            pl.BlockSpec((slots, half), lambda i, info: (i, pick(info))),
            pl.BlockSpec(
                (1, 1, H // 2, slots, slots), lambda i, info: (pick(info), i, 0, 0, 0)
            ),
        ],
        [
            pl.BlockSpec((1, slots, columns), lambda i, info: (0, i, 0)),
            whole_block((8, columns)),
        ],
        [struct((1, rows, columns), bf16), struct((8, columns), f32)],
        [],
        16 * rows * slots * half,
        12e6,
        "attention_backward",
    )(info, qkv, da, probs)


def run_feed_forward(info, vec, x, attended, cot, pieces_a, pieces_b, block):
    rows, width = x.shape
    ff = 2 * pieces_b[0].shape[-1]
    kernel = functools.partial(feed_forward, len(pieces_a), len(pieces_b))
    return call(
        kernel,
        (rows // block,),
        [whole_block(vec.shape)]
        + [rows_block(block, width)] * 3
        + [ANY] * (len(pieces_a) + len(pieces_b)),
        [
            rows_block(block, width),
            rows_block(block, ff),
            rows_block(block, ff),
            rows_block(block, width),
            rows_block(block, width),
            rows_block(block, 1),
            rows_block(block, width),
            rows_block(block, width),
            whole_block((3, 8, width)),
        ],
        [
            struct((rows, width), bf16),
            struct((rows, ff), bf16),
            struct((rows, ff), bf16),
            struct((rows, width), bf16),
            struct((rows, width), f32),
            struct((rows, 1), f32),
            struct((rows, width), f32),
            struct((rows, width), bf16),
            struct((3, 8, width), f32),
        ],
        [
            pltpu.VMEM((2, width, pieces_a[0].shape[-1]), bf16),
            pltpu.VMEM((2, width, pieces_b[0].shape[-1]), bf16),
            pltpu.SemaphoreType.DMA((sem_count(pieces_a),)),
            pltpu.SemaphoreType.DMA((sem_count(pieces_b),)),
        ],
        2 * rows * width * (width + 2 * ff),
        45e6,
        "feed_forward",
    )(info, vec, x, attended, cot, *pieces_a, *pieces_b)


def run_feed_backward(info, vec, df, slope, dr2, z1, rstd, pieces_a, pieces_b, block):
    rows, width = df.shape
    ff = slope.shape[1]
    kernel = functools.partial(feed_backward, len(pieces_a), len(pieces_b))
    return call(
        kernel,
        (rows // block,),
        [
            whole_block(vec.shape),
            rows_block(block, width),
            rows_block(block, ff),
            rows_block(block, width),
            rows_block(block, width),
            rows_block(block, 1),
        ]
        + [ANY] * (len(pieces_a) + len(pieces_b)),
        [
            rows_block(block, ff),
            rows_block(block, width),
            rows_block(block, width),
            rows_block(block, width),
            whole_block((3, 8, width)),
            whole_block((4, 8, width)),
        ],
        [
            struct((rows, ff), bf16),
            struct((rows, width), f32),
            struct((rows, width), bf16),
            struct((rows, width), bf16),
            struct((3, 8, width), f32),
            struct((4, 8, width), f32),
        ],
        [
            pltpu.VMEM((2, width, pieces_a[0].shape[-1]), bf16),
            pltpu.VMEM((2, width, pieces_b[0].shape[-1]), bf16),
            pltpu.SemaphoreType.DMA((sem_count(pieces_a),)),
            pltpu.SemaphoreType.DMA((sem_count(pieces_b),)),
        ],
        2 * rows * width * (width + 2 * ff),
        45e6,
        "feed_backward",
    )(info, vec, df, slope, dr2, z1, rstd, *pieces_a, *pieces_b)


def run_token_gradient(info, dqkv, dr1, pieces, block):
    rows, width = dr1.shape
    columns = dqkv.shape[2]
    kernel = functools.partial(token_gradient, len(pieces))
    return call(
        kernel,
        (rows // block,),
        [
            pl.BlockSpec((2, block, columns), lambda i, info: (0, i, 0)),
            rows_block(block, width),
        ]
        + [ANY] * len(pieces),
        rows_block(block, width),
        struct((rows, width), f32),
        [
            pltpu.VMEM((2, width, pieces[0].shape[-1]), bf16),
            pltpu.SemaphoreType.DMA((sem_count(pieces),)),
        ],
        4 * rows * width * columns,
        20e6,
        "token_gradient",
    )(info, dqkv, dr1, *pieces)


def run_weight_gradient(info, pairs, columns, block, pick, recv, ext, full):
    rows, width = pairs[0][0].shape
    starts, step = [], 0
    rhs_specs = []
    for _, rhs, size in pairs:
        count = size // block
        starts.append(step)

        def place(i, info, step=step, count=count):
            return pick(info) * count + jnp.clip(i - step, 0, count - 1)

        if rhs.ndim == 3:
            rhs_specs.append(
                pl.BlockSpec(
                    (1, rows, block),
                    lambda i, info, step=step, count=count: (
                        0,
                        0,
                        jnp.clip(i - step, 0, count - 1),
                    ),
                )
            )
        else:
            rhs_specs.append(
                pl.BlockSpec((rows, block), lambda i, info, place=place: (0, place(i, info)))
            )
        step += count
    operands = [p[0] for p in pairs] + [p[1] for p in pairs]
    specs = [whole_block((rows, width)) for _ in pairs] + rhs_specs
    if recv is not None:
        operands.append(recv)
        specs.append(whole_block(recv.shape))
    if ext is not None:
        operands.append(ext)
        specs.append(whole_block(ext.shape))
    if recv is None:
        out_specs = [whole_block((width, columns))]
        out_shape = [struct((width, columns), f32 if full else bf16)]
    else:
        out_specs = [whole_block((4, 48, columns))] * 4
        out_shape = [struct((4, 48, columns), bf16)] * 4
    kernel = functools.partial(
        weight_gradient,
        tuple(starts),
        block,
        recv is not None,
        len(out_shape),
        None if ext is None else columns - EXT,
    )
    out = call(
        kernel,
        (step,),
        specs,
        out_specs,
        out_shape,
        [pltpu.VMEM((width, rows), bf16), pltpu.VMEM((width, block), f32)],
        2 * rows * width * columns,
        12e6,
        "weight_gradient",
    )(info, *operands)
    return out


def neighbours(n):
    flip = lambda bits: [(i, i ^ bits) for i in range(n)]
    shift = lambda k: [(i, (i + 8 * k) % n) for i in range(n)]
    return {"core": flip(1), "x": flip(2), "y": flip(4), "xy": flip(6)}, shift


def send(value, pairs):
    return lax.ppermute(value, "dp", pairs)


def gather_pieces(core, first, second, n):
    flips, shift = neighbours(n)
    keep = jnp.where(core == 0, first, second)
    give = jnp.where(core == 0, second, first)
    got = send(give, flips["core"])
    piece = jnp.where(
        core == 0, jnp.concatenate([keep, got]), jnp.concatenate([got, keep])
    )
    base = jnp.concatenate([piece] + [send(piece, shift(k)) for k in (1, 2, 3)])
    by_x, by_y = send(base, flips["x"]), send(base, flips["y"])
    mid = base.shape[0] // 2
    far = [send(by_x[:mid], flips["y"]), send(by_y[mid:], flips["x"])]
    own = [base, by_x, by_y] + far
    return own + [send(v, flips["core"]) for v in own]


def scatter_sum(core, parts, n):
    flips, shift = neighbours(n)
    own, to_x, to_y, to_xy = parts
    total = (
        own.astype(f32)
        + send(to_x, flips["x"]).astype(f32)
        + send(to_y, flips["y"]).astype(f32)
        + send(to_xy, flips["xy"]).astype(f32)
    )
    done = total[0]
    for k in (1, 2, 3):
        done = done + send(total[k].astype(bf16), shift(k)).astype(f32)
    rows = done.shape[0] // 2
    keep = jnp.where(core == 0, done[:rows], done[rows:])
    give = jnp.where(core == 0, done[rows:], done[:rows])
    got = send(give, flips["core"])
    return jnp.where(core == 0, keep, got), jnp.where(core == 0, got, keep)


def halves(matrix, groups):
    size = matrix.shape[1] // groups
    cut = size // 2
    return [
        jnp.concatenate(
            [matrix[:, g * size + h * cut : g * size + (h + 1) * cut] for g in range(groups)],
            axis=1,
        )
        for h in range(2)
    ]


def join(first, second, groups):
    cut = first.shape[1] // groups
    return jnp.concatenate(
        [v[:, g * cut : (g + 1) * cut] for g in range(groups) for v in (first, second)],
        axis=1,
    )


def momentum_step(weight, copy):
    return (weight.astype(f32) - copy) * 0.0005


def local(
    n,
    tokens,
    lengths,
    w_qkv,
    w_out,
    w_in,
    w_down,
    vector,
    key_qkv,
    key_out,
    key_in,
    key_down,
    key_vector,
    cotangent,
):
    width = tokens.shape[1]
    half = width // 2
    ff = w_in.shape[1]
    crops = lengths.shape[0]
    near = n == 32 and w_qkv.shape[0] == 24
    me = lax.axis_index("dp").astype(jnp.int32)
    core = me & 1
    place = jnp.stack([core, (me >> 1) & 1, (me >> 2) & 1, (me >> 3) & 3])
    info = jnp.concatenate([place, lengths.astype(jnp.int32)])

    qkv_halves = halves(w_qkv, 3)
    out_halves = halves(w_out, 1)
    in_halves = halves(w_in, 1)
    down_halves = halves(w_down, 1)
    mixed = [jnp.concatenate([out_halves[h], in_halves[h]], axis=1) for h in range(2)]
    if near:
        own_rows = w_qkv.shape[0]
        ext = jnp.pad(
            vector.reshape(own_rows, vector.shape[0] // own_rows),
            ((0, 0), (0, EXT - vector.shape[0] // own_rows)),
        )
        first = [jnp.concatenate([q, ext], axis=1) for q in qkv_halves]
        p_qkv = gather_pieces(core, first[0], first[1], n)
        p_mixed = gather_pieces(core, mixed[0], mixed[1], n)
        p_down = gather_pieces(core, down_halves[0], down_halves[1], n)
        vec = None
    else:
        everywhere = lambda pair: [
            lax.all_gather(jnp.stack(pair), "dp", axis=1, tiled=True)
        ]
        p_qkv, p_mixed, p_down = map(everywhere, (qkv_halves, mixed, down_halves))
        vec = lax.all_gather(vector, "dp", axis=0, tiled=True).astype(f32)
        vec = jnp.pad(vec.reshape(-1, width), ((0, 16 - vec.shape[0] // width), (0, 0)))

    vec, qkv, probs, attended = run_attention_forward(info, tokens, p_qkv, vec, crops)
    output, active, slope, n1, z1, rstd, dr2, df, sums_two = run_feed_forward(
        info, vec, tokens, attended, cotangent, p_mixed, p_down, 256
    )
    flips, _ = neighbours(n)
    other = lambda info: 1 - info[0]
    mine = lambda info: info[0]

    def gradient(pairs_of, columns, block, ext=(None, None)):
        if not near:
            return [
                run_weight_gradient(
                    info, pairs_of(h), columns, block, lambda info, h=h: h, None, None, True
                )[0]
                for h in range(2)
            ]
        away = run_weight_gradient(
            info, pairs_of(0), columns, block, other, None, ext[0], False
        )[0]
        got = send(away, flips["core"])
        parts = run_weight_gradient(
            info, pairs_of(1), columns, block, mine, got, ext[1], False
        )
        return scatter_sum(core, parts, n)

    g_down = gradient(lambda w: [(df, active, ff // 2)], ff // 2, 512)
    du, dr1, db, da, sums_one, sums_b1 = run_feed_backward(
        info, vec, df, slope, dr2, z1, rstd, p_mixed, p_down, 256
    )
    g_mixed = gradient(
        lambda w: [(attended, db, half), (n1, du, ff // 2)], half + ff // 2, half
    )
    if near:
        dqkv_other, sums_other = run_attention_backward(info, qkv, da, probs, crops, 0)
        dqkv_mine, sums_mine = run_attention_backward(info, qkv, da, probs, crops, 1)
        dqkv = jnp.where(
            core == 0,
            jnp.concatenate([dqkv_mine, dqkv_other]),
            jnp.concatenate([dqkv_other, dqkv_mine]),
        )
        sums_qkv = jnp.where(
            core == 0,
            jnp.stack([sums_mine, sums_other]),
            jnp.stack([sums_other, sums_mine]),
        )
        dqkv_by = [dqkv_other, dqkv_mine]
    else:
        info_of = lambda h: info.at[0].set(h)
        results = [
            run_attention_backward(info_of(h), qkv, da, probs, crops, 1) for h in range(2)
        ]
        dqkv_by = [r[0] for r in results]
        dqkv = jnp.concatenate(dqkv_by)
        sums_qkv = jnp.stack([r[1] for r in results])
    bias_sums = jnp.sum(sums_qkv, axis=1).reshape(2, 3, half)
    vec_grad = jnp.concatenate(
        [
            bias_sums[:, 0].reshape(-1),
            bias_sums[:, 2].reshape(-1),
            jnp.sum(sums_one[2], axis=0),
            jnp.sum(sums_one[0], axis=0),
            jnp.sum(sums_one[1], axis=0),
            jnp.sum(sums_two[0], axis=0),
            jnp.sum(sums_two[1], axis=0),
            jnp.sum(sums_two[2], axis=0),
            jnp.sum(sums_b1, axis=1).reshape(-1),
        ]
    )
    if near:
        per = vec_grad.shape[0] // width
        block = jnp.pad(vec_grad.reshape(width, per), ((0, 0), (0, EXT - per))).astype(bf16)
        g_qkv = gradient(
            lambda w: [(tokens, dqkv_by[w], 3 * half)], 3 * half + EXT, half, (block, block)
        )
        grad_vector = g_qkv[0][:, 3 * half : 3 * half + per].reshape(-1)
        g_qkv = [v[:, : 3 * half] for v in g_qkv]
    else:
        g_qkv = gradient(lambda w: [(tokens, dqkv_by[w], 3 * half)], 3 * half, half)
        grad_vector = lax.psum_scatter(vec_grad, "dp", scatter_dimension=0, tiled=True)
    grad_tokens = run_token_gradient(info, dqkv, dr1, p_qkv, 256)
    grad_qkv = join(g_qkv[0], g_qkv[1], 3)
    grad_out = join(g_mixed[0][:, :half], g_mixed[1][:, :half], 1)
    grad_in = join(g_mixed[0][:, half:], g_mixed[1][:, half:], 1)
    grad_down = join(g_down[0], g_down[1], 1)
    if not near:
        grad_qkv, grad_out, grad_in, grad_down = (
            lax.psum_scatter(g, "dp", scatter_dimension=0, tiled=True)
            for g in (grad_qkv, grad_out, grad_in, grad_down)
        )
    return (
        output,
        grad_tokens,
        grad_qkv,
        grad_out,
        grad_in,
        grad_down,
        grad_vector,
        momentum_step(w_qkv, key_qkv),
        momentum_step(w_out, key_out),
        momentum_step(w_in, key_in),
        momentum_step(w_down, key_down),
        momentum_step(vector, key_vector),
    )


def solution(mesh):
    n = mesh.shape["dp"]
    rows, flat = P("dp", None), P("dp")
    return jax.shard_map(
        functools.partial(local, n),
        mesh=mesh,
        in_specs=(rows, flat, rows, rows, rows, rows, flat, rows, rows, rows, rows, flat, rows),
        out_specs=(rows, rows, rows, rows, rows, rows, flat, rows, rows, rows, rows, flat),
        check_vma=False,
    )
```

```python
import functools

import jax
import jax.numpy as jnp
import numpy as np
from jax import lax
from jax.experimental import pallas as pl
from jax.experimental.pallas import tpu as pltpu
from jax.sharding import PartitionSpec as P

H = 12
EPS = 1e-12
EXT = 128
bf16 = jnp.bfloat16
f32 = jnp.float32
VMEM_LIMIT = 60 * 1024 * 1024
COST = 0.001
ANY = pl.BlockSpec(memory_space=pl.ANY)

NT = (((1,), (1,)), ((), ()))
TN = (((0,), (0,)), ((), ()))


def mm(a, b):
    return jnp.dot(a, b, preferred_element_type=f32)


def mm_nt(a, b):
    return lax.dot_general(a, b, NT, preferred_element_type=f32)


def mm_tn(a, b):
    return lax.dot_general(a, b, TN, preferred_element_type=f32)


def row_mean(v):
    return jnp.mean(v, axis=-1, keepdims=True)


def fold_rows(v):
    return jnp.sum(v.reshape(v.shape[0] // 8, 8, v.shape[1]), axis=0)


def chip_row(info, a, k, flip):
    x, y, z = info[1], info[2], info[3]
    xx = x ^ (a & 1)
    yy = y ^ (a >> 1)
    zz = z ^ k if flip else (z - k + 4) & 3
    return pl.multiple_of(((zz * 2 + yy) * 2 + xx) * 48, 16)


def weight_copies(info, refs, w, sems):
    if len(refs) == 1:
        return [pltpu.make_async_copy(refs[0], w, sems.at[0])]
    out = []
    per = len(refs) // 2
    far = [[(3, 0), (3, 1)], [(3, 2), (3, 3)]] if per == 5 else [[(3, k) for k in range(4)]]
    places = [[(a, k) for k in range(4)] for a in range(3)] + far
    for source in range(2):
        half = info[0] if source == 0 else 1 - info[0]
        for number, slots in enumerate(places):
            ref = refs[source * per + number]
            for j, (a, k) in enumerate(slots):
                row = chip_row(info, a, k, False)
                out.append(
                    pltpu.make_async_copy(
                        ref.at[pl.ds(48 * j, 48)],
                        w.at[half, pl.ds(row, 48)],
                        sems.at[len(out)],
                    )
                )
    return out


def sem_count(pieces):
    return 1 if len(pieces) == 1 else 32


def attention_forward(n_src, has_ext, pairs, info, x_ref, *refs):
    src = refs[:n_src]
    if has_ext:
        spread_ref, pick_ref = refs[n_src : n_src + 2]
        refs = refs[n_src + 2 :]
    else:
        vec_in = refs[n_src]
        refs = refs[n_src + 1 :]
    vec_ref, qkv_ref, p_ref, a_ref, w, bias, sems = refs
    crop = pl.program_id(0)
    half_width = pairs * 128

    @pl.when(crop == 0)
    def _():
        copies = weight_copies(info, src, w, sems)
        for copy in copies:
            copy.start()
        for copy in copies:
            copy.wait()
        if has_ext:
            spread = mm(w[0, :, 3 * half_width :], spread_ref[...])
            groups = spread.shape[0] // 64
            picked = spread.reshape(groups, 64, spread.shape[1]) * pick_ref[...][None]
            vec_ref[0:groups, :] = jnp.sum(picked, axis=1)
        else:
            vec_ref[...] = vec_in[...]
        for h in range(2):
            for part, row in ((0, 0), (2, 1)):
                bias[h, :, part * half_width : (part + 1) * half_width] = vec_ref[
                    row : row + 1, h * half_width : (h + 1) * half_width
                ]
            bias[h, :, half_width : 2 * half_width] = jnp.zeros((1, half_width), f32)

    x = x_ref[...]
    slots = x.shape[0]
    length = info[4 + crop]
    usable = lax.broadcasted_iota(jnp.int32, (1, slots), 1) < length
    mask_row = jnp.where(usable, 0.0, -1e30).astype(f32)
    lane = lax.broadcasted_iota(jnp.int32, (1, 128), 1)
    sides = (
        jnp.where(lane < 64, 1.0, 0.0).astype(bf16),
        jnp.where(lane < 64, 0.0, 1.0).astype(bf16),
    )
    units = [(h, p, side) for h in range(2) for p in range(pairs) for side in range(2)]

    def project(h):
        qkv_ref[h] = (mm(x, w[h, :, : 3 * half_width]) + bias[h]).astype(bf16)

    def columns(h, part, p):
        lo = part * half_width + p * 128
        return qkv_ref[h, :, lo : lo + 128]

    scores, probs, first = {}, {}, None
    project(0)
    for t in range(len(units) + 4):
        if t == 3:
            project(1)
        if t < len(units):
            h, p, side = units[t]
            q2 = columns(h, 0, p) * jnp.asarray(0.125, bf16)
            scores[t] = mm_nt(q2, columns(h, 1, p) * sides[side]) + mask_row
        if 0 <= t - 3 < len(units):
            h, p, side = units[t - 3]
            value = scores.pop(t - 3)
            terms = jnp.exp(value - jnp.max(value, axis=1, keepdims=True))
            mass = jnp.sum(terms, axis=1, keepdims=True)
            rounded = (terms * (1.0 / mass)).astype(bf16)
            p_ref[h, 0, p * 2 + side] = rounded
            probs[t - 3] = rounded
        if 0 <= t - 4 < len(units):
            h, p, side = units[t - 4]
            part = mm(probs.pop(t - 4), columns(h, 2, p) * sides[side])
            if side == 0:
                first = part
            else:
                lo = h * half_width + p * 128
                a_ref[:, lo : lo + 128] = (first + part).astype(bf16)


def attention_backward(pairs, info, qkv_ref, da_ref, p_ref, out_ref, sums_ref):
    half_width = pairs * 128
    lane = lax.broadcasted_iota(jnp.int32, (1, 128), 1)
    sides = (
        jnp.where(lane < 64, 1.0, 0.0).astype(bf16),
        jnp.where(lane < 64, 0.0, 1.0).astype(bf16),
    )

    @pl.when(pl.program_id(0) == 0)
    def _():
        sums_ref[...] = jnp.zeros_like(sums_ref)

    units = [(p, side) for p in range(pairs) for side in range(2)]

    def columns(part, p):
        lo = part * half_width + p * 128
        return qkv_ref[0, :, lo : lo + 128]

    d_probs, d_scores, total = {}, {}, None
    for t in range(len(units) + 4):
        if t < len(units):
            p, side = units[t]
            da2 = da_ref[:, p * 128 : (p + 1) * 128]
            d_probs[t] = mm_nt(da2, columns(2, p) * sides[side])
        if 0 <= t - 2 < len(units):
            p, side = units[t - 2]
            probs = p_ref[0, 0, p * 2 + side].astype(f32)
            value = d_probs.pop(t - 2)
            inner = jnp.sum(probs * value, axis=1, keepdims=True)
            d_scores[t - 2] = (probs * (value - inner)).astype(bf16)
        if 0 <= t - 4 < len(units):
            p, side = units[t - 4]
            value = d_scores.pop(t - 4)
            da2 = da_ref[:, p * 128 : (p + 1) * 128]
            parts = [
                mm(value, columns(1, p) * sides[side]) * 0.125,
                mm_tn(value, columns(0, p) * sides[side]) * 0.125,
                mm_tn(p_ref[0, 0, p * 2 + side], da2 * sides[side]),
            ]
            total = parts if side == 0 else [a + b for a, b in zip(total, parts)]
            if side == 1:
                for part in range(3):
                    lo = part * half_width + p * 128
                    rounded = total[part].astype(bf16)
                    out_ref[0, :, lo : lo + 128] = rounded
                    if part != 1:
                        sums_ref[:, lo : lo + 128] += fold_rows(rounded.astype(f32))


def gelu_parts(u):
    size = jnp.abs(u)
    t = 1.0 / (1.0 + size * (0.3275911 * 0.7071067811865476))
    bell = jnp.exp(u * u * -0.5)
    poly = t * (
        0.127414796
        + t * (-0.142248368 + t * (0.7107068705 + t * (-0.7265760135 + t * 0.5307027145)))
    )
    tail = poly * bell
    cdf = jnp.where(u < 0.0, tail, 1.0 - tail)
    return u * cdf, cdf + u * (bell * 0.3989422804014327)


def feed_stages(cut, vec_ref, ins, outs, sums_ref, slope, wa, wb, ready):
    x_ref, a_ref, cot_ref = ins
    out_ref, g_ref, du_ref, n1_ref, df_ref, db_ref, da_ref, dr1_ref = outs
    width = x_ref.shape[1]
    half = width // 2
    place = lambda j: (j // 2, (j % 2) * width)

    attended = a_ref[cut, :]
    branch = jnp.concatenate(
        [mm(attended, wa[h, :, :half]) for h in range(2)], axis=1
    ) + vec_ref[2:3, :]
    yield
    resid = x_ref[cut, :].astype(f32) + branch
    center = resid - row_mean(resid)
    rstd = lax.rsqrt(row_mean(center * center) + EPS)
    z1 = center * rstd
    n1 = z1 * (1.0 + vec_ref[3:4, :]) + vec_ref[4:5, :]
    n1b = n1.astype(bf16)
    n1_ref[cut, :] = n1b
    yield

    def up(j):
        h, lo = place(j)
        return mm(n1b, wa[h, :, half + lo : half + lo + width]) + vec_ref[8 + j : 9 + j, :]

    hidden = [up(0)]
    yield
    feed = None
    for j in range(4):
        if j < 3:
            hidden.append(up(j + 1))
            yield
        active, tilt = gelu_parts(hidden[j])
        hidden[j] = None
        active = active.astype(bf16)
        at = slice(j * width, (j + 1) * width)
        g_ref[cut, at] = active
        slope[cut, at] = tilt
        yield
        if j == 0:
            ready()
        h, lo = place(j)
        part = mm_nt(active, wb[h, :, lo : lo + width])
        feed = part if feed is None else feed + part
        yield
    resid2 = n1 + feed + vec_ref[7:8, :]
    center2 = resid2 - row_mean(resid2)
    rstd2 = lax.rsqrt(row_mean(center2 * center2) + EPS)
    z2 = center2 * rstd2
    gain2 = 1.0 + vec_ref[5:6, :]
    out_ref[cut, :] = (z2 * gain2 + vec_ref[6:7, :]).astype(bf16)
    dy = cot_ref[cut, :].astype(f32)
    s = dy * gain2
    dr2 = rstd2 * (s - row_mean(s) - z2 * row_mean(s * z2))
    df = dr2.astype(bf16)
    df_ref[cut, :] = df
    sums_ref[3] += fold_rows(dy * z2)
    sums_ref[4] += fold_rows(dy)
    sums_ref[5] += fold_rows(df.astype(f32))
    yield

    def back(j):
        h, lo = place(j)
        return mm(df, wb[h, :, lo : lo + width])

    d_active = [back(0)]
    yield
    dn1 = dr2
    for j in range(4):
        if j < 3:
            d_active.append(back(j + 1))
            yield
        at = slice(j * width, (j + 1) * width)
        du = (d_active[j] * slope[cut, at]).astype(bf16)
        d_active[j] = None
        du_ref[cut, at] = du
        sums_ref[6 + j] += fold_rows(du.astype(f32))
        yield
        h, lo = place(j)
        dn1 = dn1 + mm_nt(du, wa[h, :, half + lo : half + lo + width])
        yield
    sums_ref[0] += fold_rows(dn1 * z1)
    sums_ref[1] += fold_rows(dn1)
    s = dn1 * (1.0 + vec_ref[3:4, :])
    dr1 = rstd * (s - row_mean(s) - z1 * row_mean(s * z1))
    dr1_ref[cut, :] = dr1
    db = dr1.astype(bf16)
    db_ref[cut, :] = db
    sums_ref[2] += fold_rows(db.astype(f32))
    yield
    da = mm_nt(db[:, :half], wa[0, :, :half]) + mm_nt(db[:, half:], wa[1, :, :half])
    da_ref[cut, :] = da.astype(bf16)
    yield


def feed_both(n_a, n_b, sub, info, vec_ref, x_ref, a_ref, cot_ref, *refs):
    src_a = refs[:n_a]
    src_b = refs[n_a : n_a + n_b]
    refs = refs[n_a + n_b :]
    outs = refs[:8]
    sums_ref, slope, wa, wb, sems_a, sems_b = refs[8:]
    step = pl.program_id(0)
    copies_a = weight_copies(info, src_a, wa, sems_a)
    copies_b = weight_copies(info, src_b, wb, sems_b)

    @pl.when(step == 0)
    def _():
        for copy in copies_a + copies_b:
            copy.start()
        sums_ref[...] = jnp.zeros_like(sums_ref)
        for copy in copies_a:
            copy.wait()

    waited = []

    def ready():
        if not waited:
            waited.append(True)

            @pl.when(step == 0)
            def _():
                for copy in copies_b:
                    copy.wait()

    ins = (x_ref, a_ref, cot_ref)
    blocks = [
        feed_stages(slice(r, r + sub), vec_ref, ins, outs, sums_ref, slope, wa, wb, ready)
        for r in range(0, x_ref.shape[0], sub)
    ]
    waiting, t = list(range(len(blocks))), 0
    while waiting:
        for i in list(waiting):
            if t >= i and next(blocks[i], True):
                waiting.remove(i)
        t += 1


def token_gradient(n_src, info, other_ref, mine_ref, dr1_ref, *refs):
    src = refs[:n_src]
    out_ref, w, sems = refs[n_src:]
    used = mine_ref.shape[2]

    @pl.when(pl.program_id(0) == 0)
    def _():
        copies = weight_copies(info, src, w, sems)
        for copy in copies:
            copy.start()
        for copy in copies:
            copy.wait()

    out_ref[...] = (
        dr1_ref[...]
        + mm_nt(other_ref[0], w[1 - info[0], :, :used])
        + mm_nt(mine_ref[0], w[info[0], :, :used])
    )


def vector_rows(info, sums_ref, other_ref, mine_ref):
    total = lambda v: jnp.sum(v, axis=0, keepdims=True)
    half = other_ref.shape[1] // 3
    rows = []
    for part in (0, 2):
        cut = slice(part * half, (part + 1) * half)
        other, mine = total(other_ref[:, cut]), total(mine_ref[:, cut])
        first = jnp.where(info[0] == 0, mine, other)
        second = jnp.where(info[0] == 0, other, mine)
        rows.append(jnp.concatenate([first, second], axis=1))
    return rows + [total(sums_ref[i]) for i in (2, 0, 1, 3, 4, 5, 6, 7, 8, 9)]


DIRECT = tuple([(a, k) for k in range(4)] for a in range(4))
RELAYED = (
    [(0, k) for k in range(4)],
    [(3, 0), (3, 1), (1, 0), (1, 1)],
    [(3, 2), (3, 3), (2, 2), (2, 3)],
    [(1, 2), (1, 3)],
    [(2, 0), (2, 1)],
)


def weight_gradient(starts, sizes, has_recv, buffers, has_ext, info, *refs):
    count = len(starts)
    lhs = refs[:count]
    rhs = refs[count : 2 * count]
    at = 2 * count
    recv = None
    if has_recv:
        recv = refs[at]
        at += 1
    if has_ext:
        sums_ref, other_ref, mine_ref, spread_ref, pick_ref = refs[at : at + 5]
        at += 5
    (*outs, acc) = refs[at:]
    step = pl.program_id(0)

    def store(value, add):
        size = value.shape[1]
        if buffers is None:
            outs[0][:, :size] = value.astype(outs[0].dtype)
            return
        acc[:, :size] = value
        for out, slots in zip(outs, buffers):
            for j, (a, k) in enumerate(slots):
                row = chip_row(info, a, k, True)
                mine = acc[pl.ds(row, 48), :size]
                if add:
                    mine = mine + recv[pl.ds(row, 48), :size].astype(f32)
                out[j, :, :size] = mine.astype(bf16)

    for number, start in enumerate(starts):
        here = step >= start
        if number + 1 < count:
            here = here & (step < starts[number + 1])
        elif has_ext:
            here = here & (step < pl.num_programs(0) - 1)

        @pl.when(here)
        def _(number=number):
            right = rhs[number]
            right = right[0] if len(right.shape) == 3 else right[...]
            store(mm_tn(lhs[number][...], right), True)

    if has_ext:

        @pl.when(step == pl.num_programs(0) - 1)
        def _():
            rows = vector_rows(info, sums_ref, other_ref, mine_ref)
            picked = jnp.concatenate([(r * pick_ref[...]).astype(bf16) for r in rows], axis=0)
            store(mm_nt(picked, spread_ref[...]), False)


def params():
    return pltpu.CompilerParams(
        dimension_semantics=("arbitrary",), vmem_limit_bytes=VMEM_LIMIT
    )


def call(kernel, grid, in_specs, out_specs, out_shape, scratch, flops, nbytes, name, after=()):
    def body(info, *refs):
        kernel(info, *refs[len(after) :])

    run = pl.pallas_call(
        body,
        grid_spec=pltpu.PrefetchScalarGridSpec(
            num_scalar_prefetch=1,
            grid=grid,
            in_specs=[ANY] * len(after) + in_specs,
            out_specs=out_specs,
            scratch_shapes=scratch,
        ),
        out_shape=out_shape,
        compiler_params=params(),
        cost_estimate=pl.CostEstimate(
            flops=int(flops * COST), bytes_accessed=int(nbytes * COST), transcendentals=0
        ),
        name=name,
    )
    return lambda info, *operands: run(info, *after, *operands)


def struct(shape, dtype):
    return jax.ShapeDtypeStruct(shape, dtype)


def whole_block(shape):
    return pl.BlockSpec(shape, lambda i, info: (0,) * len(shape))


def rows_block(rows, columns):
    return pl.BlockSpec((rows, columns), lambda i, info: (i, 0))


def spread_tables(width):
    per = width // 64
    e = np.arange(width)
    spread = (np.arange(EXT)[:, None] == (e % per)[None, :]).astype(np.float32)
    pick = (np.arange(64)[:, None] == (e // per)[None, :]).astype(np.float32)
    return spread, pick


def run_attention_forward(info, x, pieces, vec, crops, after):
    rows, width = x.shape
    slots = rows // crops
    half = width // 2
    w_columns = pieces[0].shape[-1]
    has_ext = vec is None
    pairs = half // 128
    if has_ext:
        spread, pick = spread_tables(width)
        extra = [jnp.asarray(spread, bf16), jnp.asarray(pick, f32)]
    else:
        extra = [vec]
    extra_specs = [whole_block(e.shape) for e in extra]
    kernel = functools.partial(attention_forward, len(pieces), has_ext, pairs)
    return call(
        kernel,
        (crops,),
        [rows_block(slots, width)] + [ANY] * len(pieces) + extra_specs,
        [
            whole_block((16, width)),
            pl.BlockSpec((2, slots, 3 * half), lambda i, info: (0, i, 0)),
            pl.BlockSpec((2, 1, H // 2, slots, slots), lambda i, info: (0, i, 0, 0, 0)),
            rows_block(slots, width),
        ],
        [
            struct((16, width), f32),
            struct((2, rows, 3 * half), bf16),
            struct((2, crops, H // 2, slots, slots), bf16),
            struct((rows, width), bf16),
        ],
        [
            pltpu.VMEM((2, width, w_columns), bf16),
            pltpu.VMEM((2, 1, 3 * half), f32),
            pltpu.SemaphoreType.DMA((sem_count(pieces),)),
        ],
        2 * rows * width * 3 * width + 8 * rows * slots * width,
        30e6,
        "attention_forward",
        after,
    )(info, x, *pieces, *extra)


def run_attention_backward(info, qkv, da, probs, crops, which, after):
    _, rows, columns = qkv.shape
    slots = rows // crops
    half = columns // 3

    def pick(info):
        return info[0] if which else 1 - info[0]

    kernel = functools.partial(attention_backward, half // 128)
    return call(
        kernel,
        (crops,),
        [
            pl.BlockSpec((1, slots, columns), lambda i, info: (pick(info), i, 0)),
            pl.BlockSpec((slots, half), lambda i, info: (i, pick(info))),
            pl.BlockSpec(
                (1, 1, H // 2, slots, slots), lambda i, info: (pick(info), i, 0, 0, 0)
            ),
        ],
        [
            pl.BlockSpec((1, slots, columns), lambda i, info: (0, i, 0)),
            whole_block((8, columns)),
        ],
        [struct((1, rows, columns), bf16), struct((8, columns), f32)],
        [],
        16 * rows * slots * half,
        12e6,
        "attention_backward",
        after,
    )(info, qkv, da, probs)


def run_feed(info, vec, x, attended, cot, pieces_a, pieces_b, block, sub, after):
    rows, width = x.shape
    ff = 2 * pieces_b[0].shape[-1]
    kernel = functools.partial(feed_both, len(pieces_a), len(pieces_b), sub)
    narrow, wide = rows_block(block, width), rows_block(block, ff)
    return call(
        kernel,
        (rows // block,),
        [whole_block(vec.shape)] + [narrow] * 3 + [ANY] * (len(pieces_a) + len(pieces_b)),
        [narrow, wide, wide] + [narrow] * 5 + [whole_block((10, 8, width))],
        [struct((rows, width), bf16), struct((rows, ff), bf16), struct((rows, ff), bf16)]
        + [struct((rows, width), bf16)] * 4
        + [struct((rows, width), f32), struct((10, 8, width), f32)],
        [
            pltpu.VMEM((block, ff), f32),
            pltpu.VMEM((2, width, pieces_a[0].shape[-1]), bf16),
            pltpu.VMEM((2, width, pieces_b[0].shape[-1]), bf16),
            pltpu.SemaphoreType.DMA((sem_count(pieces_a),)),
            pltpu.SemaphoreType.DMA((sem_count(pieces_b),)),
        ],
        4 * rows * width * (width + 2 * ff),
        53e6,
        "feed_both",
        after,
    )(info, vec, x, attended, cot, *pieces_a, *pieces_b)


def run_token_gradient(info, dqkv_by, dr1, pieces, block, after):
    rows, width = dr1.shape
    columns = dqkv_by[0].shape[2]
    kernel = functools.partial(token_gradient, len(pieces))
    return call(
        kernel,
        (rows // block,),
        [
            pl.BlockSpec((1, block, columns), lambda i, info: (0, i, 0)),
            pl.BlockSpec((1, block, columns), lambda i, info: (0, i, 0)),
            rows_block(block, width),
        ]
        + [ANY] * len(pieces),
        rows_block(block, width),
        struct((rows, width), f32),
        [
            pltpu.VMEM((2, width, pieces[0].shape[-1]), bf16),
            pltpu.SemaphoreType.DMA((sem_count(pieces),)),
        ],
        4 * rows * width * columns,
        20e6,
        "token_gradient",
        after,
    )(info, *dqkv_by, dr1, *pieces)


def run_weight_gradient(info, pairs, columns, block, pick, recv, ext, full, after, buffers=None):
    rows, width = pairs[0][0].shape
    once = pl.Buffered(1)
    starts, sizes, step = [], [], 0
    rhs_specs = []
    for _, rhs, total, size in pairs:
        count = total // size
        starts.append(step)
        sizes.append(size)
        near = lambda i, step=step, count=count: jnp.clip(i - step, 0, count - 1)
        if rhs.ndim == 3:
            rhs_specs.append(
                pl.BlockSpec((1, rows, size), lambda i, info, near=near: (0, 0, near(i)))
            )
        else:
            rhs_specs.append(
                pl.BlockSpec(
                    (rows, size),
                    lambda i, info, near=near, count=count: (0, pick(info) * count + near(i)),
                )
            )
        step += count
    operands = [p[0] for p in pairs] + [p[1] for p in pairs]
    left = pl.BlockSpec((rows, width), lambda i, info: (0, 0), pipeline_mode=once)
    specs = [left for _ in pairs] + rhs_specs
    if recv is not None:
        recv, base = recv
        operands.append(recv)
        last = step - 1
        specs.append(
            pl.BlockSpec((width, block), lambda i, info: (0, base + jnp.minimum(i, last)))
        )
    if ext is not None:
        spread, pick_rows = spread_tables(width)
        more = list(ext) + [jnp.asarray(spread, bf16), jnp.asarray(pick_rows, f32)]
        operands += more
        specs += [whole_block(v.shape) for v in more]
        step += 1
    if recv is None:
        out_specs = [pl.BlockSpec((width, block), lambda i, info: (0, i))]
        out_shape = [struct((width, columns), f32 if full else bf16)]
    else:
        out_specs = [
            pl.BlockSpec((len(b), 48, block), lambda i, info: (0, 0, i)) for b in buffers
        ]
        out_shape = [struct((len(b), 48, columns), bf16) for b in buffers]
    kernel = functools.partial(
        weight_gradient, tuple(starts), tuple(sizes), recv is not None, buffers, ext is not None
    )
    return call(
        kernel,
        (step,),
        specs,
        out_specs,
        out_shape,
        [pltpu.VMEM((width, block), f32)],
        2 * rows * width * columns,
        12e6,
        "weight_gradient",
        after,
    )(info, *operands)


def neighbours(n):
    flip = lambda bits: [(i, i ^ bits) for i in range(n)]
    shift = lambda k: [(i, (i + 8 * k) % n) for i in range(n)]
    ways = {"core": 1, "x": 2, "y": 4, "xy": 6, "z": 8, "zz": 16, "zzz": 24}
    return {way: flip(bits) for way, bits in ways.items()}, shift


def send(value, pairs):
    return lax.ppermute(value, "dp", pairs)


def chip_piece(core, first, second, n):
    flips, _ = neighbours(n)
    keep = jnp.where(core == 0, first, second)
    give = jnp.where(core == 0, second, first)
    got = send(give, flips["core"])
    return jnp.where(core == 0, jnp.concatenate([keep, got]), jnp.concatenate([got, keep]))


def along_z(piece, n):
    _, shift = neighbours(n)
    return jnp.concatenate([piece] + [send(piece, shift(k)) for k in (1, 2, 3)])


def across_relayed(base, n):
    flips, _ = neighbours(n)
    by_x, by_y = send(base, flips["x"]), send(base, flips["y"])
    mid = base.shape[0] // 2
    return [base, by_x, by_y, send(by_x[:mid], flips["y"]), send(by_y[mid:], flips["x"])]


def across_direct(base, n):
    flips, _ = neighbours(n)
    return [base] + [send(base, flips[way]) for way in ("x", "y", "xy")]


def both_cores(own, n):
    flips, _ = neighbours(n)
    return own + [send(v, flips["core"]) for v in own]


def behind(value, *others):
    return lax.optimization_barrier((value,) + others)[0]


def sum_first(parts, n, *gates):
    flips, _ = neighbours(n)
    got_x, got_y = send(parts[1], flips["x"]), send(parts[2], flips["y"])
    got_x, got_y = lax.optimization_barrier((got_x, got_y) + gates)[:2]
    to_x = (parts[3].astype(f32) + got_y[:2].astype(f32)).astype(bf16)
    to_y = (parts[4].astype(f32) + got_x[:2].astype(f32)).astype(bf16)
    return got_x, got_y, to_x, to_y


def sum_rest(parts, first, n, *gates):
    flips, _ = neighbours(n)
    got_x, got_y, to_x, to_y = first
    rest_x, rest_y = send(to_x, flips["x"]), send(to_y, flips["y"])
    got_x, got_y, rest_x, rest_y = lax.optimization_barrier(
        (got_x, got_y, rest_x, rest_y) + gates
    )[:4]
    low = parts[0][:2].astype(f32) + got_x[2:].astype(f32) + rest_y.astype(f32)
    high = parts[0][2:].astype(f32) + got_y[2:].astype(f32) + rest_x.astype(f32)
    return [low[0]] + [v.astype(bf16) for v in (low[1], high[0], high[1])]


def share_rows(core, done, n):
    flips, _ = neighbours(n)
    rows = done.shape[0] // 2
    keep = jnp.where(core == 0, done[:rows], done[rows:])
    give = jnp.where(core == 0, done[rows:], done[:rows])
    got = send(give, flips["core"])
    return jnp.where(core == 0, keep, got), jnp.where(core == 0, got, keep)


def sum_along(total, n):
    flips, _ = neighbours(n)
    done = total[0]
    for value, way in zip(total[1:], ("z", "zz", "zzz")):
        done = done + send(value, flips[way]).astype(f32)
    return done


def halves(matrix, groups):
    size = matrix.shape[1] // groups
    cut = size // 2
    return [
        jnp.concatenate(
            [matrix[:, g * size + h * cut : g * size + (h + 1) * cut] for g in range(groups)],
            axis=1,
        )
        for h in range(2)
    ]


def join(first, second, groups):
    rows, columns = first.shape
    shape = (rows, groups, 1, columns // groups)
    both = jnp.concatenate([first.reshape(shape), second.reshape(shape)], axis=2)
    return both.reshape(rows, 2 * columns)


def momentum_step(weight, copy):
    return (weight.astype(f32) - copy) * 0.0005


def momentum_all(info, *refs):
    count = len(refs) // 3
    for weight, copy, out in zip(refs[:count], refs[count : 2 * count], refs[2 * count :]):
        out[...] = momentum_step(weight[...], copy[...])


def run_momentum(info, weights, copies, after):
    blocks = [whole_block(w.shape) for w in weights]
    return call(
        momentum_all,
        (1,),
        blocks + blocks,
        blocks,
        [struct(w.shape, f32) for w in weights],
        [],
        0,
        0,
        "momentum",
        after,
    )(info, *weights, *copies)


def local(
    n,
    tokens,
    lengths,
    w_qkv,
    w_out,
    w_in,
    w_down,
    vector,
    key_qkv,
    key_out,
    key_in,
    key_down,
    key_vector,
    cotangent,
):
    width = tokens.shape[1]
    half = width // 2
    ff = w_in.shape[1]
    crops = lengths.shape[0]
    near = n == 32 and w_qkv.shape[0] == 24
    me = lax.axis_index("dp").astype(jnp.int32)
    core = me & 1
    place = jnp.stack([core, (me >> 1) & 1, (me >> 2) & 1, (me >> 3) & 3])
    info = jnp.concatenate([place, lengths.astype(jnp.int32)])

    qkv_halves = halves(w_qkv, 3)
    out_halves = halves(w_out, 1)
    in_halves = halves(w_in, 1)
    down_halves = halves(w_down, 1)
    mixed = [jnp.concatenate([out_halves[h], in_halves[h]], axis=1) for h in range(2)]
    if near:
        own_rows = w_qkv.shape[0]
        ext = jnp.pad(
            vector.reshape(own_rows, vector.shape[0] // own_rows),
            ((0, 0), (0, EXT - vector.shape[0] // own_rows)),
        )
        first = [jnp.concatenate([q, ext], axis=1) for q in qkv_halves]
        base = along_z(chip_piece(core, first[0], first[1], n), n)
        p_qkv = across_relayed(base, n)
        piece = chip_piece(core, mixed[0], mixed[1], n)
        base_mixed = along_z(behind(piece, base), n)
        p_mixed = across_direct(behind(base_mixed, *p_qkv), n)
        p_qkv = both_cores(p_qkv, n)
        p_down = [lax.all_gather(jnp.stack(down_halves), "dp", axis=1, tiled=True)]
        deltas = run_momentum(
            info,
            (w_qkv, w_out, w_in, w_down, vector.reshape(1, -1)),
            (key_qkv, key_out, key_in, key_down, key_vector.reshape(1, -1)),
            (base,),
        )
        order = [base_mixed, deltas[0]]
        vec = None
    else:
        everywhere = lambda pair: [
            lax.all_gather(jnp.stack(pair), "dp", axis=1, tiled=True)
        ]
        p_qkv, p_mixed, p_down = map(everywhere, (qkv_halves, mixed, down_halves))
        vec = lax.all_gather(vector, "dp", axis=0, tiled=True).astype(f32)
        vec = jnp.pad(vec.reshape(-1, width), ((0, 16 - vec.shape[0] // width), (0, 0)))
        order = []
        pairs = zip(
            (w_qkv, w_out, w_in, w_down, vector), (key_qkv, key_out, key_in, key_down, key_vector)
        )
        deltas = [momentum_step(weight, copy) for weight, copy in pairs]

    vec, qkv, probs, attended = run_attention_forward(info, tokens, p_qkv, vec, crops, order)
    if near:
        p_mixed = both_cores([behind(v, attended) for v in p_mixed], n)
    output, active, du, n1, df, db, da, dr1, sums = run_feed(
        info, vec, tokens, attended, cotangent, p_mixed, p_down, 512, 256, ()
    )
    down_pairs = [(df, active, ff // 2, width)]
    mixed_pairs = [(n1, du, ff // 2, width), (attended, db, half, half)]
    if near:
        flips, _ = neighbours(n)

        def away(pairs, columns, block, after):
            return run_weight_gradient(
                info, pairs, columns, block, lambda info: 1 - info[0], None, None, False, after
            )[0]

        def mine(pairs, columns, block, got, ext, after, buffers=RELAYED):
            return run_weight_gradient(
                info, pairs, columns, block, lambda info: info[0], got, ext, False, after, buffers
            )

        away_ff = away(down_pairs + mixed_pairs, half + ff, width, ())
        got_ff = send(away_ff, flips["core"])
        dqkv_other, sums_other = run_attention_backward(
            info, qkv, da, probs, crops, 0, (away_ff,)
        )
        parts_down = mine(down_pairs, ff // 2, width, (got_ff, 0), None, (sums_other,))
        qkv_pairs = lambda dqkv: [(tokens, dqkv, 3 * half, half)]
        away_qkv = away(qkv_pairs(dqkv_other), 3 * half, half, (parts_down[0],))
        got_qkv = send(away_qkv, flips["core"])
        parts_mixed = mine(
            mixed_pairs, half + ff // 2, width, (got_ff, ff // 2 // width), None, (away_qkv,)
        )
        first_down = sum_first(parts_down, n, parts_mixed[0])
        dqkv_mine, sums_mine = run_attention_backward(
            info, qkv, da, probs, crops, 1, (parts_mixed[0],) + first_down[2:]
        )
        total_down = sum_rest(parts_down, first_down, n, sums_mine)
        sums_all = (sums, sums_other, sums_mine)
        parts_qkv = mine(
            qkv_pairs(dqkv_mine), 3 * half + EXT, half, (got_qkv, 0), sums_all, (total_down[1],)
        )
        first_mixed = sum_first(parts_mixed, n, parts_qkv[0])
        grad_tokens = run_token_gradient(
            info, [dqkv_other, dqkv_mine], dr1, p_qkv, 256, (parts_qkv[0],) + first_mixed[2:]
        )
        total_mixed = sum_rest(parts_mixed, first_mixed, n, grad_tokens)
        first_qkv = sum_first(parts_qkv, n, grad_tokens)
        g_down = share_rows(core, sum_along(total_down, n), n)
        g_mixed = share_rows(core, sum_along(total_mixed, n), n)
        g_in = [v[:, : ff // 2] for v in g_mixed]
        g_out = [v[:, ff // 2 :] for v in g_mixed]
        g_qkv = share_rows(core, sum_along(sum_rest(parts_qkv, first_qkv, n), n), n)
        per = vector.shape[0] // w_qkv.shape[0]
        grad_down = join(g_down[0], g_down[1], 1)
        grad_vector = (g_qkv[0] + g_qkv[1])[:, 3 * half : 3 * half + per].reshape(-1)
        g_qkv = [v[:, : 3 * half] for v in g_qkv]
    else:

        def gradient(pairs_of, columns, block):
            return [
                run_weight_gradient(
                    info, pairs_of(h), columns, block, lambda info, h=h: h, None, None, True, ()
                )[0]
                for h in range(2)
            ]

        info_of = lambda h: info.at[0].set(h)
        results = [
            run_attention_backward(info_of(h), qkv, da, probs, crops, 1, ()) for h in range(2)
        ]
        dqkv_by = [r[0] for r in results]
        bias_sums = jnp.stack([jnp.sum(r[1], axis=0) for r in results]).reshape(2, 3, half)
        sums = jnp.sum(sums, axis=1)
        vec_grad = jnp.concatenate(
            [bias_sums[:, 0].reshape(-1), bias_sums[:, 2].reshape(-1)]
            + [sums[i] for i in (2, 0, 1, 3, 4, 5, 6, 7, 8, 9)]
        )
        g_down = gradient(lambda h: down_pairs, ff // 2, width)
        g_mixed = gradient(lambda h: mixed_pairs, half + ff // 2, width)
        g_in = [v[:, : ff // 2] for v in g_mixed]
        g_out = [v[:, ff // 2 :] for v in g_mixed]
        grad_down = join(g_down[0], g_down[1], 1)
        g_qkv = gradient(lambda h: [(tokens, dqkv_by[h], 3 * half, half)], 3 * half, half)
        grad_vector = lax.psum_scatter(vec_grad, "dp", scatter_dimension=0, tiled=True)
        grad_tokens = run_token_gradient(info_of(1), dqkv_by, dr1, p_qkv, 256, ())
    grad_qkv = join(g_qkv[0], g_qkv[1], 3)
    grad_out = join(g_out[0], g_out[1], 1)
    grad_in = join(g_in[0], g_in[1], 1)
    if not near:
        grad_qkv, grad_out, grad_in, grad_down = (
            lax.psum_scatter(g, "dp", scatter_dimension=0, tiled=True)
            for g in (grad_qkv, grad_out, grad_in, grad_down)
        )
    return (
        output,
        grad_tokens,
        grad_qkv,
        grad_out,
        grad_in,
        grad_down,
        grad_vector,
        *deltas[:4],
        deltas[4].reshape(-1),
    )


def solution(mesh):
    n = mesh.shape["dp"]
    rows, flat = P("dp", None), P("dp")
    return jax.shard_map(
        functools.partial(local, n),
        mesh=mesh,
        in_specs=(rows, flat, rows, rows, rows, rows, flat, rows, rows, rows, rows, flat, rows),
        out_specs=(rows, rows, rows, rows, rows, rows, flat, rows, rows, rows, rows, flat),
        check_vma=False,
    )
```

```python
import functools

import jax
import jax.numpy as jnp
import numpy as np
from jax import lax
from jax.experimental import pallas as pl
from jax.experimental.pallas import tpu as pltpu
from jax.sharding import PartitionSpec as P

H = 12
EPS = 1e-12
EXT = 128
bf16 = jnp.bfloat16
f32 = jnp.float32
VMEM_LIMIT = 60 * 1024 * 1024
COST = 0.001
ANY = pl.BlockSpec(memory_space=pl.ANY)

NT = (((1,), (1,)), ((), ()))
TN = (((0,), (0,)), ((), ()))


def mm(a, b):
    return jnp.dot(a, b, preferred_element_type=f32)


def mm_nt(a, b):
    return lax.dot_general(a, b, NT, preferred_element_type=f32)


def mm_tn(a, b):
    return lax.dot_general(a, b, TN, preferred_element_type=f32)


def row_mean(v):
    return jnp.mean(v, axis=-1, keepdims=True)


def fold_rows(v):
    return jnp.sum(v.reshape(v.shape[0] // 8, 8, v.shape[1]), axis=0)


def chip_row(info, a, k, flip):
    x, y, z = info[1], info[2], info[3]
    xx = x ^ (a & 1)
    yy = y ^ (a >> 1)
    zz = z ^ k if flip else (z - k + 4) & 3
    return pl.multiple_of(((zz * 2 + yy) * 2 + xx) * 48, 16)


def weight_copies(info, refs, w, sems):
    if len(refs) == 1:
        return [pltpu.make_async_copy(refs[0], w, sems.at[0])]
    out = []
    per = len(refs) // 2
    far = [[(3, 0), (3, 1)], [(3, 2), (3, 3)]] if per == 5 else [[(3, k) for k in range(4)]]
    places = [[(a, k) for k in range(4)] for a in range(3)] + far
    for source in range(2):
        half = info[0] if source == 0 else 1 - info[0]
        for number, slots in enumerate(places):
            ref = refs[source * per + number]
            for j, (a, k) in enumerate(slots):
                row = chip_row(info, a, k, False)
                out.append(
                    pltpu.make_async_copy(
                        ref.at[pl.ds(48 * j, 48)],
                        w.at[half, pl.ds(row, 48)],
                        sems.at[len(out)],
                    )
                )
    return out


def sem_count(pieces):
    return 1 if len(pieces) == 1 else 32


def attention_forward(n_src, has_ext, pairs, info, x_ref, *refs):
    src = refs[:n_src]
    if has_ext:
        spread_ref, pick_ref = refs[n_src : n_src + 2]
        refs = refs[n_src + 2 :]
    else:
        vec_in = refs[n_src]
        refs = refs[n_src + 1 :]
    vec_ref, qkv_ref, p_ref, a_ref, w, bias, sems = refs
    crop = pl.program_id(0)
    half_width = pairs * 128

    @pl.when(crop == 0)
    def _():
        copies = weight_copies(info, src, w, sems)
        for copy in copies:
            copy.start()
        for copy in copies:
            copy.wait()
        if has_ext:
            spread = mm(w[0, :, 3 * half_width :], spread_ref[...])
            groups = spread.shape[0] // 64
            picked = spread.reshape(groups, 64, spread.shape[1]) * pick_ref[...][None]
            vec_ref[0:groups, :] = jnp.sum(picked, axis=1)
        else:
            vec_ref[...] = vec_in[...]
        for h in range(2):
            for part, row in ((0, 0), (2, 1)):
                bias[h, :, part * half_width : (part + 1) * half_width] = vec_ref[
                    row : row + 1, h * half_width : (h + 1) * half_width
                ]
            bias[h, :, half_width : 2 * half_width] = jnp.zeros((1, half_width), f32)

    x = x_ref[...]
    slots = x.shape[0]
    length = info[4 + crop]
    usable = lax.broadcasted_iota(jnp.int32, (1, slots), 1) < length
    mask_row = jnp.where(usable, 0.0, -1e30).astype(f32)
    lane = lax.broadcasted_iota(jnp.int32, (1, 128), 1)
    sides = (
        jnp.where(lane < 64, 1.0, 0.0).astype(bf16),
        jnp.where(lane < 64, 0.0, 1.0).astype(bf16),
    )
    units = [(h, p, side) for h in range(2) for p in range(pairs) for side in range(2)]

    def project(h):
        qkv_ref[h] = (mm(x, w[h, :, : 3 * half_width]) + bias[h]).astype(bf16)

    def columns(h, part, p):
        lo = part * half_width + p * 128
        return qkv_ref[h, :, lo : lo + 128]

    scores, probs, first = {}, {}, None
    project(0)
    for t in range(len(units) + 4):
        if t == 3:
            project(1)
        if t < len(units):
            h, p, side = units[t]
            q2 = columns(h, 0, p) * jnp.asarray(0.125, bf16)
            scores[t] = mm_nt(q2, columns(h, 1, p) * sides[side]) + mask_row
        if 0 <= t - 3 < len(units):
            h, p, side = units[t - 3]
            value = scores.pop(t - 3)
            terms = jnp.exp(value - jnp.max(value, axis=1, keepdims=True))
            mass = jnp.sum(terms, axis=1, keepdims=True)
            rounded = (terms * (1.0 / mass)).astype(bf16)
            p_ref[h, 0, p * 2 + side] = rounded
            probs[t - 3] = rounded
        if 0 <= t - 4 < len(units):
            h, p, side = units[t - 4]
            part = mm(probs.pop(t - 4), columns(h, 2, p) * sides[side])
            if side == 0:
                first = part
            else:
                lo = h * half_width + p * 128
                a_ref[:, lo : lo + 128] = (first + part).astype(bf16)


def attention_backward(pairs, info, qkv_ref, da_ref, p_ref, out_ref, sums_ref, keep=None):
    half_width = pairs * 128
    lane = lax.broadcasted_iota(jnp.int32, (1, 128), 1)
    sides = (
        jnp.where(lane < 64, 1.0, 0.0).astype(bf16),
        jnp.where(lane < 64, 0.0, 1.0).astype(bf16),
    )

    @pl.when(pl.program_id(0) == 0)
    def _():
        sums_ref[...] = jnp.zeros_like(sums_ref)

    units = [(p, side) for p in range(pairs) for side in range(2)]

    def columns(part, p):
        lo = part * half_width + p * 128
        return qkv_ref[0, :, lo : lo + 128]

    d_probs, d_scores, total = {}, {}, None
    for t in range(len(units) + 4):
        if t < len(units):
            p, side = units[t]
            da2 = da_ref[:, p * 128 : (p + 1) * 128]
            d_probs[t] = mm_nt(da2, columns(2, p) * sides[side])
        if 0 <= t - 2 < len(units):
            p, side = units[t - 2]
            probs = p_ref[0, 0, p * 2 + side].astype(f32)
            value = d_probs.pop(t - 2)
            inner = jnp.sum(probs * value, axis=1, keepdims=True)
            d_scores[t - 2] = (probs * (value - inner)).astype(bf16)
        if 0 <= t - 4 < len(units):
            p, side = units[t - 4]
            value = d_scores.pop(t - 4)
            da2 = da_ref[:, p * 128 : (p + 1) * 128]
            parts = [
                mm(value, columns(1, p) * sides[side]) * 0.125,
                mm_tn(value, columns(0, p) * sides[side]) * 0.125,
                mm_tn(p_ref[0, 0, p * 2 + side], da2 * sides[side]),
            ]
            total = parts if side == 0 else [a + b for a, b in zip(total, parts)]
            if side == 1:
                for part in range(3):
                    lo = part * half_width + p * 128
                    rounded = total[part].astype(bf16)
                    out_ref[0, :, lo : lo + 128] = rounded
                    if keep is not None:
                        rows = pl.ds(pl.program_id(0) * rounded.shape[0], rounded.shape[0])
                        keep[part, rows, p * 128 : (p + 1) * 128] = rounded
                    if part != 1:
                        sums_ref[:, lo : lo + 128] += fold_rows(rounded.astype(f32))


def gelu_parts(u):
    size = jnp.abs(u)
    t = 1.0 / (1.0 + size * (0.3275911 * 0.7071067811865476))
    bell = jnp.exp(u * u * -0.5)
    poly = t * (
        0.127414796
        + t * (-0.142248368 + t * (0.7107068705 + t * (-0.7265760135 + t * 0.5307027145)))
    )
    tail = poly * bell
    cdf = jnp.where(u < 0.0, tail, 1.0 - tail)
    return u * cdf, cdf + u * (bell * 0.3989422804014327)


def feed_stages(cut, vec_ref, ins, outs, sums_ref, slope, wa, wb, ready):
    x_ref, a_ref, cot_ref = ins
    out_ref, g_ref, du_ref, n1_ref, df_ref, db_ref, da_ref, dr1_ref = outs
    width = x_ref.shape[1]
    half = width // 2
    place = lambda j: (j // 2, (j % 2) * width)

    attended = a_ref[cut, :]
    branch = jnp.concatenate(
        [mm(attended, wa[h, :, :half]) for h in range(2)], axis=1
    ) + vec_ref[2:3, :]
    yield
    resid = x_ref[cut, :].astype(f32) + branch
    center = resid - row_mean(resid)
    rstd = lax.rsqrt(row_mean(center * center) + EPS)
    z1 = center * rstd
    n1 = z1 * (1.0 + vec_ref[3:4, :]) + vec_ref[4:5, :]
    n1b = n1.astype(bf16)
    n1_ref[cut, :] = n1b
    yield

    def up(j):
        h, lo = place(j)
        return mm(n1b, wa[h, :, half + lo : half + lo + width]) + vec_ref[8 + j : 9 + j, :]

    hidden = [up(0)]
    yield
    feed = None
    for j in range(4):
        if j < 3:
            hidden.append(up(j + 1))
            yield
        active, tilt = gelu_parts(hidden[j])
        hidden[j] = None
        active = active.astype(bf16)
        at = slice(j * width, (j + 1) * width)
        g_ref[cut, at] = active
        slope[cut, at] = tilt
        yield
        if j == 0:
            ready()
        h, lo = place(j)
        part = mm_nt(active, wb[h, :, lo : lo + width])
        feed = part if feed is None else feed + part
        yield
    resid2 = n1 + feed + vec_ref[7:8, :]
    center2 = resid2 - row_mean(resid2)
    rstd2 = lax.rsqrt(row_mean(center2 * center2) + EPS)
    z2 = center2 * rstd2
    gain2 = 1.0 + vec_ref[5:6, :]
    out_ref[cut, :] = (z2 * gain2 + vec_ref[6:7, :]).astype(bf16)
    dy = cot_ref[cut, :].astype(f32)
    s = dy * gain2
    dr2 = rstd2 * (s - row_mean(s) - z2 * row_mean(s * z2))
    df = dr2.astype(bf16)
    df_ref[cut, :] = df
    sums_ref[3] += fold_rows(dy * z2)
    sums_ref[4] += fold_rows(dy)
    sums_ref[5] += fold_rows(df.astype(f32))
    yield

    def back(j):
        h, lo = place(j)
        return mm(df, wb[h, :, lo : lo + width])

    d_active = [back(0)]
    yield
    dn1 = dr2
    for j in range(4):
        if j < 3:
            d_active.append(back(j + 1))
            yield
        at = slice(j * width, (j + 1) * width)
        du = (d_active[j] * slope[cut, at]).astype(bf16)
        d_active[j] = None
        du_ref[cut, at] = du
        sums_ref[6 + j] += fold_rows(du.astype(f32))
        yield
        h, lo = place(j)
        dn1 = dn1 + mm_nt(du, wa[h, :, half + lo : half + lo + width])
        yield
    sums_ref[0] += fold_rows(dn1 * z1)
    sums_ref[1] += fold_rows(dn1)
    s = dn1 * (1.0 + vec_ref[3:4, :])
    dr1 = rstd * (s - row_mean(s) - z1 * row_mean(s * z1))
    dr1_ref[cut, :] = dr1
    db = dr1.astype(bf16)
    db_ref[cut, :] = db
    sums_ref[2] += fold_rows(db.astype(f32))
    yield
    da = mm_nt(db[:, :half], wa[0, :, :half]) + mm_nt(db[:, half:], wa[1, :, :half])
    da_ref[cut, :] = da.astype(bf16)
    yield


def feed_both(n_a, n_b, sub, info, vec_ref, x_ref, a_ref, cot_ref, *refs):
    src_a = refs[:n_a]
    src_b = refs[n_a : n_a + n_b]
    refs = refs[n_a + n_b :]
    outs = refs[:8]
    sums_ref, slope, wa, wb, sems_a, sems_b = refs[8:]
    step = pl.program_id(0)
    copies_a = weight_copies(info, src_a, wa, sems_a)
    copies_b = weight_copies(info, src_b, wb, sems_b)

    @pl.when(step == 0)
    def _():
        for copy in copies_a + copies_b:
            copy.start()
        sums_ref[...] = jnp.zeros_like(sums_ref)
        for copy in copies_a:
            copy.wait()

    waited = []

    def ready():
        if not waited:
            waited.append(True)

            @pl.when(step == 0)
            def _():
                for copy in copies_b:
                    copy.wait()

    ins = (x_ref, a_ref, cot_ref)
    blocks = [
        feed_stages(slice(r, r + sub), vec_ref, ins, outs, sums_ref, slope, wa, wb, ready)
        for r in range(0, x_ref.shape[0], sub)
    ]
    waiting, t = list(range(len(blocks))), 0
    while waiting:
        for i in list(waiting):
            if t >= i and next(blocks[i], True):
                waiting.remove(i)
        t += 1


def token_gradient(n_src, info, other_ref, mine_ref, dr1_ref, *refs):
    src = refs[:n_src]
    out_ref, w, sems = refs[n_src:]
    used = mine_ref.shape[2]

    @pl.when(pl.program_id(0) == 0)
    def _():
        copies = weight_copies(info, src, w, sems)
        for copy in copies:
            copy.start()
        for copy in copies:
            copy.wait()

    out_ref[...] = (
        dr1_ref[...]
        + mm_nt(other_ref[0], w[1 - info[0], :, :used])
        + mm_nt(mine_ref[0], w[info[0], :, :used])
    )


def vector_rows(info, sums_ref, other_ref, mine_ref):
    total = lambda v: jnp.sum(v, axis=0, keepdims=True)
    half = other_ref.shape[1] // 3
    rows = []
    for part in (0, 2):
        cut = slice(part * half, (part + 1) * half)
        other, mine = total(other_ref[:, cut]), total(mine_ref[:, cut])
        first = jnp.where(info[0] == 0, mine, other)
        second = jnp.where(info[0] == 0, other, mine)
        rows.append(jnp.concatenate([first, second], axis=1))
    return rows + [total(sums_ref[i]) for i in (2, 0, 1, 3, 4, 5, 6, 7, 8, 9)]


RELAYED = (
    [(0, k) for k in range(4)],
    [(3, 0), (3, 1), (1, 0), (1, 1)],
    [(3, 2), (3, 3), (2, 2), (2, 3)],
    [(1, 2), (1, 3)],
    [(2, 0), (2, 1)],
)


def store_parts(info, value, outs, acc, recv, buffers):
    size = value.shape[1]
    if buffers is None:
        outs[0][:, :size] = value.astype(outs[0].dtype)
        return
    acc[:, :size] = value
    for out, slots in zip(outs, buffers):
        for j, (a, k) in enumerate(slots):
            row = chip_row(info, a, k, True)
            mine = acc[pl.ds(row, 48), :size]
            if recv is not None:
                mine = mine + recv[pl.ds(row, 48), :size].astype(f32)
            out[j, :, :size] = mine.astype(bf16)


def attention_weight(pairs, crops, buffers, info, qkv_ref, da_ref, p_ref, x_ref, *refs):
    if buffers is not None:
        recv, all_sums_ref, other_ref, spread_ref, pick_ref, *refs = refs
    out_ref, sums_ref, *outs, keep, acc = refs
    step = pl.program_id(0)

    @pl.when(step < crops)
    def _():
        attention_backward(pairs, info, qkv_ref, da_ref, p_ref, out_ref, sums_ref, keep)

    @pl.when((step >= crops) & (step < crops + 3))
    def _():
        value = mm_tn(x_ref[...], keep[jnp.clip(step - crops, 0, 2)])
        store_parts(info, value, outs, acc, None if buffers is None else recv, buffers)

    if buffers is not None:

        @pl.when(step == crops + 3)
        def _():
            rows = vector_rows(info, all_sums_ref, other_ref, sums_ref)
            picked = jnp.concatenate([(r * pick_ref[...]).astype(bf16) for r in rows], axis=0)
            store_parts(info, mm_nt(picked, spread_ref[...]), outs, acc, None, buffers)


def weight_gradient(starts, sizes, has_recv, buffers, info, *refs):
    count = len(starts)
    lhs = refs[:count]
    rhs = refs[count : 2 * count]
    at = 2 * count
    recv = None
    if has_recv:
        recv = refs[at]
        at += 1
    (*outs, acc) = refs[at:]
    step = pl.program_id(0)

    def store(value, add):
        store_parts(info, value, outs, acc, recv if add else None, buffers)

    for number, start in enumerate(starts):
        here = step >= start
        if number + 1 < count:
            here = here & (step < starts[number + 1])

        @pl.when(here)
        def _(number=number):
            right = rhs[number]
            right = right[0] if len(right.shape) == 3 else right[...]
            store(mm_tn(lhs[number][...], right), True)


def params():
    return pltpu.CompilerParams(
        dimension_semantics=("arbitrary",), vmem_limit_bytes=VMEM_LIMIT
    )


def call(kernel, grid, in_specs, out_specs, out_shape, scratch, flops, nbytes, name, after=()):
    def body(info, *refs):
        kernel(info, *refs[len(after) :])

    run = pl.pallas_call(
        body,
        grid_spec=pltpu.PrefetchScalarGridSpec(
            num_scalar_prefetch=1,
            grid=grid,
            in_specs=[ANY] * len(after) + in_specs,
            out_specs=out_specs,
            scratch_shapes=scratch,
        ),
        out_shape=out_shape,
        compiler_params=params(),
        cost_estimate=pl.CostEstimate(
            flops=int(flops * COST), bytes_accessed=int(nbytes * COST), transcendentals=0
        ),
        name=name,
    )
    return lambda info, *operands: run(info, *after, *operands)


def struct(shape, dtype):
    return jax.ShapeDtypeStruct(shape, dtype)


def whole_block(shape):
    return pl.BlockSpec(shape, lambda i, info: (0,) * len(shape))


def rows_block(rows, columns):
    return pl.BlockSpec((rows, columns), lambda i, info: (i, 0))


def spread_tables(width):
    per = width // 64
    e = np.arange(width)
    spread = (np.arange(EXT)[:, None] == (e % per)[None, :]).astype(np.float32)
    pick = (np.arange(64)[:, None] == (e // per)[None, :]).astype(np.float32)
    return spread, pick


def run_attention_forward(info, x, pieces, vec, crops, after):
    rows, width = x.shape
    slots = rows // crops
    half = width // 2
    w_columns = pieces[0].shape[-1]
    has_ext = vec is None
    pairs = half // 128
    if has_ext:
        spread, pick = spread_tables(width)
        extra = [jnp.asarray(spread, bf16), jnp.asarray(pick, f32)]
    else:
        extra = [vec]
    extra_specs = [whole_block(e.shape) for e in extra]
    kernel = functools.partial(attention_forward, len(pieces), has_ext, pairs)
    return call(
        kernel,
        (crops,),
        [rows_block(slots, width)] + [ANY] * len(pieces) + extra_specs,
        [
            whole_block((16, width)),
            pl.BlockSpec((2, slots, 3 * half), lambda i, info: (0, i, 0)),
            pl.BlockSpec((2, 1, H // 2, slots, slots), lambda i, info: (0, i, 0, 0, 0)),
            rows_block(slots, width),
        ],
        [
            struct((16, width), f32),
            struct((2, rows, 3 * half), bf16),
            struct((2, crops, H // 2, slots, slots), bf16),
            struct((rows, width), bf16),
        ],
        [
            pltpu.VMEM((2, width, w_columns), bf16),
            pltpu.VMEM((2, 1, 3 * half), f32),
            pltpu.SemaphoreType.DMA((sem_count(pieces),)),
        ],
        2 * rows * width * 3 * width + 8 * rows * slots * width,
        30e6,
        "attention_forward",
        after,
    )(info, x, *pieces, *extra)


def run_attention_backward(info, qkv, da, probs, crops, which, after):
    _, rows, columns = qkv.shape
    slots = rows // crops
    half = columns // 3

    def pick(info):
        return info[0] if which else 1 - info[0]

    kernel = functools.partial(attention_backward, half // 128)
    return call(
        kernel,
        (crops,),
        [
            pl.BlockSpec((1, slots, columns), lambda i, info: (pick(info), i, 0)),
            pl.BlockSpec((slots, half), lambda i, info: (i, pick(info))),
            pl.BlockSpec(
                (1, 1, H // 2, slots, slots), lambda i, info: (pick(info), i, 0, 0, 0)
            ),
        ],
        [
            pl.BlockSpec((1, slots, columns), lambda i, info: (0, i, 0)),
            whole_block((8, columns)),
        ],
        [struct((1, rows, columns), bf16), struct((8, columns), f32)],
        [],
        16 * rows * slots * half,
        12e6,
        "attention_backward",
        after,
    )(info, qkv, da, probs)


def run_attention_weight(info, qkv, da, probs, x, crops, which, more, after):
    _, rows, columns = qkv.shape
    width = x.shape[1]
    slots = rows // crops
    half = columns // 3
    pick = lambda info: info[0] if which else 1 - info[0]
    crop = lambda i: jnp.minimum(i, crops - 1)
    part = lambda i, last: jnp.clip(i - crops, 0, last)
    in_specs = [
        pl.BlockSpec((1, slots, columns), lambda i, info: (pick(info), crop(i), 0)),
        pl.BlockSpec((slots, half), lambda i, info: (crop(i), pick(info))),
        pl.BlockSpec(
            (1, 1, H // 2, slots, slots), lambda i, info: (pick(info), crop(i), 0, 0, 0)
        ),
        pl.BlockSpec((rows, width), lambda i, info: (0, 0), pipeline_mode=pl.Buffered(1)),
    ]
    operands = [qkv, da, probs, x]
    out_specs = [
        pl.BlockSpec((1, slots, columns), lambda i, info: (0, crop(i), 0)),
        whole_block((8, columns)),
    ]
    out_shape = [struct((1, rows, columns), bf16), struct((8, columns), f32)]
    if which:
        recv, sums, other = more
        spread, pick_rows = spread_tables(width)
        rest = [sums, other, jnp.asarray(spread, bf16), jnp.asarray(pick_rows, f32)]
        operands += [recv] + rest
        in_specs.append(pl.BlockSpec((width, half), lambda i, info: (0, part(i, 2))))
        in_specs += [whole_block(v.shape) for v in rest]
        out_specs += [
            pl.BlockSpec((len(b), 48, half), lambda i, info: (0, 0, part(i, 3))) for b in RELAYED
        ]
        out_shape += [struct((len(b), 48, columns + EXT), bf16) for b in RELAYED]
    else:
        out_specs.append(pl.BlockSpec((width, half), lambda i, info: (0, part(i, 2))))
        out_shape.append(struct((width, columns), bf16))
    kernel = functools.partial(attention_weight, half // 128, crops, RELAYED if which else None)
    out = call(
        kernel,
        (crops + 3 + which,),
        in_specs,
        out_specs,
        out_shape,
        [pltpu.VMEM((3, rows, half), bf16), pltpu.VMEM((width, half), f32)],
        16 * rows * slots * half + 2 * rows * width * columns,
        20e6,
        "attention_weight",
        after,
    )(info, *operands)
    return out[0], out[1], out[2:]


def run_feed(info, vec, x, attended, cot, pieces_a, pieces_b, block, sub, after):
    rows, width = x.shape
    ff = 2 * pieces_b[0].shape[-1]
    kernel = functools.partial(feed_both, len(pieces_a), len(pieces_b), sub)
    narrow, wide = rows_block(block, width), rows_block(block, ff)
    return call(
        kernel,
        (rows // block,),
        [whole_block(vec.shape)] + [narrow] * 3 + [ANY] * (len(pieces_a) + len(pieces_b)),
        [narrow, wide, wide] + [narrow] * 5 + [whole_block((10, 8, width))],
        [struct((rows, width), bf16), struct((rows, ff), bf16), struct((rows, ff), bf16)]
        + [struct((rows, width), bf16)] * 4
        + [struct((rows, width), f32), struct((10, 8, width), f32)],
        [
            pltpu.VMEM((block, ff), f32),
            pltpu.VMEM((2, width, pieces_a[0].shape[-1]), bf16),
            pltpu.VMEM((2, width, pieces_b[0].shape[-1]), bf16),
            pltpu.SemaphoreType.DMA((sem_count(pieces_a),)),
            pltpu.SemaphoreType.DMA((sem_count(pieces_b),)),
        ],
        4 * rows * width * (width + 2 * ff),
        53e6,
        "feed_both",
        after,
    )(info, vec, x, attended, cot, *pieces_a, *pieces_b)


def run_token_gradient(info, dqkv_by, dr1, pieces, block, after):
    rows, width = dr1.shape
    columns = dqkv_by[0].shape[2]
    kernel = functools.partial(token_gradient, len(pieces))
    return call(
        kernel,
        (rows // block,),
        [
            pl.BlockSpec((1, block, columns), lambda i, info: (0, i, 0)),
            pl.BlockSpec((1, block, columns), lambda i, info: (0, i, 0)),
            rows_block(block, width),
        ]
        + [ANY] * len(pieces),
        rows_block(block, width),
        struct((rows, width), f32),
        [
            pltpu.VMEM((2, width, pieces[0].shape[-1]), bf16),
            pltpu.SemaphoreType.DMA((sem_count(pieces),)),
        ],
        4 * rows * width * columns,
        20e6,
        "token_gradient",
        after,
    )(info, *dqkv_by, dr1, *pieces)


def run_weight_gradient(info, pairs, columns, block, pick, recv, full, after, buffers=None):
    rows, width = pairs[0][0].shape
    once = pl.Buffered(1)
    starts, sizes, step = [], [], 0
    rhs_specs = []
    for _, rhs, total, size in pairs:
        count = total // size
        starts.append(step)
        sizes.append(size)
        near = lambda i, step=step, count=count: jnp.clip(i - step, 0, count - 1)
        if rhs.ndim == 3:
            rhs_specs.append(
                pl.BlockSpec((1, rows, size), lambda i, info, near=near: (0, 0, near(i)))
            )
        else:
            rhs_specs.append(
                pl.BlockSpec(
                    (rows, size),
                    lambda i, info, near=near, count=count: (0, pick(info) * count + near(i)),
                )
            )
        step += count
    operands = [p[0] for p in pairs] + [p[1] for p in pairs]
    left = pl.BlockSpec((rows, width), lambda i, info: (0, 0), pipeline_mode=once)
    specs = [left for _ in pairs] + rhs_specs
    if recv is not None:
        recv, base = recv
        operands.append(recv)
        last = step - 1
        specs.append(
            pl.BlockSpec((width, block), lambda i, info: (0, base + jnp.minimum(i, last)))
        )
    if recv is None:
        out_specs = [pl.BlockSpec((width, block), lambda i, info: (0, i))]
        out_shape = [struct((width, columns), f32 if full else bf16)]
    else:
        out_specs = [
            pl.BlockSpec((len(b), 48, block), lambda i, info: (0, 0, i)) for b in buffers
        ]
        out_shape = [struct((len(b), 48, columns), bf16) for b in buffers]
    kernel = functools.partial(
        weight_gradient, tuple(starts), tuple(sizes), recv is not None, buffers
    )
    return call(
        kernel,
        (step,),
        specs,
        out_specs,
        out_shape,
        [pltpu.VMEM((width, block), f32)],
        2 * rows * width * columns,
        12e6,
        "weight_gradient",
        after,
    )(info, *operands)


def neighbours(n):
    flip = lambda bits: [(i, i ^ bits) for i in range(n)]
    shift = lambda k: [(i, (i + 8 * k) % n) for i in range(n)]
    ways = {"core": 1, "x": 2, "y": 4, "xy": 6, "z": 8, "zz": 16, "zzz": 24}
    return {way: flip(bits) for way, bits in ways.items()}, shift


def send(value, pairs):
    return lax.ppermute(value, "dp", pairs)


def chip_piece(core, first, second, n):
    flips, _ = neighbours(n)
    keep = jnp.where(core == 0, first, second)
    give = jnp.where(core == 0, second, first)
    got = send(give, flips["core"])
    return jnp.where(core == 0, jnp.concatenate([keep, got]), jnp.concatenate([got, keep]))


def along_z(piece, n):
    _, shift = neighbours(n)
    return jnp.concatenate([piece] + [send(piece, shift(k)) for k in (1, 2, 3)])


def across_relayed(base, n):
    flips, _ = neighbours(n)
    by_x, by_y = send(base, flips["x"]), send(base, flips["y"])
    mid = base.shape[0] // 2
    return [base, by_x, by_y, send(by_x[:mid], flips["y"]), send(by_y[mid:], flips["x"])]


def across_direct(base, n):
    flips, _ = neighbours(n)
    return [base] + [send(base, flips[way]) for way in ("x", "y", "xy")]


def both_cores(own, n):
    flips, _ = neighbours(n)
    return own + [send(v, flips["core"]) for v in own]


def behind(value, *others):
    return lax.optimization_barrier((value,) + others)[0]


def sum_first(chunks, n, *gates):
    flips, _ = neighbours(n)
    got = [(send(parts[1], flips["x"]), send(parts[2], flips["y"])) for parts in chunks]
    got = lax.optimization_barrier((got,) + gates)[0]
    beside = lambda values: jnp.concatenate(values, axis=2).astype(bf16)
    to_x = beside(
        [p[3].astype(f32) + got_y[:2].astype(f32) for p, (_, got_y) in zip(chunks, got)]
    )
    to_y = beside(
        [p[4].astype(f32) + got_x[:2].astype(f32) for p, (got_x, _) in zip(chunks, got)]
    )
    return got, to_x, to_y


def sum_rest(chunks, first, n, *gates):
    flips, _ = neighbours(n)
    got, to_x, to_y = first
    rest_x, rest_y = send(to_x, flips["x"]), send(to_y, flips["y"])
    got, rest_x, rest_y = lax.optimization_barrier((got, rest_x, rest_y) + gates)[:3]
    beside = lambda values: jnp.concatenate(values, axis=2)
    low = beside(
        [p[0][:2].astype(f32) + got_x[2:].astype(f32) for p, (got_x, _) in zip(chunks, got)]
    ) + rest_y.astype(f32)
    high = beside(
        [p[0][2:].astype(f32) + got_y[2:].astype(f32) for p, (_, got_y) in zip(chunks, got)]
    ) + rest_x.astype(f32)
    return [low[0]] + [v.astype(bf16) for v in (low[1], high[0], high[1])], rest_x


def share_rows(core, done, n):
    flips, _ = neighbours(n)
    rows = done.shape[0] // 2
    keep = jnp.where(core == 0, done[:rows], done[rows:])
    give = jnp.where(core == 0, done[rows:], done[:rows])
    got = send(give, flips["core"])
    return jnp.where(core == 0, keep, got), jnp.where(core == 0, got, keep)


def sum_to_owner(total, ways, n, *gates):
    flips, _ = neighbours(n)
    got = [send(value, flips[way]) for value, way in zip(total[1:], ways)]
    got = lax.optimization_barrier((got,) + gates)[0]
    return total[0] + sum(v.astype(f32) for v in got)


def sum_by_halves(total, n):
    flips, _ = neighbours(n)
    got = send(jnp.stack([total[1], total[3]]), flips["z"]).astype(f32)
    far = send((total[2].astype(f32) + got[1]).astype(bf16), flips["zz"])
    return total[0] + got[0] + far.astype(f32), far


def halves(matrix, groups):
    size = matrix.shape[1] // groups
    cut = size // 2
    return [
        jnp.concatenate(
            [matrix[:, g * size + h * cut : g * size + (h + 1) * cut] for g in range(groups)],
            axis=1,
        )
        for h in range(2)
    ]


def join(first, second, groups):
    rows, columns = first.shape
    shape = (rows, groups, 1, columns // groups)
    both = jnp.concatenate([first.reshape(shape), second.reshape(shape)], axis=2)
    return both.reshape(rows, 2 * columns)


def momentum_step(weight, copy):
    return (weight.astype(f32) - copy) * 0.0005


def momentum_all(info, *refs):
    count = len(refs) // 3
    for weight, copy, out in zip(refs[:count], refs[count : 2 * count], refs[2 * count :]):
        out[...] = momentum_step(weight[...], copy[...])


def run_momentum(info, weights, copies, after):
    blocks = [whole_block(w.shape) for w in weights]
    return call(
        momentum_all,
        (1,),
        blocks + blocks,
        blocks,
        [struct(w.shape, f32) for w in weights],
        [],
        0,
        0,
        "momentum",
        after,
    )(info, *weights, *copies)


def local(
    n,
    tokens,
    lengths,
    w_qkv,
    w_out,
    w_in,
    w_down,
    vector,
    key_qkv,
    key_out,
    key_in,
    key_down,
    key_vector,
    cotangent,
):
    width = tokens.shape[1]
    half = width // 2
    ff = w_in.shape[1]
    crops = lengths.shape[0]
    near = n == 32 and w_qkv.shape[0] == 24
    me = lax.axis_index("dp").astype(jnp.int32)
    core = me & 1
    place = jnp.stack([core, (me >> 1) & 1, (me >> 2) & 1, (me >> 3) & 3])
    info = jnp.concatenate([place, lengths.astype(jnp.int32)])

    qkv_halves = halves(w_qkv, 3)
    out_halves = halves(w_out, 1)
    in_halves = halves(w_in, 1)
    down_halves = halves(w_down, 1)
    mixed = [jnp.concatenate([out_halves[h], in_halves[h]], axis=1) for h in range(2)]
    if near:
        own_rows = w_qkv.shape[0]
        ext = jnp.pad(
            vector.reshape(own_rows, vector.shape[0] // own_rows),
            ((0, 0), (0, EXT - vector.shape[0] // own_rows)),
        )
        first = [jnp.concatenate([q, ext], axis=1) for q in qkv_halves]
        base = along_z(chip_piece(core, first[0], first[1], n), n)
        p_qkv = across_relayed(base, n)
        piece = chip_piece(core, mixed[0], mixed[1], n)
        base_mixed = along_z(behind(piece, base), n)
        p_mixed = across_direct(behind(base_mixed, *p_qkv), n)
        p_qkv = both_cores(p_qkv, n)
        p_down = [lax.all_gather(jnp.stack(down_halves), "dp", axis=1, tiled=True)]
        order = [base_mixed]
        vec = None
    else:
        everywhere = lambda pair: [
            lax.all_gather(jnp.stack(pair), "dp", axis=1, tiled=True)
        ]
        p_qkv, p_mixed, p_down = map(everywhere, (qkv_halves, mixed, down_halves))
        vec = lax.all_gather(vector, "dp", axis=0, tiled=True).astype(f32)
        vec = jnp.pad(vec.reshape(-1, width), ((0, 16 - vec.shape[0] // width), (0, 0)))
        order = []
        pairs = zip(
            (w_qkv, w_out, w_in, w_down, vector), (key_qkv, key_out, key_in, key_down, key_vector)
        )
        deltas = [momentum_step(weight, copy) for weight, copy in pairs]

    vec, qkv, probs, attended = run_attention_forward(info, tokens, p_qkv, vec, crops, order)
    if near:
        deltas = run_momentum(
            info,
            (w_qkv, w_out, w_in, w_down, vector.reshape(1, -1)),
            (key_qkv, key_out, key_in, key_down, key_vector.reshape(1, -1)),
            (attended,),
        )
        p_mixed = both_cores([behind(v, deltas[0]) for v in p_mixed], n)
    output, active, du, n1, df, db, da, dr1, sums = run_feed(
        info, vec, tokens, attended, cotangent, p_mixed, p_down, 512, 256, (deltas[0],)
    )
    down_pairs = [(df, active, ff // 2, width)]
    mixed_pairs = [(n1, du, ff // 2, width), (attended, db, half, half)]
    if near:
        flips, _ = neighbours(n)

        def mine(pairs, columns, base, after):
            return run_weight_gradient(
                info,
                pairs,
                columns,
                width,
                lambda info: info[0],
                (got_ff, base),
                False,
                after,
                RELAYED,
            )

        away_ff = run_weight_gradient(
            info,
            down_pairs + mixed_pairs,
            half + ff,
            width,
            lambda info: 1 - info[0],
            None,
            False,
            (),
        )[0]
        got_ff = send(away_ff, flips["core"])
        dqkv_other, sums_other, (away_qkv,) = run_attention_weight(
            info, qkv, da, probs, tokens, crops, 0, None, (away_ff,)
        )
        got_qkv = send(away_qkv, flips["core"])
        parts_down = mine(down_pairs, ff // 2, 0, (sums_other,))
        parts_mixed = mine(mixed_pairs, half + ff // 2, ff // 2 // width, (parts_down[0],))
        first_down = sum_first([parts_down], n, parts_mixed[0])
        dqkv_mine, sums_mine, parts_qkv = run_attention_weight(
            info,
            qkv,
            da,
            probs,
            tokens,
            crops,
            1,
            (got_qkv, sums, sums_other),
            (parts_mixed[0],) + first_down[1:],
        )
        first_mixed = sum_first([parts_mixed], n, sums_mine)
        total_down, _ = sum_rest([parts_down], first_down, n, sums_mine)
        total_mixed, arrived = sum_rest([parts_mixed], first_mixed, n)
        first_qkv = sum_first([parts_qkv], n, arrived)
        grad_tokens = run_token_gradient(
            info, [dqkv_other, dqkv_mine], dr1, p_qkv, 256, first_qkv[1:]
        )
        total_qkv, _ = sum_rest([parts_qkv], first_qkv, n, grad_tokens)
        done_down, _ = sum_by_halves(total_down, n)
        done_mixed, last = sum_by_halves(total_mixed, n)
        done_qkv = sum_to_owner(total_qkv, ("z", "zz", "zzz"), n, last)
        g_down = share_rows(core, done_down, n)
        g_mixed = share_rows(core, done_mixed, n)
        g_in = [v[:, : ff // 2] for v in g_mixed]
        g_out = [v[:, ff // 2 :] for v in g_mixed]
        g_qkv = share_rows(core, done_qkv, n)
        per = vector.shape[0] // w_qkv.shape[0]
        grad_down = join(g_down[0], g_down[1], 1)
        grad_vector = (g_qkv[0] + g_qkv[1])[:, 3 * half : 3 * half + per].reshape(-1)
        g_qkv = [v[:, : 3 * half] for v in g_qkv]
    else:

        def gradient(pairs_of, columns, block):
            return [
                run_weight_gradient(
                    info, pairs_of(h), columns, block, lambda info, h=h: h, None, True, ()
                )[0]
                for h in range(2)
            ]

        info_of = lambda h: info.at[0].set(h)
        results = [
            run_attention_backward(info_of(h), qkv, da, probs, crops, 1, ()) for h in range(2)
        ]
        dqkv_by = [r[0] for r in results]
        bias_sums = jnp.stack([jnp.sum(r[1], axis=0) for r in results]).reshape(2, 3, half)
        sums = jnp.sum(sums, axis=1)
        vec_grad = jnp.concatenate(
            [bias_sums[:, 0].reshape(-1), bias_sums[:, 2].reshape(-1)]
            + [sums[i] for i in (2, 0, 1, 3, 4, 5, 6, 7, 8, 9)]
        )
        g_down = gradient(lambda h: down_pairs, ff // 2, width)
        g_mixed = gradient(lambda h: mixed_pairs, half + ff // 2, width)
        g_in = [v[:, : ff // 2] for v in g_mixed]
        g_out = [v[:, ff // 2 :] for v in g_mixed]
        grad_down = join(g_down[0], g_down[1], 1)
        g_qkv = gradient(lambda h: [(tokens, dqkv_by[h], 3 * half, half)], 3 * half, half)
        grad_vector = lax.psum_scatter(vec_grad, "dp", scatter_dimension=0, tiled=True)
        grad_tokens = run_token_gradient(info_of(1), dqkv_by, dr1, p_qkv, 256, ())
    grad_qkv = join(g_qkv[0], g_qkv[1], 3)
    grad_out = join(g_out[0], g_out[1], 1)
    grad_in = join(g_in[0], g_in[1], 1)
    if not near:
        grad_qkv, grad_out, grad_in, grad_down = (
            lax.psum_scatter(g, "dp", scatter_dimension=0, tiled=True)
            for g in (grad_qkv, grad_out, grad_in, grad_down)
        )
    return (
        output,
        grad_tokens,
        grad_qkv,
        grad_out,
        grad_in,
        grad_down,
        grad_vector,
        *deltas[:4],
        deltas[4].reshape(-1),
    )


def solution(mesh):
    n = mesh.shape["dp"]
    rows, flat = P("dp", None), P("dp")
    return jax.shard_map(
        functools.partial(local, n),
        mesh=mesh,
        in_specs=(rows, flat, rows, rows, rows, rows, flat, rows, rows, rows, rows, flat, rows),
        out_specs=(rows, rows, rows, rows, rows, rows, flat, rows, rows, rows, rows, flat),
        check_vma=False,
    )
```

```python
import functools

import jax
import jax.numpy as jnp
import numpy as np
from jax import lax
from jax.experimental import pallas as pl
from jax.experimental.pallas import tpu as pltpu
from jax.sharding import PartitionSpec as P

H = 12
EPS = 1e-12
EXT = 128
bf16 = jnp.bfloat16
f32 = jnp.float32
VMEM_LIMIT = 60 * 1024 * 1024
COST = 0.001
ANY = pl.BlockSpec(memory_space=pl.ANY)

NT = (((1,), (1,)), ((), ()))
TN = (((0,), (0,)), ((), ()))


def mm(a, b):
    return jnp.dot(a, b, preferred_element_type=f32)


def mm_nt(a, b):
    return lax.dot_general(a, b, NT, preferred_element_type=f32)


def mm_tn(a, b):
    return lax.dot_general(a, b, TN, preferred_element_type=f32)


def row_mean(v):
    return jnp.mean(v, axis=-1, keepdims=True)


def fold_rows(v):
    return jnp.sum(v.reshape(v.shape[0] // 8, 8, v.shape[1]), axis=0)


def chip_row(info, a, k, flip):
    x, y, z = info[1], info[2], info[3]
    xx = x ^ (a & 1)
    yy = y ^ (a >> 1)
    zz = z ^ k if flip else (z - k + 4) & 3
    return pl.multiple_of(((zz * 2 + yy) * 2 + xx) * 48, 16)


LAYER_LAST = tuple([(a, k) for k in range(4)] for a in range(3)) + (
    [(3, 0), (3, 1)],
    [(3, 2), (3, 3)],
)
Z_LAST = tuple([(a, k) for a in range(4)] for k in (0, 1, 3)) + (
    [(0, 2), (1, 2)],
    [(2, 2), (3, 2)],
)


def weight_copies(info, refs, w, sems, places=LAYER_LAST):
    if len(refs) == 1:
        return [pltpu.make_async_copy(refs[0], w, sems.at[0])]
    out = []
    for source in range(2):
        half = info[0] if source == 0 else 1 - info[0]
        for number, slots in enumerate(places):
            ref = refs[source * len(places) + number]
            for j, (a, k) in enumerate(slots):
                row = chip_row(info, a, k, False)
                out.append(
                    pltpu.make_async_copy(
                        ref.at[pl.ds(48 * j, 48)],
                        w.at[half, pl.ds(row, 48)],
                        sems.at[len(out)],
                    )
                )
    return out


def sem_count(pieces):
    return 1 if len(pieces) == 1 else 32


def attention_forward(n_src, has_ext, pairs, info, x_ref, *refs):
    weights, copies_in, deltas = refs[:5], refs[5:10], refs[-8:-3]
    refs = refs[10:-8] + refs[-3:]
    src = refs[:n_src]
    if has_ext:
        spread_ref, pick_ref = refs[n_src : n_src + 2]
        refs = refs[n_src + 2 :]
    else:
        vec_in = refs[n_src]
        refs = refs[n_src + 1 :]
    vec_ref, qkv_ref, p_ref, a_ref, w, bias, sems = refs
    crop = pl.program_id(0)
    half_width = pairs * 128

    @pl.when(crop == 0)
    def _():
        copies = weight_copies(info, src, w, sems)
        for copy in copies:
            copy.start()
        for copy in copies:
            copy.wait()
        if has_ext:
            spread = mm(w[0, :, 3 * half_width :], spread_ref[...])
            groups = spread.shape[0] // 64
            picked = spread.reshape(groups, 64, spread.shape[1]) * pick_ref[...][None]
            vec_ref[0:groups, :] = jnp.sum(picked, axis=1)
        else:
            vec_ref[...] = vec_in[...]
        for h in range(2):
            for part, row in ((0, 0), (2, 1)):
                bias[h, :, part * half_width : (part + 1) * half_width] = vec_ref[
                    row : row + 1, h * half_width : (h + 1) * half_width
                ]
            bias[h, :, half_width : 2 * half_width] = jnp.zeros((1, half_width), f32)

    @pl.when(crop == 1)
    def _():
        for weight, old, out in zip(weights, copies_in, deltas):
            out[...] = (weight[...].astype(f32) - old[...]) * 0.0005

    x = x_ref[...]
    slots = x.shape[0]
    length = info[4 + crop]
    usable = lax.broadcasted_iota(jnp.int32, (1, slots), 1) < length
    mask_row = jnp.where(usable, 0.0, -1e30).astype(f32)
    lane = lax.broadcasted_iota(jnp.int32, (1, 128), 1)
    sides = (
        jnp.where(lane < 64, 1.0, 0.0).astype(bf16),
        jnp.where(lane < 64, 0.0, 1.0).astype(bf16),
    )
    units = [(h, p, side) for h in range(2) for p in range(pairs) for side in range(2)]

    def project(h):
        qkv_ref[h] = (mm(x, w[h, :, : 3 * half_width]) + bias[h]).astype(bf16)

    def columns(h, part, p):
        lo = part * half_width + p * 128
        return qkv_ref[h, :, lo : lo + 128]

    scores, probs, first = {}, {}, None
    project(0)
    for t in range(len(units) + 4):
        if t == 3:
            project(1)
        if t < len(units):
            h, p, side = units[t]
            q2 = columns(h, 0, p) * jnp.asarray(0.125, bf16)
            scores[t] = mm_nt(q2, columns(h, 1, p) * sides[side]) + mask_row
        if 0 <= t - 3 < len(units):
            h, p, side = units[t - 3]
            value = scores.pop(t - 3)
            terms = jnp.exp(value - jnp.max(value, axis=1, keepdims=True))
            mass = jnp.sum(terms, axis=1, keepdims=True)
            rounded = (terms * (1.0 / mass)).astype(bf16)
            p_ref[h, 0, p * 2 + side] = rounded
            probs[t - 3] = rounded
        if 0 <= t - 4 < len(units):
            h, p, side = units[t - 4]
            part = mm(probs.pop(t - 4), columns(h, 2, p) * sides[side])
            if side == 0:
                first = part
            else:
                lo = h * half_width + p * 128
                a_ref[:, lo : lo + 128] = (first + part).astype(bf16)


def attention_backward(pairs, info, qkv_ref, da_ref, p_ref, out_ref, sums_ref, keep=None):
    half_width = pairs * 128
    lane = lax.broadcasted_iota(jnp.int32, (1, 128), 1)
    sides = (
        jnp.where(lane < 64, 1.0, 0.0).astype(bf16),
        jnp.where(lane < 64, 0.0, 1.0).astype(bf16),
    )

    @pl.when(pl.program_id(0) == 0)
    def _():
        sums_ref[...] = jnp.zeros_like(sums_ref)

    units = [(p, side) for p in range(pairs) for side in range(2)]

    def columns(part, p):
        lo = part * half_width + p * 128
        return qkv_ref[0, :, lo : lo + 128]

    d_probs, d_scores, total = {}, {}, None
    for t in range(len(units) + 4):
        if t < len(units):
            p, side = units[t]
            da2 = da_ref[:, p * 128 : (p + 1) * 128]
            d_probs[t] = mm_nt(da2, columns(2, p) * sides[side])
        if 0 <= t - 2 < len(units):
            p, side = units[t - 2]
            probs = p_ref[0, 0, p * 2 + side].astype(f32)
            value = d_probs.pop(t - 2)
            inner = jnp.sum(probs * value, axis=1, keepdims=True)
            d_scores[t - 2] = (probs * (value - inner)).astype(bf16)
        if 0 <= t - 4 < len(units):
            p, side = units[t - 4]
            value = d_scores.pop(t - 4)
            da2 = da_ref[:, p * 128 : (p + 1) * 128]
            parts = [
                mm(value, columns(1, p) * sides[side]) * 0.125,
                mm_tn(value, columns(0, p) * sides[side]) * 0.125,
                mm_tn(p_ref[0, 0, p * 2 + side], da2 * sides[side]),
            ]
            total = parts if side == 0 else [a + b for a, b in zip(total, parts)]
            if side == 1:
                for part in range(3):
                    lo = part * half_width + p * 128
                    rounded = total[part].astype(bf16)
                    out_ref[0, :, lo : lo + 128] = rounded
                    if keep is not None:
                        rows = pl.ds(pl.program_id(0) * rounded.shape[0], rounded.shape[0])
                        keep[part, rows, p * 128 : (p + 1) * 128] = rounded
                    if part != 1:
                        sums_ref[:, lo : lo + 128] += fold_rows(rounded.astype(f32))


def gelu_parts(u):
    size = jnp.abs(u)
    t = 1.0 / (1.0 + size * (0.3275911 * 0.7071067811865476))
    bell = jnp.exp(u * u * -0.5)
    poly = t * (
        0.127414796
        + t * (-0.142248368 + t * (0.7107068705 + t * (-0.7265760135 + t * 0.5307027145)))
    )
    tail = poly * bell
    cdf = jnp.where(u < 0.0, tail, 1.0 - tail)
    return u * cdf, cdf + u * (bell * 0.3989422804014327)


def feed_stages(cut, vec_ref, ins, outs, sums_ref, slope, wa, wb, ready):
    x_ref, a_ref, cot_ref = ins
    out_ref, g_ref, du_ref, n1_ref, df_ref, db_ref, da_ref, dr1_ref = outs
    width = x_ref.shape[1]
    half = width // 2
    place = lambda j: (j // 2, (j % 2) * width)

    attended = a_ref[cut, :]
    branch = jnp.concatenate(
        [mm(attended, wa[h, :, :half]) for h in range(2)], axis=1
    ) + vec_ref[2:3, :]
    yield
    resid = x_ref[cut, :].astype(f32) + branch
    center = resid - row_mean(resid)
    rstd = lax.rsqrt(row_mean(center * center) + EPS)
    z1 = center * rstd
    n1 = z1 * (1.0 + vec_ref[3:4, :]) + vec_ref[4:5, :]
    n1b = n1.astype(bf16)
    n1_ref[cut, :] = n1b
    yield

    def up(j):
        h, lo = place(j)
        return mm(n1b, wa[h, :, half + lo : half + lo + width]) + vec_ref[8 + j : 9 + j, :]

    hidden = [up(0)]
    yield
    feed = None
    for j in range(4):
        if j < 3:
            hidden.append(up(j + 1))
            yield
        active, tilt = gelu_parts(hidden[j])
        hidden[j] = None
        active = active.astype(bf16)
        at = slice(j * width, (j + 1) * width)
        g_ref[cut, at] = active
        slope[cut, at] = tilt
        yield
        if j == 0:
            ready()
        h, lo = place(j)
        part = mm_nt(active, wb[h, :, lo : lo + width])
        feed = part if feed is None else feed + part
        yield
    resid2 = n1 + feed + vec_ref[7:8, :]
    center2 = resid2 - row_mean(resid2)
    rstd2 = lax.rsqrt(row_mean(center2 * center2) + EPS)
    z2 = center2 * rstd2
    gain2 = 1.0 + vec_ref[5:6, :]
    out_ref[cut, :] = (z2 * gain2 + vec_ref[6:7, :]).astype(bf16)
    dy = cot_ref[cut, :].astype(f32)
    s = dy * gain2
    dr2 = rstd2 * (s - row_mean(s) - z2 * row_mean(s * z2))
    df = dr2.astype(bf16)
    df_ref[cut, :] = df
    sums_ref[3] += fold_rows(dy * z2)
    sums_ref[4] += fold_rows(dy)
    sums_ref[5] += fold_rows(df.astype(f32))
    yield

    def back(j):
        h, lo = place(j)
        return mm(df, wb[h, :, lo : lo + width])

    d_active = [back(0)]
    yield
    dn1 = dr2
    for j in range(4):
        if j < 3:
            d_active.append(back(j + 1))
            yield
        at = slice(j * width, (j + 1) * width)
        du = (d_active[j] * slope[cut, at]).astype(bf16)
        d_active[j] = None
        du_ref[cut, at] = du
        sums_ref[6 + j] += fold_rows(du.astype(f32))
        yield
        h, lo = place(j)
        dn1 = dn1 + mm_nt(du, wa[h, :, half + lo : half + lo + width])
        yield
    sums_ref[0] += fold_rows(dn1 * z1)
    sums_ref[1] += fold_rows(dn1)
    s = dn1 * (1.0 + vec_ref[3:4, :])
    dr1 = rstd * (s - row_mean(s) - z1 * row_mean(s * z1))
    dr1_ref[cut, :] = dr1
    db = dr1.astype(bf16)
    db_ref[cut, :] = db
    sums_ref[2] += fold_rows(db.astype(f32))
    yield
    da = mm_nt(db[:, :half], wa[0, :, :half]) + mm_nt(db[:, half:], wa[1, :, :half])
    da_ref[cut, :] = da.astype(bf16)
    yield


def feed_both(n_a, n_b, sub, info, vec_ref, x_ref, a_ref, cot_ref, *refs):
    src_a = refs[:n_a]
    src_b = refs[n_a : n_a + n_b]
    refs = refs[n_a + n_b :]
    outs = refs[:8]
    sums_ref, slope, wa, wb, sems_a, sems_b = refs[8:]
    step = pl.program_id(0)
    copies_a = weight_copies(info, src_a, wa, sems_a)
    copies_b = weight_copies(info, src_b, wb, sems_b, Z_LAST)

    @pl.when(step == 0)
    def _():
        for copy in copies_a + copies_b:
            copy.start()
        sums_ref[...] = jnp.zeros_like(sums_ref)
        for copy in copies_a:
            copy.wait()

    waited = []

    def ready():
        if not waited:
            waited.append(True)

            @pl.when(step == 0)
            def _():
                for copy in copies_b:
                    copy.wait()

    ins = (x_ref, a_ref, cot_ref)
    blocks = [
        feed_stages(slice(r, r + sub), vec_ref, ins, outs, sums_ref, slope, wa, wb, ready)
        for r in range(0, x_ref.shape[0], sub)
    ]
    waiting, t = list(range(len(blocks))), 0
    while waiting:
        for i in list(waiting):
            if t >= i and next(blocks[i], True):
                waiting.remove(i)
        t += 1


def token_gradient(n_src, info, other_ref, mine_ref, dr1_ref, *refs):
    src = refs[:n_src]
    out_ref, w, sems = refs[n_src:]
    used = mine_ref.shape[2]

    @pl.when(pl.program_id(0) == 0)
    def _():
        copies = weight_copies(info, src, w, sems)
        for copy in copies:
            copy.start()
        for copy in copies:
            copy.wait()

    out_ref[...] = (
        dr1_ref[...]
        + mm_nt(other_ref[0], w[1 - info[0], :, :used])
        + mm_nt(mine_ref[0], w[info[0], :, :used])
    )


def vector_rows(info, sums_ref, other_ref, mine_ref):
    total = lambda v: jnp.sum(v, axis=0, keepdims=True)
    half = other_ref.shape[1] // 3
    rows = []
    for part in (0, 2):
        cut = slice(part * half, (part + 1) * half)
        other, mine = total(other_ref[:, cut]), total(mine_ref[:, cut])
        first = jnp.where(info[0] == 0, mine, other)
        second = jnp.where(info[0] == 0, other, mine)
        rows.append(jnp.concatenate([first, second], axis=1))
    return rows + [total(sums_ref[i]) for i in (2, 0, 1, 3, 4, 5, 6, 7, 8, 9)]


RELAYED = (
    [(0, k) for k in range(4)],
    [(3, 0), (3, 1), (1, 0), (1, 1)],
    [(3, 2), (3, 3), (2, 2), (2, 3)],
    [(1, 2), (1, 3)],
    [(2, 0), (2, 1)],
)


def store_parts(info, value, outs, acc, recv, buffers):
    size = value.shape[1]
    if buffers is None:
        outs[0][:, :size] = value.astype(outs[0].dtype)
        return
    acc[:, :size] = value
    for out, slots in zip(outs, buffers):
        for j, (a, k) in enumerate(slots):
            row = chip_row(info, a, k, True)
            mine = acc[pl.ds(row, 48), :size]
            if recv is not None:
                mine = mine + recv[pl.ds(row, 48), :size].astype(f32)
            out[j, :, :size] = mine.astype(bf16)


def attention_weight(pairs, crops, buffers, info, qkv_ref, da_ref, p_ref, x_ref, *refs):
    if buffers is not None:
        recv, all_sums_ref, other_ref, spread_ref, pick_ref, *refs = refs
    out_ref, sums_ref, *outs, keep, acc = refs
    step = pl.program_id(0)

    @pl.when(step < crops)
    def _():
        attention_backward(pairs, info, qkv_ref, da_ref, p_ref, out_ref, sums_ref, keep)

    @pl.when((step >= crops) & (step < crops + 3))
    def _():
        value = mm_tn(x_ref[...], keep[jnp.clip(step - crops, 0, 2)])
        store_parts(info, value, outs, acc, None if buffers is None else recv, buffers)

    if buffers is not None:

        @pl.when(step == crops + 3)
        def _():
            rows = vector_rows(info, all_sums_ref, other_ref, sums_ref)
            picked = jnp.concatenate([(r * pick_ref[...]).astype(bf16) for r in rows], axis=0)
            store_parts(info, mm_nt(picked, spread_ref[...]), outs, acc, None, buffers)


def weight_gradient(starts, sizes, has_recv, buffers, info, *refs):
    count = len(starts)
    lhs = refs[:count]
    rhs = refs[count : 2 * count]
    at = 2 * count
    recv = None
    if has_recv:
        recv = refs[at]
        at += 1
    (*outs, acc) = refs[at:]
    step = pl.program_id(0)

    def store(value, add):
        store_parts(info, value, outs, acc, recv if add else None, buffers)

    for number, start in enumerate(starts):
        here = step >= start
        if number + 1 < count:
            here = here & (step < starts[number + 1])

        @pl.when(here)
        def _(number=number):
            right = rhs[number]
            right = right[0] if len(right.shape) == 3 else right[...]
            store(mm_tn(lhs[number][...], right), True)


def params():
    return pltpu.CompilerParams(
        dimension_semantics=("arbitrary",), vmem_limit_bytes=VMEM_LIMIT
    )


def call(kernel, grid, in_specs, out_specs, out_shape, scratch, flops, nbytes, name, after=()):
    def body(info, *refs):
        kernel(info, *refs[len(after) :])

    run = pl.pallas_call(
        body,
        grid_spec=pltpu.PrefetchScalarGridSpec(
            num_scalar_prefetch=1,
            grid=grid,
            in_specs=[ANY] * len(after) + in_specs,
            out_specs=out_specs,
            scratch_shapes=scratch,
        ),
        out_shape=out_shape,
        compiler_params=params(),
        cost_estimate=pl.CostEstimate(
            flops=int(flops * COST), bytes_accessed=int(nbytes * COST), transcendentals=0
        ),
        name=name,
    )
    return lambda info, *operands: run(info, *after, *operands)


def struct(shape, dtype):
    return jax.ShapeDtypeStruct(shape, dtype)


def whole_block(shape):
    return pl.BlockSpec(shape, lambda i, info: (0,) * len(shape))


def rows_block(rows, columns):
    return pl.BlockSpec((rows, columns), lambda i, info: (i, 0))


def spread_tables(width):
    per = width // 64
    e = np.arange(width)
    spread = (np.arange(EXT)[:, None] == (e % per)[None, :]).astype(np.float32)
    pick = (np.arange(64)[:, None] == (e // per)[None, :]).astype(np.float32)
    return spread, pick


def run_attention_forward(info, x, weights, copies, pieces, vec, crops, after):
    rows, width = x.shape
    slots = rows // crops
    half = width // 2
    w_columns = pieces[0].shape[-1]
    has_ext = vec is None
    pairs = half // 128
    if has_ext:
        spread, pick = spread_tables(width)
        extra = [jnp.asarray(spread, bf16), jnp.asarray(pick, f32)]
    else:
        extra = [vec]
    extra_specs = [whole_block(e.shape) for e in extra]
    kernel = functools.partial(attention_forward, len(pieces), has_ext, pairs)
    return call(
        kernel,
        (crops,),
        [rows_block(slots, width)]
        + [whole_block(w.shape) for w in weights + copies]
        + [ANY] * len(pieces)
        + extra_specs,
        [
            whole_block((16, width)),
            pl.BlockSpec((2, slots, 3 * half), lambda i, info: (0, i, 0)),
            pl.BlockSpec((2, 1, H // 2, slots, slots), lambda i, info: (0, i, 0, 0, 0)),
            rows_block(slots, width),
        ]
        + [whole_block(w.shape) for w in weights],
        [
            struct((16, width), f32),
            struct((2, rows, 3 * half), bf16),
            struct((2, crops, H // 2, slots, slots), bf16),
            struct((rows, width), bf16),
        ]
        + [struct(w.shape, f32) for w in weights],
        [
            pltpu.VMEM((2, width, w_columns), bf16),
            pltpu.VMEM((2, 1, 3 * half), f32),
            pltpu.SemaphoreType.DMA((sem_count(pieces),)),
        ],
        2 * rows * width * 3 * width + 8 * rows * slots * width,
        30e6,
        "attention_forward",
        after,
    )(info, x, *weights, *copies, *pieces, *extra)


def run_attention_backward(info, qkv, da, probs, crops, which, after):
    _, rows, columns = qkv.shape
    slots = rows // crops
    half = columns // 3

    def pick(info):
        return info[0] if which else 1 - info[0]

    kernel = functools.partial(attention_backward, half // 128)
    return call(
        kernel,
        (crops,),
        [
            pl.BlockSpec((1, slots, columns), lambda i, info: (pick(info), i, 0)),
            pl.BlockSpec((slots, half), lambda i, info: (i, pick(info))),
            pl.BlockSpec(
                (1, 1, H // 2, slots, slots), lambda i, info: (pick(info), i, 0, 0, 0)
            ),
        ],
        [
            pl.BlockSpec((1, slots, columns), lambda i, info: (0, i, 0)),
            whole_block((8, columns)),
        ],
        [struct((1, rows, columns), bf16), struct((8, columns), f32)],
        [],
        16 * rows * slots * half,
        12e6,
        "attention_backward",
        after,
    )(info, qkv, da, probs)


def run_attention_weight(info, qkv, da, probs, x, crops, which, more, after):
    _, rows, columns = qkv.shape
    width = x.shape[1]
    slots = rows // crops
    half = columns // 3
    pick = lambda info: info[0] if which else 1 - info[0]
    crop = lambda i: jnp.minimum(i, crops - 1)
    part = lambda i, last: jnp.clip(i - crops, 0, last)
    in_specs = [
        pl.BlockSpec((1, slots, columns), lambda i, info: (pick(info), crop(i), 0)),
        pl.BlockSpec((slots, half), lambda i, info: (crop(i), pick(info))),
        pl.BlockSpec(
            (1, 1, H // 2, slots, slots), lambda i, info: (pick(info), crop(i), 0, 0, 0)
        ),
        pl.BlockSpec((rows, width), lambda i, info: (0, 0), pipeline_mode=pl.Buffered(1)),
    ]
    operands = [qkv, da, probs, x]
    out_specs = [
        pl.BlockSpec((1, slots, columns), lambda i, info: (0, crop(i), 0)),
        whole_block((8, columns)),
    ]
    out_shape = [struct((1, rows, columns), bf16), struct((8, columns), f32)]
    if which:
        recv, sums, other = more
        spread, pick_rows = spread_tables(width)
        rest = [sums, other, jnp.asarray(spread, bf16), jnp.asarray(pick_rows, f32)]
        operands += [recv] + rest
        in_specs.append(pl.BlockSpec((width, half), lambda i, info: (0, part(i, 2))))
        in_specs += [whole_block(v.shape) for v in rest]
        out_specs += [
            pl.BlockSpec((len(b), 48, half), lambda i, info: (0, 0, part(i, 3))) for b in RELAYED
        ]
        out_shape += [struct((len(b), 48, columns + EXT), bf16) for b in RELAYED]
    else:
        out_specs.append(pl.BlockSpec((width, half), lambda i, info: (0, part(i, 2))))
        out_shape.append(struct((width, columns), bf16))
    kernel = functools.partial(attention_weight, half // 128, crops, RELAYED if which else None)
    out = call(
        kernel,
        (crops + 3 + which,),
        in_specs,
        out_specs,
        out_shape,
        [pltpu.VMEM((3, rows, half), bf16), pltpu.VMEM((width, half), f32)],
        16 * rows * slots * half + 2 * rows * width * columns,
        20e6,
        "attention_weight",
        after,
    )(info, *operands)
    return out[0], out[1], out[2:]


def run_feed(info, vec, x, attended, cot, pieces_a, pieces_b, block, sub, after):
    rows, width = x.shape
    ff = 2 * pieces_b[0].shape[-1]
    kernel = functools.partial(feed_both, len(pieces_a), len(pieces_b), sub)
    narrow, wide = rows_block(block, width), rows_block(block, ff)
    return call(
        kernel,
        (rows // block,),
        [whole_block(vec.shape)] + [narrow] * 3 + [ANY] * (len(pieces_a) + len(pieces_b)),
        [narrow, wide, wide] + [narrow] * 5 + [whole_block((10, 8, width))],
        [struct((rows, width), bf16), struct((rows, ff), bf16), struct((rows, ff), bf16)]
        + [struct((rows, width), bf16)] * 4
        + [struct((rows, width), f32), struct((10, 8, width), f32)],
        [
            pltpu.VMEM((block, ff), f32),
            pltpu.VMEM((2, width, pieces_a[0].shape[-1]), bf16),
            pltpu.VMEM((2, width, pieces_b[0].shape[-1]), bf16),
            pltpu.SemaphoreType.DMA((sem_count(pieces_a),)),
            pltpu.SemaphoreType.DMA((sem_count(pieces_b),)),
        ],
        4 * rows * width * (width + 2 * ff),
        53e6,
        "feed_both",
        after,
    )(info, vec, x, attended, cot, *pieces_a, *pieces_b)


def run_token_gradient(info, dqkv_by, dr1, pieces, block, after):
    rows, width = dr1.shape
    columns = dqkv_by[0].shape[2]
    kernel = functools.partial(token_gradient, len(pieces))
    return call(
        kernel,
        (rows // block,),
        [
            pl.BlockSpec((1, block, columns), lambda i, info: (0, i, 0)),
            pl.BlockSpec((1, block, columns), lambda i, info: (0, i, 0)),
            rows_block(block, width),
        ]
        + [ANY] * len(pieces),
        rows_block(block, width),
        struct((rows, width), f32),
        [
            pltpu.VMEM((2, width, pieces[0].shape[-1]), bf16),
            pltpu.SemaphoreType.DMA((sem_count(pieces),)),
        ],
        4 * rows * width * columns,
        20e6,
        "token_gradient",
        after,
    )(info, *dqkv_by, dr1, *pieces)


def run_weight_gradient(info, pairs, columns, block, pick, recv, full, after, buffers=None):
    rows, width = pairs[0][0].shape
    once = pl.Buffered(1)
    starts, sizes, step = [], [], 0
    rhs_specs = []
    for _, rhs, total, size in pairs:
        count = total // size
        starts.append(step)
        sizes.append(size)
        near = lambda i, step=step, count=count: jnp.clip(i - step, 0, count - 1)
        if rhs.ndim == 3:
            rhs_specs.append(
                pl.BlockSpec((1, rows, size), lambda i, info, near=near: (0, 0, near(i)))
            )
        else:
            rhs_specs.append(
                pl.BlockSpec(
                    (rows, size),
                    lambda i, info, near=near, count=count: (0, pick(info) * count + near(i)),
                )
            )
        step += count
    operands = [p[0] for p in pairs] + [p[1] for p in pairs]
    left = pl.BlockSpec((rows, width), lambda i, info: (0, 0), pipeline_mode=once)
    specs = [left for _ in pairs] + rhs_specs
    if recv is not None:
        recv, base = recv
        operands.append(recv)
        last = step - 1
        specs.append(
            pl.BlockSpec((width, block), lambda i, info: (0, base + jnp.minimum(i, last)))
        )
    if recv is None:
        out_specs = [pl.BlockSpec((width, block), lambda i, info: (0, i))]
        out_shape = [struct((width, columns), f32 if full else bf16)]
    else:
        out_specs = [
            pl.BlockSpec((len(b), 48, block), lambda i, info: (0, 0, i)) for b in buffers
        ]
        out_shape = [struct((len(b), 48, columns), bf16) for b in buffers]
    kernel = functools.partial(
        weight_gradient, tuple(starts), tuple(sizes), recv is not None, buffers
    )
    return call(
        kernel,
        (step,),
        specs,
        out_specs,
        out_shape,
        [pltpu.VMEM((width, block), f32)],
        2 * rows * width * columns,
        12e6,
        "weight_gradient",
        after,
    )(info, *operands)


def neighbours(n):
    flip = lambda bits: [(i, i ^ bits) for i in range(n)]
    shift = lambda k: [(i, (i + 8 * k) % n) for i in range(n)]
    ways = {"core": 1, "x": 2, "y": 4, "xy": 6, "z": 8, "zz": 16, "zzz": 24}
    return {way: flip(bits) for way, bits in ways.items()}, shift


def send(value, pairs):
    return lax.ppermute(value, "dp", pairs)


def chip_piece(core, first, second, n):
    flips, _ = neighbours(n)
    keep = jnp.where(core == 0, first, second)
    give = jnp.where(core == 0, second, first)
    got = send(give, flips["core"])
    return jnp.where(core == 0, jnp.concatenate([keep, got]), jnp.concatenate([got, keep]))


def along_z(piece, n):
    _, shift = neighbours(n)
    return jnp.concatenate([piece] + [send(piece, shift(k)) for k in (1, 2, 3)])


def across_relayed(base, n, *gates):
    flips, _ = neighbours(n)
    by_x, by_y = send(base, flips["x"]), send(base, flips["y"])
    by_x, by_y = lax.optimization_barrier((by_x, by_y) + gates)[:2]
    mid = base.shape[0] // 2
    return [base, by_x, by_y, send(by_x[:mid], flips["y"]), send(by_y[mid:], flips["x"])]


def across_doubling(piece, n):
    flips, _ = neighbours(n)
    for way in ("x", "y"):
        piece = jnp.concatenate([piece, send(piece, flips[way])])
    return piece


def both_cores(own, n):
    flips, _ = neighbours(n)
    return own + [send(v, flips["core"]) for v in own]


def behind(value, *others):
    return lax.optimization_barrier((value,) + others)[0]


def sum_first(chunks, n, *gates):
    flips, _ = neighbours(n)
    got = [(send(parts[1], flips["x"]), send(parts[2], flips["y"])) for parts in chunks]
    got = lax.optimization_barrier((got,) + gates)[0]
    beside = lambda values: jnp.concatenate(values, axis=2).astype(bf16)
    to_x = beside(
        [p[3].astype(f32) + got_y[:2].astype(f32) for p, (_, got_y) in zip(chunks, got)]
    )
    to_y = beside(
        [p[4].astype(f32) + got_x[:2].astype(f32) for p, (got_x, _) in zip(chunks, got)]
    )
    return got, to_x, to_y


def sum_rest(chunks, first, n, *gates):
    flips, _ = neighbours(n)
    got, to_x, to_y = first
    rest_x, rest_y = send(to_x, flips["x"]), send(to_y, flips["y"])
    got, rest_x, rest_y = lax.optimization_barrier((got, rest_x, rest_y) + gates)[:3]
    beside = lambda values: jnp.concatenate(values, axis=2)
    low = beside(
        [p[0][:2].astype(f32) + got_x[2:].astype(f32) for p, (got_x, _) in zip(chunks, got)]
    ) + rest_y.astype(f32)
    high = beside(
        [p[0][2:].astype(f32) + got_y[2:].astype(f32) for p, (_, got_y) in zip(chunks, got)]
    ) + rest_x.astype(f32)
    return [low[0]] + [v.astype(bf16) for v in (low[1], high[0], high[1])], rest_x


def share_rows(core, done, n):
    flips, _ = neighbours(n)
    rows = done.shape[0] // 2
    keep = jnp.where(core == 0, done[:rows], done[rows:])
    give = jnp.where(core == 0, done[rows:], done[:rows])
    got = send(give, flips["core"])
    return jnp.where(core == 0, keep, got), jnp.where(core == 0, got, keep)


def sum_to_owner(total, ways, n, *gates):
    flips, _ = neighbours(n)
    got = [send(value, flips[way]) for value, way in zip(total[1:], ways)]
    got = lax.optimization_barrier((got,) + gates)[0]
    return total[0] + sum(v.astype(f32) for v in got)


def sum_by_halves(total, n):
    flips, _ = neighbours(n)
    got = send(jnp.stack([total[1], total[3]]), flips["z"]).astype(f32)
    far = send((total[2].astype(f32) + got[1]).astype(bf16), flips["zz"])
    return total[0] + got[0] + far.astype(f32), far


def halves(matrix, groups):
    size = matrix.shape[1] // groups
    cut = size // 2
    return [
        jnp.concatenate(
            [matrix[:, g * size + h * cut : g * size + (h + 1) * cut] for g in range(groups)],
            axis=1,
        )
        for h in range(2)
    ]


def join(first, second, groups):
    rows, columns = first.shape
    shape = (rows, groups, 1, columns // groups)
    both = jnp.concatenate([first.reshape(shape), second.reshape(shape)], axis=2)
    return both.reshape(rows, 2 * columns)


def local(
    n,
    tokens,
    lengths,
    w_qkv,
    w_out,
    w_in,
    w_down,
    vector,
    key_qkv,
    key_out,
    key_in,
    key_down,
    key_vector,
    cotangent,
):
    width = tokens.shape[1]
    half = width // 2
    ff = w_in.shape[1]
    crops = lengths.shape[0]
    near = n == 32 and w_qkv.shape[0] == 24
    me = lax.axis_index("dp").astype(jnp.int32)
    core = me & 1
    place = jnp.stack([core, (me >> 1) & 1, (me >> 2) & 1, (me >> 3) & 3])
    info = jnp.concatenate([place, lengths.astype(jnp.int32)])

    qkv_halves = halves(w_qkv, 3)
    out_halves = halves(w_out, 1)
    in_halves = halves(w_in, 1)
    down_halves = halves(w_down, 1)
    mixed = [jnp.concatenate([out_halves[h], in_halves[h]], axis=1) for h in range(2)]
    if near:
        own_rows = w_qkv.shape[0]
        ext = jnp.pad(
            vector.reshape(own_rows, vector.shape[0] // own_rows),
            ((0, 0), (0, EXT - vector.shape[0] // own_rows)),
        )
        first = [jnp.concatenate([q, ext], axis=1) for q in qkv_halves]
        base = along_z(chip_piece(core, first[0], first[1], n), n)
        layer_down = across_doubling(chip_piece(core, down_halves[0], down_halves[1], n), n)
        p_qkv = across_relayed(base, n)
        piece = chip_piece(core, mixed[0], mixed[1], n)
        base_mixed = along_z(behind(piece, base, layer_down), n)
        layer_down = behind(layer_down, base_mixed)
        _, shift = neighbours(n)
        down_one, down_three = send(layer_down, shift(1)), send(layer_down, shift(3))
        base_late = behind(base_mixed, *p_qkv)
        p_qkv = both_cores(p_qkv, n)
        order = [base_mixed]
        vec = None
    else:
        everywhere = lambda pair: [
            lax.all_gather(jnp.stack(pair), "dp", axis=1, tiled=True)
        ]
        p_qkv, p_mixed, p_down = map(everywhere, (qkv_halves, mixed, down_halves))
        vec = lax.all_gather(vector, "dp", axis=0, tiled=True).astype(f32)
        vec = jnp.pad(vec.reshape(-1, width), ((0, 16 - vec.shape[0] // width), (0, 0)))
        order = []

    vec, qkv, probs, attended, *deltas = run_attention_forward(
        info,
        tokens,
        [w_qkv, w_out, w_in, w_down, vector.reshape(1, -1)],
        [key_qkv, key_out, key_in, key_down, key_vector.reshape(1, -1)],
        p_qkv,
        vec,
        crops,
        order,
    )
    if near:
        p_mixed = across_relayed(base_late, n, attended)
        down_one, down_three = lax.optimization_barrier((down_one, down_three, attended))[:2]
        mid = layer_down.shape[0] // 2
        p_down = [layer_down, down_one, down_three]
        p_down += [send(down_one[:mid], shift(1)), send(down_three[mid:], shift(3))]
        p_mixed[3:], p_down[3:] = lax.optimization_barrier((p_mixed[3:], p_down[3:], attended))[:2]
        p_down[:3] = [behind(v, attended) for v in p_down[:3]]
        p_down = both_cores(p_down, n)
        p_mixed = both_cores(p_mixed, n)
    output, active, du, n1, df, db, da, dr1, sums = run_feed(
        info, vec, tokens, attended, cotangent, p_mixed, p_down, 512, 256, ()
    )
    down_pairs = [(df, active, ff // 2, width)]
    mixed_pairs = [(n1, du, ff // 2, width), (attended, db, half, half)]
    if near:
        flips, _ = neighbours(n)

        def mine(pairs, columns, base, after):
            return run_weight_gradient(
                info,
                pairs,
                columns,
                width,
                lambda info: info[0],
                (got_ff, base),
                False,
                after,
                RELAYED,
            )

        away_ff = run_weight_gradient(
            info,
            down_pairs + mixed_pairs,
            half + ff,
            width,
            lambda info: 1 - info[0],
            None,
            False,
            (),
        )[0]
        got_ff = send(away_ff, flips["core"])
        dqkv_other, sums_other, (away_qkv,) = run_attention_weight(
            info, qkv, da, probs, tokens, crops, 0, None, (away_ff,)
        )
        got_qkv = send(away_qkv, flips["core"])
        parts_down = mine(down_pairs, ff // 2, 0, (sums_other,))
        parts_mixed = mine(mixed_pairs, half + ff // 2, ff // 2 // width, (parts_down[0],))
        first_down = sum_first([parts_down], n, parts_mixed[0])
        dqkv_mine, sums_mine, parts_qkv = run_attention_weight(
            info,
            qkv,
            da,
            probs,
            tokens,
            crops,
            1,
            (got_qkv, sums, sums_other),
            (parts_mixed[0],) + first_down[1:],
        )
        first_mixed = sum_first([parts_mixed], n, sums_mine)
        total_down, _ = sum_rest([parts_down], first_down, n, sums_mine)
        grad_tokens = run_token_gradient(
            info,
            [dqkv_other, dqkv_mine],
            dr1,
            p_qkv,
            256,
            first_mixed[1:] + (total_down[1],),
        )
        first_qkv = sum_first([parts_qkv], n, grad_tokens)
        total_mixed, _ = sum_rest([parts_mixed], first_mixed, n, grad_tokens)
        total_qkv, _ = sum_rest([parts_qkv], first_qkv, n)
        done_down, _ = sum_by_halves(total_down, n)
        done_mixed, last = sum_by_halves(total_mixed, n)
        done_qkv = sum_to_owner(total_qkv, ("z", "zz", "zzz"), n, last)
        g_down = share_rows(core, done_down, n)
        g_mixed = share_rows(core, done_mixed, n)
        g_in = [v[:, : ff // 2] for v in g_mixed]
        g_out = [v[:, ff // 2 :] for v in g_mixed]
        g_qkv = share_rows(core, done_qkv, n)
        per = vector.shape[0] // w_qkv.shape[0]
        grad_down = join(g_down[0], g_down[1], 1)
        grad_vector = (g_qkv[0] + g_qkv[1])[:, 3 * half : 3 * half + per].reshape(-1)
        g_qkv = [v[:, : 3 * half] for v in g_qkv]
    else:

        def gradient(pairs_of, columns, block):
            return [
                run_weight_gradient(
                    info, pairs_of(h), columns, block, lambda info, h=h: h, None, True, ()
                )[0]
                for h in range(2)
            ]

        info_of = lambda h: info.at[0].set(h)
        results = [
            run_attention_backward(info_of(h), qkv, da, probs, crops, 1, ()) for h in range(2)
        ]
        dqkv_by = [r[0] for r in results]
        bias_sums = jnp.stack([jnp.sum(r[1], axis=0) for r in results]).reshape(2, 3, half)
        sums = jnp.sum(sums, axis=1)
        vec_grad = jnp.concatenate(
            [bias_sums[:, 0].reshape(-1), bias_sums[:, 2].reshape(-1)]
            + [sums[i] for i in (2, 0, 1, 3, 4, 5, 6, 7, 8, 9)]
        )
        g_down = gradient(lambda h: down_pairs, ff // 2, width)
        g_mixed = gradient(lambda h: mixed_pairs, half + ff // 2, width)
        g_in = [v[:, : ff // 2] for v in g_mixed]
        g_out = [v[:, ff // 2 :] for v in g_mixed]
        grad_down = join(g_down[0], g_down[1], 1)
        g_qkv = gradient(lambda h: [(tokens, dqkv_by[h], 3 * half, half)], 3 * half, half)
        grad_vector = lax.psum_scatter(vec_grad, "dp", scatter_dimension=0, tiled=True)
        grad_tokens = run_token_gradient(info_of(1), dqkv_by, dr1, p_qkv, 256, ())
    grad_qkv = join(g_qkv[0], g_qkv[1], 3)
    grad_out = join(g_out[0], g_out[1], 1)
    grad_in = join(g_in[0], g_in[1], 1)
    if not near:
        grad_qkv, grad_out, grad_in, grad_down = (
            lax.psum_scatter(g, "dp", scatter_dimension=0, tiled=True)
            for g in (grad_qkv, grad_out, grad_in, grad_down)
        )
    return (
        output,
        grad_tokens,
        grad_qkv,
        grad_out,
        grad_in,
        grad_down,
        grad_vector,
        *deltas[:4],
        deltas[4].reshape(-1),
    )


def solution(mesh):
    n = mesh.shape["dp"]
    rows, flat = P("dp", None), P("dp")
    return jax.shard_map(
        functools.partial(local, n),
        mesh=mesh,
        in_specs=(rows, flat, rows, rows, rows, rows, flat, rows, rows, rows, rows, flat, rows),
        out_specs=(rows, rows, rows, rows, rows, rows, flat, rows, rows, rows, rows, flat),
        check_vma=False,
    )
```

```python
import functools

import jax
import jax.numpy as jnp
import numpy as np
from jax import lax
from jax.experimental import pallas as pl
from jax.experimental.pallas import tpu as pltpu
from jax.sharding import PartitionSpec as P

H = 12
EPS = 1e-12
EXT = 128
bf16 = jnp.bfloat16
f32 = jnp.float32
VMEM_LIMIT = 60 * 1024 * 1024
COST = 0.001
ANY = pl.BlockSpec(memory_space=pl.ANY)

NT = (((1,), (1,)), ((), ()))
TN = (((0,), (0,)), ((), ()))


def mm(a, b):
    return jnp.dot(a, b, preferred_element_type=f32)


def mm_nt(a, b):
    return lax.dot_general(a, b, NT, preferred_element_type=f32)


def mm_tn(a, b):
    return lax.dot_general(a, b, TN, preferred_element_type=f32)


def row_mean(v):
    return jnp.mean(v, axis=-1, keepdims=True)


def fold_rows(v):
    return jnp.sum(v.reshape(v.shape[0] // 8, 8, v.shape[1]), axis=0)


def chip_row(info, a, k, flip):
    x, y, z = info[1], info[2], info[3]
    xx = x ^ (a & 1)
    yy = y ^ (a >> 1)
    zz = z ^ k if flip else (z - k + 4) & 3
    return pl.multiple_of(((zz * 2 + yy) * 2 + xx) * 48, 16)


LAYER_LAST = tuple([(a, k) for k in range(4)] for a in range(3)) + (
    [(3, 0), (3, 1)],
    [(3, 2), (3, 3)],
)
Z_LAST = tuple([(a, k) for a in range(4)] for k in (0, 1, 3)) + (
    [(0, 2), (1, 2)],
    [(2, 2), (3, 2)],
)


def weight_copies(info, refs, w, sems, places=LAYER_LAST):
    if len(refs) == 1:
        return [pltpu.make_async_copy(refs[0], w, sems.at[0])]
    out = []
    for source in range(2):
        half = info[0] if source == 0 else 1 - info[0]
        for number, slots in enumerate(places):
            ref = refs[source * len(places) + number]
            for j, (a, k) in enumerate(slots):
                row = chip_row(info, a, k, False)
                out.append(
                    pltpu.make_async_copy(
                        ref.at[pl.ds(48 * j, 48)],
                        w.at[half, pl.ds(row, 48)],
                        sems.at[len(out)],
                    )
                )
    return out


def sem_count(pieces):
    return 1 if len(pieces) == 1 else 32


def attention_forward(n_src, has_ext, pairs, info, x_ref, *refs):
    weights, copies_in, deltas = refs[:4], refs[4:8], refs[-7:-3]
    refs = refs[8:-7] + refs[-3:]
    src = refs[:n_src]
    if has_ext:
        spread_ref, pick_ref = refs[n_src : n_src + 2]
        refs = refs[n_src + 2 :]
    else:
        vec_in = refs[n_src]
        refs = refs[n_src + 1 :]
    vec_ref, qkv_ref, p_ref, a_ref, w, bias, sems = refs
    crop = pl.program_id(0)
    half_width = pairs * 128

    @pl.when(crop == 0)
    def _():
        copies = weight_copies(info, src, w, sems)
        for copy in copies:
            copy.start()
        for copy in copies:
            copy.wait()
        if has_ext:
            spread = mm(w[0, :, 3 * half_width :], spread_ref[...])
            groups = spread.shape[0] // 64
            picked = spread.reshape(groups, 64, spread.shape[1]) * pick_ref[...][None]
            vec_ref[0:groups, :] = jnp.sum(picked, axis=1)
        else:
            vec_ref[...] = vec_in[...]
        for h in range(2):
            for part, row in ((0, 0), (2, 1)):
                bias[h, :, part * half_width : (part + 1) * half_width] = vec_ref[
                    row : row + 1, h * half_width : (h + 1) * half_width
                ]
            bias[h, :, half_width : 2 * half_width] = jnp.zeros((1, half_width), f32)

    @pl.when(crop == 1)
    def _():
        for weight, old, out in zip(weights, copies_in, deltas):
            out[...] = (weight[...].astype(f32) - old[...]) * 0.0005

    x = x_ref[...]
    slots = x.shape[0]
    length = info[4 + crop]
    usable = lax.broadcasted_iota(jnp.int32, (1, slots), 1) < length
    mask_row = jnp.where(usable, 0.0, -1e30).astype(f32)
    lane = lax.broadcasted_iota(jnp.int32, (1, 128), 1)
    sides = (
        jnp.where(lane < 64, 1.0, 0.0).astype(bf16),
        jnp.where(lane < 64, 0.0, 1.0).astype(bf16),
    )
    units = [(h, p, side) for h in range(2) for p in range(pairs) for side in range(2)]

    def project(h):
        qkv_ref[h] = (mm(x, w[h, :, : 3 * half_width]) + bias[h]).astype(bf16)

    def columns(h, part, p):
        lo = part * half_width + p * 128
        return qkv_ref[h, :, lo : lo + 128]

    scores, probs, first = {}, {}, None
    project(0)
    for t in range(len(units) + 4):
        if t == 3:
            project(1)
        if t < len(units):
            h, p, side = units[t]
            q2 = columns(h, 0, p) * jnp.asarray(0.125, bf16)
            scores[t] = mm_nt(q2, columns(h, 1, p) * sides[side]) + mask_row
        if 0 <= t - 3 < len(units):
            h, p, side = units[t - 3]
            value = scores.pop(t - 3)
            terms = jnp.exp(value - jnp.max(value, axis=1, keepdims=True))
            mass = jnp.sum(terms, axis=1, keepdims=True)
            rounded = (terms * (1.0 / mass)).astype(bf16)
            p_ref[h, 0, p * 2 + side] = rounded
            probs[t - 3] = rounded
        if 0 <= t - 4 < len(units):
            h, p, side = units[t - 4]
            part = mm(probs.pop(t - 4), columns(h, 2, p) * sides[side])
            if side == 0:
                first = part
            else:
                lo = h * half_width + p * 128
                a_ref[:, lo : lo + 128] = (first + part).astype(bf16)


def attention_backward(pairs, info, qkv_ref, da_ref, p_ref, out_ref, sums_ref, keep=None):
    half_width = pairs * 128
    lane = lax.broadcasted_iota(jnp.int32, (1, 128), 1)
    sides = (
        jnp.where(lane < 64, 1.0, 0.0).astype(bf16),
        jnp.where(lane < 64, 0.0, 1.0).astype(bf16),
    )

    @pl.when(pl.program_id(0) == 0)
    def _():
        sums_ref[...] = jnp.zeros_like(sums_ref)

    units = [(p, side) for p in range(pairs) for side in range(2)]

    def columns(part, p):
        lo = part * half_width + p * 128
        return qkv_ref[0, :, lo : lo + 128]

    d_probs, d_scores, total = {}, {}, None
    for t in range(len(units) + 4):
        if t < len(units):
            p, side = units[t]
            da2 = da_ref[:, p * 128 : (p + 1) * 128]
            d_probs[t] = mm_nt(da2, columns(2, p) * sides[side])
        if 0 <= t - 2 < len(units):
            p, side = units[t - 2]
            probs = p_ref[0, 0, p * 2 + side].astype(f32)
            value = d_probs.pop(t - 2)
            inner = jnp.sum(probs * value, axis=1, keepdims=True)
            d_scores[t - 2] = (probs * (value - inner)).astype(bf16)
        if 0 <= t - 4 < len(units):
            p, side = units[t - 4]
            value = d_scores.pop(t - 4)
            da2 = da_ref[:, p * 128 : (p + 1) * 128]
            parts = [
                mm(value, columns(1, p) * sides[side]) * 0.125,
                mm_tn(value, columns(0, p) * sides[side]) * 0.125,
                mm_tn(p_ref[0, 0, p * 2 + side], da2 * sides[side]),
            ]
            total = parts if side == 0 else [a + b for a, b in zip(total, parts)]
            if side == 1:
                for part in range(3):
                    lo = part * half_width + p * 128
                    rounded = total[part].astype(bf16)
                    out_ref[0, :, lo : lo + 128] = rounded
                    if keep is not None:
                        rows = pl.ds(pl.program_id(0) * rounded.shape[0], rounded.shape[0])
                        keep[part, rows, p * 128 : (p + 1) * 128] = rounded
                    if part != 1:
                        sums_ref[:, lo : lo + 128] += fold_rows(rounded.astype(f32))


def gelu_parts(u):
    size = jnp.abs(u)
    t = 1.0 / (1.0 + size * (0.3275911 * 0.7071067811865476))
    bell = jnp.exp(u * u * -0.5)
    poly = t * (
        0.127414796
        + t * (-0.142248368 + t * (0.7107068705 + t * (-0.7265760135 + t * 0.5307027145)))
    )
    tail = poly * bell
    cdf = jnp.where(u < 0.0, tail, 1.0 - tail)
    return u * cdf, cdf + u * (bell * 0.3989422804014327)


def feed_stages(cut, vec_ref, ins, outs, sums_ref, slope, wa, wb):
    x_ref, a_ref, cot_ref = ins
    out_ref, g_ref, du_ref, n1_ref, df_ref, db_ref, da_ref, dr1_ref = outs
    width = x_ref.shape[1]
    half = width // 2
    place = lambda j: (j // 2, (j % 2) * width)

    attended = a_ref[cut, :]
    branch = jnp.concatenate(
        [mm(attended, wa[h, :, :half]) for h in range(2)], axis=1
    ) + vec_ref[2:3, :]
    yield
    resid = x_ref[cut, :].astype(f32) + branch
    center = resid - row_mean(resid)
    rstd = lax.rsqrt(row_mean(center * center) + EPS)
    z1 = center * rstd
    n1 = z1 * (1.0 + vec_ref[3:4, :]) + vec_ref[4:5, :]
    n1b = n1.astype(bf16)
    n1_ref[cut, :] = n1b
    yield

    def up(j):
        h, lo = place(j)
        return mm(n1b, wa[h, :, half + lo : half + lo + width]) + vec_ref[8 + j : 9 + j, :]

    hidden = [up(0)]
    yield
    feed = None
    for j in range(4):
        if j < 3:
            hidden.append(up(j + 1))
            yield
        active, tilt = gelu_parts(hidden[j])
        hidden[j] = None
        active = active.astype(bf16)
        at = slice(j * width, (j + 1) * width)
        g_ref[cut, at] = active
        slope[cut, at] = tilt
        yield
        h, lo = place(j)
        part = mm_nt(active, wb[h, :, lo : lo + width])
        feed = part if feed is None else feed + part
        yield
    resid2 = n1 + feed + vec_ref[7:8, :]
    center2 = resid2 - row_mean(resid2)
    rstd2 = lax.rsqrt(row_mean(center2 * center2) + EPS)
    z2 = center2 * rstd2
    gain2 = 1.0 + vec_ref[5:6, :]
    out_ref[cut, :] = (z2 * gain2 + vec_ref[6:7, :]).astype(bf16)
    dy = cot_ref[cut, :].astype(f32)
    s = dy * gain2
    dr2 = rstd2 * (s - row_mean(s) - z2 * row_mean(s * z2))
    df = dr2.astype(bf16)
    df_ref[cut, :] = df
    sums_ref[3] += fold_rows(dy * z2)
    sums_ref[4] += fold_rows(dy)
    sums_ref[5] += fold_rows(df.astype(f32))
    yield

    def back(j):
        h, lo = place(j)
        return mm(df, wb[h, :, lo : lo + width])

    d_active = [back(0)]
    yield
    dn1 = dr2
    for j in range(4):
        if j < 3:
            d_active.append(back(j + 1))
            yield
        at = slice(j * width, (j + 1) * width)
        du = (d_active[j] * slope[cut, at]).astype(bf16)
        d_active[j] = None
        du_ref[cut, at] = du
        sums_ref[6 + j] += fold_rows(du.astype(f32))
        yield
        h, lo = place(j)
        dn1 = dn1 + mm_nt(du, wa[h, :, half + lo : half + lo + width])
        yield
    sums_ref[0] += fold_rows(dn1 * z1)
    sums_ref[1] += fold_rows(dn1)
    s = dn1 * (1.0 + vec_ref[3:4, :])
    dr1 = rstd * (s - row_mean(s) - z1 * row_mean(s * z1))
    dr1_ref[cut, :] = dr1
    db = dr1.astype(bf16)
    db_ref[cut, :] = db
    sums_ref[2] += fold_rows(db.astype(f32))
    yield
    da = mm_nt(db[:, :half], wa[0, :, :half]) + mm_nt(db[:, half:], wa[1, :, :half])
    da_ref[cut, :] = da.astype(bf16)
    yield


def feed_both(n_a, n_b, sub, info, vec_ref, x_ref, a_ref, cot_ref, *refs):
    src_a = refs[:n_a]
    src_b = refs[n_a : n_a + n_b]
    refs = refs[n_a + n_b :]
    outs = refs[:8]
    sums_ref, slope, wa, wb, sems_a, sems_b = refs[8:]
    step = pl.program_id(0)
    copies_a = weight_copies(info, src_a, wa, sems_a)
    copies_b = weight_copies(info, src_b, wb, sems_b, Z_LAST)

    @pl.when(step == 0)
    def _():
        for copy in copies_a + copies_b:
            copy.start()
        sums_ref[...] = jnp.zeros_like(sums_ref)
        for copy in copies_a + copies_b:
            copy.wait()

    ins = (x_ref, a_ref, cot_ref)
    blocks = [
        feed_stages(slice(r, r + sub), vec_ref, ins, outs, sums_ref, slope, wa, wb)
        for r in range(0, x_ref.shape[0], sub)
    ]
    waiting, t = list(range(len(blocks))), 0
    while waiting:
        for i in list(waiting):
            if t >= i and next(blocks[i], True):
                waiting.remove(i)
        t += 1


def token_gradient(n_src, info, other_ref, mine_ref, dr1_ref, *refs):
    src = refs[:n_src]
    out_ref, w, sems = refs[n_src:]
    used = mine_ref.shape[2]

    @pl.when(pl.program_id(0) == 0)
    def _():
        copies = weight_copies(info, src, w, sems)
        for copy in copies:
            copy.start()
        for copy in copies:
            copy.wait()

    out_ref[...] = (
        dr1_ref[...]
        + mm_nt(other_ref[0], w[1 - info[0], :, :used])
        + mm_nt(mine_ref[0], w[info[0], :, :used])
    )


def vector_rows(info, sums_ref, other_ref, mine_ref):
    total = lambda v: jnp.sum(v, axis=0, keepdims=True)
    half = other_ref.shape[1] // 3
    rows = []
    for part in (0, 2):
        cut = slice(part * half, (part + 1) * half)
        other, mine = total(other_ref[:, cut]), total(mine_ref[:, cut])
        first = jnp.where(info[0] == 0, mine, other)
        second = jnp.where(info[0] == 0, other, mine)
        rows.append(jnp.concatenate([first, second], axis=1))
    return rows + [total(sums_ref[i]) for i in (2, 0, 1, 3, 4, 5, 6, 7, 8, 9)]


RELAYED = (
    [(0, k) for k in range(4)],
    [(3, 0), (3, 1), (1, 0), (1, 1)],
    [(3, 2), (3, 3), (2, 2), (2, 3)],
    [(1, 2), (1, 3)],
    [(2, 0), (2, 1)],
)


def store_parts(info, value, outs, acc, recv, buffers):
    size = value.shape[1]
    if buffers is None:
        outs[0][:, :size] = value.astype(outs[0].dtype)
        return
    acc[:, :size] = value
    for out, slots in zip(outs, buffers):
        for j, (a, k) in enumerate(slots):
            row = chip_row(info, a, k, True)
            mine = acc[pl.ds(row, 48), :size]
            if recv is not None:
                mine = mine + recv[pl.ds(row, 48), :size].astype(f32)
            out[j, :, :size] = mine.astype(bf16)


def attention_weight(pairs, crops, buffers, info, qkv_ref, da_ref, p_ref, x_ref, *refs):
    if buffers is not None:
        recv, all_sums_ref, other_ref, spread_ref, pick_ref, *refs = refs
    out_ref, sums_ref, *outs, keep, acc, left, sem = refs
    step = pl.program_id(0)
    tokens_copy = pltpu.make_async_copy(x_ref, left, sem)

    @pl.when(step == 0)
    def _():
        tokens_copy.start()

    @pl.when(step == crops)
    def _():
        tokens_copy.wait()

    @pl.when(step < crops)
    def _():
        attention_backward(pairs, info, qkv_ref, da_ref, p_ref, out_ref, sums_ref, keep)

    @pl.when((step >= crops) & (step < crops + 3))
    def _():
        value = mm_tn(left[...], keep[jnp.clip(step - crops, 0, 2)])
        store_parts(info, value, outs, acc, None if buffers is None else recv, buffers)

    if buffers is not None:

        @pl.when(step == crops + 3)
        def _():
            rows = vector_rows(info, all_sums_ref, other_ref, sums_ref)
            picked = jnp.concatenate([(r * pick_ref[...]).astype(bf16) for r in rows], axis=0)
            store_parts(info, mm_nt(picked, spread_ref[...]), outs, acc, None, buffers)


def weight_gradient(starts, sizes, has_recv, buffers, info, *refs):
    count = len(starts)
    lhs = refs[:count]
    rhs = refs[count : 2 * count]
    at = 2 * count
    recv = None
    if has_recv:
        recv = refs[at]
        at += 1
    (*outs, acc, left, sems) = refs[at:]
    step = pl.program_id(0)
    if recv is None:
        copies = [
            pltpu.make_async_copy(lhs[number], left.at[number], sems.at[number])
            for number in range(count)
        ]

        @pl.when(step == 0)
        def _():
            for copy in copies:
                copy.start()

        for number, start in enumerate(starts):

            @pl.when(step == start)
            def _(number=number):
                copies[number].wait()

    for number, start in enumerate(starts):
        here = step >= start
        if number + 1 < count:
            here = here & (step < starts[number + 1])

        @pl.when(here)
        def _(number=number):
            right = rhs[number]
            right = right[0] if len(right.shape) == 3 else right[...]
            value = mm_tn(left[number] if recv is None else lhs[number][...], right)
            store_parts(info, value, outs, acc, recv, buffers)


def params():
    return pltpu.CompilerParams(
        dimension_semantics=("arbitrary",), vmem_limit_bytes=VMEM_LIMIT
    )


def call(kernel, grid, in_specs, out_specs, out_shape, scratch, flops, nbytes, name, after=()):
    def body(info, *refs):
        kernel(info, *refs[len(after) :])

    run = pl.pallas_call(
        body,
        grid_spec=pltpu.PrefetchScalarGridSpec(
            num_scalar_prefetch=1,
            grid=grid,
            in_specs=[ANY] * len(after) + in_specs,
            out_specs=out_specs,
            scratch_shapes=scratch,
        ),
        out_shape=out_shape,
        compiler_params=params(),
        cost_estimate=pl.CostEstimate(
            flops=int(flops * COST), bytes_accessed=int(nbytes * COST), transcendentals=0
        ),
        name=name,
    )
    return lambda info, *operands: run(info, *after, *operands)


def struct(shape, dtype):
    return jax.ShapeDtypeStruct(shape, dtype)


def whole_block(shape):
    return pl.BlockSpec(shape, lambda i, info: (0,) * len(shape))


def rows_block(rows, columns):
    return pl.BlockSpec((rows, columns), lambda i, info: (i, 0))


def spread_tables(width):
    per = width // 64
    e = np.arange(width)
    spread = (np.arange(EXT)[:, None] == (e % per)[None, :]).astype(np.float32)
    pick = (np.arange(64)[:, None] == (e // per)[None, :]).astype(np.float32)
    return spread, pick


def run_attention_forward(info, x, weights, copies, pieces, vec, crops, after):
    rows, width = x.shape
    slots = rows // crops
    half = width // 2
    w_columns = pieces[0].shape[-1]
    has_ext = vec is None
    pairs = half // 128
    if has_ext:
        spread, pick = spread_tables(width)
        extra = [jnp.asarray(spread, bf16), jnp.asarray(pick, f32)]
    else:
        extra = [vec]
    extra_specs = [whole_block(e.shape) for e in extra]
    kernel = functools.partial(attention_forward, len(pieces), has_ext, pairs)
    return call(
        kernel,
        (crops,),
        [rows_block(slots, width)]
        + [whole_block(w.shape) for w in weights + copies]
        + [ANY] * len(pieces)
        + extra_specs,
        [
            whole_block((16, width)),
            pl.BlockSpec((2, slots, 3 * half), lambda i, info: (0, i, 0)),
            pl.BlockSpec((2, 1, H // 2, slots, slots), lambda i, info: (0, i, 0, 0, 0)),
            rows_block(slots, width),
        ]
        + [whole_block(w.shape) for w in weights],
        [
            struct((16, width), f32),
            struct((2, rows, 3 * half), bf16),
            struct((2, crops, H // 2, slots, slots), bf16),
            struct((rows, width), bf16),
        ]
        + [struct(w.shape, f32) for w in weights],
        [
            pltpu.VMEM((2, width, w_columns), bf16),
            pltpu.VMEM((2, 1, 3 * half), f32),
            pltpu.SemaphoreType.DMA((sem_count(pieces),)),
        ],
        2 * rows * width * 3 * width + 8 * rows * slots * width,
        30e6,
        "attention_forward",
        after,
    )(info, x, *weights, *copies, *pieces, *extra)


def run_attention_backward(info, qkv, da, probs, crops, which, after):
    _, rows, columns = qkv.shape
    slots = rows // crops
    half = columns // 3

    def pick(info):
        return info[0] if which else 1 - info[0]

    kernel = functools.partial(attention_backward, half // 128)
    return call(
        kernel,
        (crops,),
        [
            pl.BlockSpec((1, slots, columns), lambda i, info: (pick(info), i, 0)),
            pl.BlockSpec((slots, half), lambda i, info: (i, pick(info))),
            pl.BlockSpec(
                (1, 1, H // 2, slots, slots), lambda i, info: (pick(info), i, 0, 0, 0)
            ),
        ],
        [
            pl.BlockSpec((1, slots, columns), lambda i, info: (0, i, 0)),
            whole_block((8, columns)),
        ],
        [struct((1, rows, columns), bf16), struct((8, columns), f32)],
        [],
        16 * rows * slots * half,
        12e6,
        "attention_backward",
        after,
    )(info, qkv, da, probs)


def run_attention_weight(info, qkv, da, probs, x, crops, which, more, after):
    _, rows, columns = qkv.shape
    width = x.shape[1]
    slots = rows // crops
    half = columns // 3
    pick = lambda info: info[0] if which else 1 - info[0]
    crop = lambda i: jnp.minimum(i, crops - 1)
    part = lambda i, last: jnp.clip(i - crops, 0, last)
    in_specs = [
        pl.BlockSpec((1, slots, columns), lambda i, info: (pick(info), crop(i), 0)),
        pl.BlockSpec((slots, half), lambda i, info: (crop(i), pick(info))),
        pl.BlockSpec(
            (1, 1, H // 2, slots, slots), lambda i, info: (pick(info), crop(i), 0, 0, 0)
        ),
        ANY,
    ]
    operands = [qkv, da, probs, x]
    out_specs = [
        pl.BlockSpec((1, slots, columns), lambda i, info: (0, crop(i), 0)),
        whole_block((8, columns)),
    ]
    out_shape = [struct((1, rows, columns), bf16), struct((8, columns), f32)]
    if which:
        recv, sums, other = more
        spread, pick_rows = spread_tables(width)
        rest = [sums, other, jnp.asarray(spread, bf16), jnp.asarray(pick_rows, f32)]
        operands += [recv] + rest
        in_specs.append(pl.BlockSpec((width, half), lambda i, info: (0, part(i, 2))))
        in_specs += [whole_block(v.shape) for v in rest]
        out_specs += [
            pl.BlockSpec((len(b), 48, half), lambda i, info: (0, 0, part(i, 3))) for b in RELAYED
        ]
        out_shape += [struct((len(b), 48, columns + EXT), bf16) for b in RELAYED]
    else:
        out_specs.append(pl.BlockSpec((width, half), lambda i, info: (0, part(i, 2))))
        out_shape.append(struct((width, columns), bf16))
    kernel = functools.partial(attention_weight, half // 128, crops, RELAYED if which else None)
    out = call(
        kernel,
        (crops + 3 + which,),
        in_specs,
        out_specs,
        out_shape,
        [
            pltpu.VMEM((3, rows, half), bf16),
            pltpu.VMEM((width, half), f32),
            pltpu.VMEM((rows, width), bf16),
            pltpu.SemaphoreType.DMA,
        ],
        16 * rows * slots * half + 2 * rows * width * columns,
        20e6,
        "attention_weight",
        after,
    )(info, *operands)
    return out[0], out[1], out[2:]


def run_feed(info, vec, x, attended, cot, pieces_a, pieces_b, block, sub, after):
    rows, width = x.shape
    ff = 2 * pieces_b[0].shape[-1]
    kernel = functools.partial(feed_both, len(pieces_a), len(pieces_b), sub)
    narrow, wide = rows_block(block, width), rows_block(block, ff)
    return call(
        kernel,
        (rows // block,),
        [whole_block(vec.shape)] + [narrow] * 3 + [ANY] * (len(pieces_a) + len(pieces_b)),
        [narrow, wide, wide] + [narrow] * 5 + [whole_block((10, 8, width))],
        [struct((rows, width), bf16), struct((rows, ff), bf16), struct((rows, ff), bf16)]
        + [struct((rows, width), bf16)] * 4
        + [struct((rows, width), f32), struct((10, 8, width), f32)],
        [
            pltpu.VMEM((block, ff), f32),
            pltpu.VMEM((2, width, pieces_a[0].shape[-1]), bf16),
            pltpu.VMEM((2, width, pieces_b[0].shape[-1]), bf16),
            pltpu.SemaphoreType.DMA((sem_count(pieces_a),)),
            pltpu.SemaphoreType.DMA((sem_count(pieces_b),)),
        ],
        4 * rows * width * (width + 2 * ff),
        53e6,
        "feed_both",
        after,
    )(info, vec, x, attended, cot, *pieces_a, *pieces_b)


def run_token_gradient(info, dqkv_by, dr1, pieces, block, after):
    rows, width = dr1.shape
    columns = dqkv_by[0].shape[2]
    kernel = functools.partial(token_gradient, len(pieces))
    return call(
        kernel,
        (rows // block,),
        [
            pl.BlockSpec((1, block, columns), lambda i, info: (0, i, 0)),
            pl.BlockSpec((1, block, columns), lambda i, info: (0, i, 0)),
            rows_block(block, width),
        ]
        + [ANY] * len(pieces),
        rows_block(block, width),
        struct((rows, width), f32),
        [
            pltpu.VMEM((2, width, pieces[0].shape[-1]), bf16),
            pltpu.SemaphoreType.DMA((sem_count(pieces),)),
        ],
        4 * rows * width * columns,
        20e6,
        "token_gradient",
        after,
    )(info, *dqkv_by, dr1, *pieces)


def run_weight_gradient(info, pairs, columns, block, pick, recv, full, after, buffers=None):
    rows, width = pairs[0][0].shape
    once = pl.Buffered(1)
    starts, sizes, step = [], [], 0
    rhs_specs = []
    for _, rhs, total, size in pairs:
        count = total // size
        starts.append(step)
        sizes.append(size)
        near = lambda i, step=step, count=count: jnp.clip(i - step, 0, count - 1)
        if rhs.ndim == 3:
            rhs_specs.append(
                pl.BlockSpec((1, rows, size), lambda i, info, near=near: (0, 0, near(i)))
            )
        else:
            rhs_specs.append(
                pl.BlockSpec(
                    (rows, size),
                    lambda i, info, near=near, count=count: (0, pick(info) * count + near(i)),
                )
            )
        step += count
    operands = [p[0] for p in pairs] + [p[1] for p in pairs]
    left = pl.BlockSpec((rows, width), lambda i, info: (0, 0), pipeline_mode=once)
    specs = [ANY if recv is None else left for _ in pairs] + rhs_specs
    if recv is not None:
        recv, base = recv
        operands.append(recv)
        last = step - 1
        specs.append(
            pl.BlockSpec((width, block), lambda i, info: (0, base + jnp.minimum(i, last)))
        )
    if recv is None:
        out_specs = [pl.BlockSpec((width, block), lambda i, info: (0, i))]
        out_shape = [struct((width, columns), f32 if full else bf16)]
    else:
        out_specs = [
            pl.BlockSpec((len(b), 48, block), lambda i, info: (0, 0, i)) for b in buffers
        ]
        out_shape = [struct((len(b), 48, columns), bf16) for b in buffers]
    kernel = functools.partial(
        weight_gradient, tuple(starts), tuple(sizes), recv is not None, buffers
    )
    return call(
        kernel,
        (step,),
        specs,
        out_specs,
        out_shape,
        [
            pltpu.VMEM((width, block), f32),
            pltpu.VMEM((len(pairs), rows, width) if recv is None else (1, 16, width), bf16),
            pltpu.SemaphoreType.DMA((len(pairs),)),
        ],
        2 * rows * width * columns,
        12e6,
        "weight_gradient",
        after,
    )(info, *operands)


def neighbours(n):
    flip = lambda bits: [(i, i ^ bits) for i in range(n)]
    shift = lambda k: [(i, (i + 8 * k) % n) for i in range(n)]
    ways = {"core": 1, "x": 2, "y": 4, "xy": 6, "z": 8, "zz": 16, "zzz": 24}
    return {way: flip(bits) for way, bits in ways.items()}, shift


def send(value, pairs):
    return lax.ppermute(value, "dp", pairs)


def chip_piece(core, first, second, n):
    flips, _ = neighbours(n)
    keep = jnp.where(core == 0, first, second)
    give = jnp.where(core == 0, second, first)
    got = send(give, flips["core"])
    return jnp.where(core == 0, jnp.concatenate([keep, got]), jnp.concatenate([got, keep]))


def along_z(piece, n):
    _, shift = neighbours(n)
    return jnp.concatenate([piece] + [send(piece, shift(k)) for k in (1, 2, 3)])


def across_relayed(base, n, *gates):
    flips, _ = neighbours(n)
    by_x, by_y = send(base, flips["x"]), send(base, flips["y"])
    by_x, by_y = lax.optimization_barrier((by_x, by_y) + gates)[:2]
    mid = base.shape[0] // 2
    return [base, by_x, by_y, send(by_x[:mid], flips["y"]), send(by_y[mid:], flips["x"])]


def across_doubling(piece, n):
    flips, _ = neighbours(n)
    for way in ("x", "y"):
        piece = jnp.concatenate([piece, send(piece, flips[way])])
    return piece


def both_cores(own, n):
    flips, _ = neighbours(n)
    return own + [send(v, flips["core"]) for v in own]


def behind(value, *others):
    return lax.optimization_barrier((value,) + others)[0]


def sum_first(chunks, n, *gates):
    flips, _ = neighbours(n)
    got = [(send(parts[1], flips["x"]), send(parts[2], flips["y"])) for parts in chunks]
    got = lax.optimization_barrier((got,) + gates)[0]
    beside = lambda values: jnp.concatenate(values, axis=2).astype(bf16)
    to_x = beside(
        [p[3].astype(f32) + got_y[:2].astype(f32) for p, (_, got_y) in zip(chunks, got)]
    )
    to_y = beside(
        [p[4].astype(f32) + got_x[:2].astype(f32) for p, (got_x, _) in zip(chunks, got)]
    )
    return got, to_x, to_y


def sum_rest(chunks, first, n, *gates):
    flips, _ = neighbours(n)
    got, to_x, to_y = first
    rest_x, rest_y = send(to_x, flips["x"]), send(to_y, flips["y"])
    got, rest_x, rest_y = lax.optimization_barrier((got, rest_x, rest_y) + gates)[:3]
    beside = lambda values: jnp.concatenate(values, axis=2)
    low = beside(
        [p[0][:2].astype(f32) + got_x[2:].astype(f32) for p, (got_x, _) in zip(chunks, got)]
    ) + rest_y.astype(f32)
    high = beside(
        [p[0][2:].astype(f32) + got_y[2:].astype(f32) for p, (_, got_y) in zip(chunks, got)]
    ) + rest_x.astype(f32)
    return [low[0]] + [v.astype(bf16) for v in (low[1], high[0], high[1])], rest_x


def share_rows(core, done, n):
    flips, _ = neighbours(n)
    rows = done.shape[0] // 2
    keep = jnp.where(core == 0, done[:rows], done[rows:])
    give = jnp.where(core == 0, done[rows:], done[:rows])
    got = send(give, flips["core"])
    return jnp.where(core == 0, keep, got), jnp.where(core == 0, got, keep)


def sum_to_owner(total, ways, n, *gates):
    flips, _ = neighbours(n)
    got = [send(value, flips[way]) for value, way in zip(total[1:], ways)]
    got = lax.optimization_barrier((got,) + gates)[0]
    return total[0] + sum(v.astype(f32) for v in got)


def sum_by_halves(total, n):
    flips, _ = neighbours(n)
    got = send(jnp.stack([total[1], total[3]]), flips["z"]).astype(f32)
    far = send((total[2].astype(f32) + got[1]).astype(bf16), flips["zz"])
    return total[0] + got[0] + far.astype(f32), far


def halves(matrix, groups):
    size = matrix.shape[1] // groups
    cut = size // 2
    return [
        jnp.concatenate(
            [matrix[:, g * size + h * cut : g * size + (h + 1) * cut] for g in range(groups)],
            axis=1,
        )
        for h in range(2)
    ]


def join(first, second, groups):
    rows, columns = first.shape
    shape = (rows, groups, 1, columns // groups)
    both = jnp.concatenate([first.reshape(shape), second.reshape(shape)], axis=2)
    return both.reshape(rows, 2 * columns)


def local(
    n,
    tokens,
    lengths,
    w_qkv,
    w_out,
    w_in,
    w_down,
    vector,
    key_qkv,
    key_out,
    key_in,
    key_down,
    key_vector,
    cotangent,
):
    width = tokens.shape[1]
    half = width // 2
    ff = w_in.shape[1]
    crops = lengths.shape[0]
    near = n == 32 and w_qkv.shape[0] == 24
    me = lax.axis_index("dp").astype(jnp.int32)
    core = me & 1
    place = jnp.stack([core, (me >> 1) & 1, (me >> 2) & 1, (me >> 3) & 3])
    info = jnp.concatenate([place, lengths.astype(jnp.int32)])

    qkv_halves = halves(w_qkv, 3)
    out_halves = halves(w_out, 1)
    in_halves = halves(w_in, 1)
    down_halves = halves(w_down, 1)
    mixed = [jnp.concatenate([out_halves[h], in_halves[h]], axis=1) for h in range(2)]
    if near:
        own_rows = w_qkv.shape[0]
        ext = jnp.pad(
            vector.reshape(own_rows, vector.shape[0] // own_rows),
            ((0, 0), (0, EXT - vector.shape[0] // own_rows)),
        )
        first = [jnp.concatenate([q, ext], axis=1) for q in qkv_halves]
        base = behind(along_z(chip_piece(core, first[0], first[1], n), n), info)
        layer_down = across_doubling(chip_piece(core, down_halves[0], down_halves[1], n), n)
        p_qkv = across_relayed(base, n)
        piece = chip_piece(core, mixed[0], mixed[1], n)
        base_mixed = along_z(behind(piece, base, layer_down), n)
        layer_down = behind(layer_down, base_mixed)
        _, shift = neighbours(n)
        down_one, down_three = send(layer_down, shift(1)), send(layer_down, shift(3))
        base_late = behind(base_mixed, *p_qkv)
        p_qkv = both_cores(lax.optimization_barrier(p_qkv), n)
        order = [base_mixed]
        vec = None
    else:
        everywhere = lambda pair: [
            lax.all_gather(jnp.stack(pair), "dp", axis=1, tiled=True)
        ]
        p_qkv, p_mixed, p_down = map(everywhere, (qkv_halves, mixed, down_halves))
        vec = lax.all_gather(vector, "dp", axis=0, tiled=True).astype(f32)
        vec = jnp.pad(vec.reshape(-1, width), ((0, 16 - vec.shape[0] // width), (0, 0)))
        order = []

    vec, qkv, probs, attended, *deltas = run_attention_forward(
        info,
        tokens,
        [w_qkv, w_out, w_in, w_down],
        [key_qkv, key_out, key_in, key_down],
        p_qkv,
        vec,
        crops,
        order,
    )
    if near:
        p_mixed = across_relayed(base_late, n, attended)
        down_one, down_three = lax.optimization_barrier((down_one, down_three, attended))[:2]
        mid = layer_down.shape[0] // 2
        p_down = [layer_down, down_one, down_three]
        p_down += [send(down_one[:mid], shift(1)), send(down_three[mid:], shift(3))]
        p_mixed[3:], p_down[3:] = lax.optimization_barrier((p_mixed[3:], p_down[3:], attended))[:2]
        p_down[:3] = [behind(v, attended) for v in p_down[:3]]
        p_down = both_cores(p_down, n)
        p_mixed = both_cores(p_mixed, n)
    output, active, du, n1, df, db, da, dr1, sums = run_feed(
        info, vec, tokens, attended, cotangent, p_mixed, p_down, 512, 256, ()
    )
    down_pairs = [(df, active, ff // 2, width)]
    mixed_pairs = [(n1, du, ff // 2, width), (attended, db, half, half)]
    if near:
        flips, _ = neighbours(n)

        def mine(pairs, columns, base, after):
            return run_weight_gradient(
                info,
                pairs,
                columns,
                width,
                lambda info: info[0],
                (got_ff, base),
                False,
                after,
                RELAYED,
            )

        away_ff = run_weight_gradient(
            info,
            down_pairs + mixed_pairs,
            half + ff,
            width,
            lambda info: 1 - info[0],
            None,
            False,
            (),
        )[0]
        got_ff = send(away_ff, flips["core"])
        dqkv_other, sums_other, (away_qkv,) = run_attention_weight(
            info, qkv, da, probs, tokens, crops, 0, None, (away_ff,)
        )
        got_qkv = send(away_qkv, flips["core"])
        parts_down = mine(down_pairs, ff // 2, 0, (sums_other,))
        parts_mixed = mine(mixed_pairs, half + ff // 2, ff // 2 // width, (parts_down[0],))
        first_down = sum_first([parts_down], n, parts_mixed[0])
        dqkv_mine, sums_mine, parts_qkv = run_attention_weight(
            info,
            qkv,
            da,
            probs,
            tokens,
            crops,
            1,
            (got_qkv, sums, sums_other),
            (parts_mixed[0],) + first_down[1:],
        )
        first_mixed = sum_first([parts_mixed], n, sums_mine)
        total_down, _ = sum_rest([parts_down], first_down, n, sums_mine)
        grad_tokens = run_token_gradient(
            info,
            [dqkv_other, dqkv_mine],
            dr1,
            p_qkv,
            256,
            first_mixed[1:] + (total_down[1],),
        )
        first_qkv = sum_first([parts_qkv], n, grad_tokens)
        total_mixed, _ = sum_rest([parts_mixed], first_mixed, n, grad_tokens)
        total_qkv, _ = sum_rest([parts_qkv], first_qkv, n)
        done_down, _ = sum_by_halves(total_down, n)
        done_mixed, last = sum_by_halves(total_mixed, n)
        done_qkv = sum_to_owner(total_qkv, ("z", "zz", "zzz"), n, last)
        g_down = share_rows(core, done_down, n)
        g_mixed = share_rows(core, done_mixed, n)
        g_in = [v[:, : ff // 2] for v in g_mixed]
        g_out = [v[:, ff // 2 :] for v in g_mixed]
        g_qkv = share_rows(core, done_qkv, n)
        per = vector.shape[0] // w_qkv.shape[0]
        grad_down = join(g_down[0], g_down[1], 1)
        grad_vector = (g_qkv[0] + g_qkv[1])[:, 3 * half : 3 * half + per].reshape(-1)
        g_qkv = [v[:, : 3 * half] for v in g_qkv]
    else:

        def gradient(pairs_of, columns, block):
            return [
                run_weight_gradient(
                    info, pairs_of(h), columns, block, lambda info, h=h: h, None, True, ()
                )[0]
                for h in range(2)
            ]

        info_of = lambda h: info.at[0].set(h)
        results = [
            run_attention_backward(info_of(h), qkv, da, probs, crops, 1, ()) for h in range(2)
        ]
        dqkv_by = [r[0] for r in results]
        bias_sums = jnp.stack([jnp.sum(r[1], axis=0) for r in results]).reshape(2, 3, half)
        sums = jnp.sum(sums, axis=1)
        vec_grad = jnp.concatenate(
            [bias_sums[:, 0].reshape(-1), bias_sums[:, 2].reshape(-1)]
            + [sums[i] for i in (2, 0, 1, 3, 4, 5, 6, 7, 8, 9)]
        )
        g_down = gradient(lambda h: down_pairs, ff // 2, width)
        g_mixed = gradient(lambda h: mixed_pairs, half + ff // 2, width)
        g_in = [v[:, : ff // 2] for v in g_mixed]
        g_out = [v[:, ff // 2 :] for v in g_mixed]
        grad_down = join(g_down[0], g_down[1], 1)
        g_qkv = gradient(lambda h: [(tokens, dqkv_by[h], 3 * half, half)], 3 * half, half)
        grad_vector = lax.psum_scatter(vec_grad, "dp", scatter_dimension=0, tiled=True)
        grad_tokens = run_token_gradient(info_of(1), dqkv_by, dr1, p_qkv, 256, ())
    grad_qkv = join(g_qkv[0], g_qkv[1], 3)
    grad_out = join(g_out[0], g_out[1], 1)
    grad_in = join(g_in[0], g_in[1], 1)
    if not near:
        grad_qkv, grad_out, grad_in, grad_down = (
            lax.psum_scatter(g, "dp", scatter_dimension=0, tiled=True)
            for g in (grad_qkv, grad_out, grad_in, grad_down)
        )
    return (
        output,
        grad_tokens,
        grad_qkv,
        grad_out,
        grad_in,
        grad_down,
        grad_vector,
        *deltas,
        (vector.astype(f32) - key_vector) * 0.0005,
    )


def solution(mesh):
    n = mesh.shape["dp"]
    rows, flat = P("dp", None), P("dp")
    return jax.shard_map(
        functools.partial(local, n),
        mesh=mesh,
        in_specs=(rows, flat, rows, rows, rows, rows, flat, rows, rows, rows, rows, flat, rows),
        out_specs=(rows, rows, rows, rows, rows, rows, flat, rows, rows, rows, rows, flat),
        check_vma=False,
    )
```

```python
import functools

import jax
import jax.numpy as jnp
import numpy as np
from jax import lax
from jax.experimental import pallas as pl
from jax.experimental.pallas import tpu as pltpu
from jax.sharding import PartitionSpec as P

H = 12
EPS = 1e-12
EXT = 128
bf16 = jnp.bfloat16
f32 = jnp.float32
VMEM_LIMIT = 60 * 1024 * 1024
COST = 0.001
ANY = pl.BlockSpec(memory_space=pl.ANY)

NT = (((1,), (1,)), ((), ()))
TN = (((0,), (0,)), ((), ()))


def mm(a, b):
    return jnp.dot(a, b, preferred_element_type=f32)


def mm_nt(a, b):
    return lax.dot_general(a, b, NT, preferred_element_type=f32)


def mm_tn(a, b):
    return lax.dot_general(a, b, TN, preferred_element_type=f32)


def row_mean(v):
    return jnp.mean(v, axis=-1, keepdims=True)


def fold_rows(v):
    return jnp.sum(v.reshape(v.shape[0] // 8, 8, v.shape[1]), axis=0)


def chip_row(info, a, k, flip):
    x, y, z = info[1], info[2], info[3]
    xx = x ^ (a & 1)
    yy = y ^ (a >> 1)
    zz = z ^ k if flip else (z - k + 4) & 3
    return pl.multiple_of(((zz * 2 + yy) * 2 + xx) * 48, 16)


LAYER_LAST = tuple([(a, k) for k in range(4)] for a in range(3)) + (
    [(3, 0), (3, 1)],
    [(3, 2), (3, 3)],
)
Z_LAST = tuple([(a, k) for a in range(4)] for k in (0, 1, 3)) + (
    [(0, 2), (1, 2)],
    [(2, 2), (3, 2)],
)


def weight_copies(info, refs, w, sems, places=LAYER_LAST):
    if len(refs) == 1:
        return [pltpu.make_async_copy(refs[0], w, sems.at[0])]
    out = []
    for source in range(2):
        half = info[0] if source == 0 else 1 - info[0]
        for number, slots in enumerate(places):
            ref = refs[source * len(places) + number]
            for j, (a, k) in enumerate(slots):
                row = chip_row(info, a, k, False)
                out.append(
                    pltpu.make_async_copy(
                        ref.at[pl.ds(48 * j, 48)],
                        w.at[half, pl.ds(row, 48)],
                        sems.at[len(out)],
                    )
                )
    return out


def sem_count(pieces):
    return 1 if len(pieces) == 1 else 32


def attention_forward(n_src, has_ext, pairs, info, x_ref, *refs):
    weights, copies_in, deltas = refs[:4], refs[4:8], refs[-7:-3]
    refs = refs[8:-7] + refs[-3:]
    src = refs[:n_src]
    if has_ext:
        spread_ref, pick_ref = refs[n_src : n_src + 2]
        refs = refs[n_src + 2 :]
    else:
        vec_in = refs[n_src]
        refs = refs[n_src + 1 :]
    vec_ref, qkv_ref, p_ref, a_ref, w, bias, sems = refs
    crop = pl.program_id(0)
    half_width = pairs * 128

    @pl.when(crop == 0)
    def _():
        copies = weight_copies(info, src, w, sems)
        for copy in copies:
            copy.start()
        for copy in copies:
            copy.wait()
        if has_ext:
            spread = mm(w[0, :, 3 * half_width :], spread_ref[...])
            groups = spread.shape[0] // 64
            picked = spread.reshape(groups, 64, spread.shape[1]) * pick_ref[...][None]
            vec_ref[0:groups, :] = jnp.sum(picked, axis=1)
        else:
            vec_ref[...] = vec_in[...]
        for h in range(2):
            for part, row in ((0, 0), (2, 1)):
                bias[h, :, part * half_width : (part + 1) * half_width] = vec_ref[
                    row : row + 1, h * half_width : (h + 1) * half_width
                ]
            bias[h, :, half_width : 2 * half_width] = jnp.zeros((1, half_width), f32)

    @pl.when(crop == 1)
    def _():
        for weight, old, out in zip(weights, copies_in, deltas):
            out[...] = (weight[...].astype(f32) - old[...]) * 0.0005

    x = x_ref[...]
    slots = x.shape[0]
    length = info[4 + crop]
    usable = lax.broadcasted_iota(jnp.int32, (1, slots), 1) < length
    mask_row = jnp.where(usable, 0.0, -1e30).astype(f32)
    lane = lax.broadcasted_iota(jnp.int32, (1, 128), 1)
    sides = (
        jnp.where(lane < 64, 1.0, 0.0).astype(bf16),
        jnp.where(lane < 64, 0.0, 1.0).astype(bf16),
    )
    units = [(h, p, side) for h in range(2) for p in range(pairs) for side in range(2)]

    def project(h):
        qkv_ref[h] = (mm(x, w[h, :, : 3 * half_width]) + bias[h]).astype(bf16)

    def columns(h, part, p):
        lo = part * half_width + p * 128
        return qkv_ref[h, :, lo : lo + 128]

    scores, probs, first = {}, {}, None
    project(0)
    for t in range(len(units) + 4):
        if t == 3:
            project(1)
        if t < len(units):
            h, p, side = units[t]
            q2 = columns(h, 0, p) * jnp.asarray(0.125, bf16)
            scores[t] = mm_nt(q2, columns(h, 1, p) * sides[side]) + mask_row
        if 0 <= t - 3 < len(units):
            h, p, side = units[t - 3]
            value = scores.pop(t - 3)
            terms = jnp.exp(value - jnp.max(value, axis=1, keepdims=True))
            mass = jnp.sum(terms, axis=1, keepdims=True)
            rounded = (terms * (1.0 / mass)).astype(bf16)
            p_ref[h, 0, p * 2 + side] = rounded
            probs[t - 3] = rounded
        if 0 <= t - 4 < len(units):
            h, p, side = units[t - 4]
            part = mm(probs.pop(t - 4), columns(h, 2, p) * sides[side])
            if side == 0:
                first = part
            else:
                lo = h * half_width + p * 128
                a_ref[:, lo : lo + 128] = (first + part).astype(bf16)


def attention_backward(pairs, info, qkv_ref, da_ref, p_ref, out_ref, sums_ref, keep=None):
    half_width = pairs * 128
    lane = lax.broadcasted_iota(jnp.int32, (1, 128), 1)
    sides = (
        jnp.where(lane < 64, 1.0, 0.0).astype(bf16),
        jnp.where(lane < 64, 0.0, 1.0).astype(bf16),
    )

    @pl.when(pl.program_id(0) == 0)
    def _():
        sums_ref[...] = jnp.zeros_like(sums_ref)

    units = [(p, side) for p in range(pairs) for side in range(2)]

    def columns(part, p):
        lo = part * half_width + p * 128
        return qkv_ref[0, :, lo : lo + 128]

    d_probs, d_scores, total = {}, {}, None
    for t in range(len(units) + 4):
        if t < len(units):
            p, side = units[t]
            da2 = da_ref[:, p * 128 : (p + 1) * 128]
            d_probs[t] = mm_nt(da2, columns(2, p) * sides[side])
        if 0 <= t - 2 < len(units):
            p, side = units[t - 2]
            probs = p_ref[0, 0, p * 2 + side].astype(f32)
            value = d_probs.pop(t - 2)
            inner = jnp.sum(probs * value, axis=1, keepdims=True)
            d_scores[t - 2] = (probs * (value - inner)).astype(bf16)
        if 0 <= t - 4 < len(units):
            p, side = units[t - 4]
            value = d_scores.pop(t - 4)
            da2 = da_ref[:, p * 128 : (p + 1) * 128]
            parts = [
                mm(value, columns(1, p) * sides[side]) * 0.125,
                mm_tn(value, columns(0, p) * sides[side]) * 0.125,
                mm_tn(p_ref[0, 0, p * 2 + side], da2 * sides[side]),
            ]
            total = parts if side == 0 else [a + b for a, b in zip(total, parts)]
            if side == 1:
                for part in range(3):
                    lo = part * half_width + p * 128
                    rounded = total[part].astype(bf16)
                    out_ref[0, :, lo : lo + 128] = rounded
                    if keep is not None:
                        rows = pl.ds(pl.program_id(0) * rounded.shape[0], rounded.shape[0])
                        keep[part, rows, p * 128 : (p + 1) * 128] = rounded
                    if part != 1:
                        sums_ref[:, lo : lo + 128] += fold_rows(rounded.astype(f32))


def gelu_parts(u):
    size = jnp.abs(u)
    t = 1.0 / (1.0 + size * (0.3275911 * 0.7071067811865476))
    bell = jnp.exp(u * u * -0.5)
    poly = t * (
        0.127414796
        + t * (-0.142248368 + t * (0.7107068705 + t * (-0.7265760135 + t * 0.5307027145)))
    )
    tail = poly * bell
    cdf = jnp.where(u < 0.0, tail, 1.0 - tail)
    return u * cdf, cdf + u * (bell * 0.3989422804014327)


def feed_stages(cut, vec_ref, ins, outs, sums_ref, slope, wa, wb):
    x_ref, a_ref, cot_ref = ins
    out_ref, g_ref, du_ref, n1_ref, df_ref, db_ref, da_ref, dr1_ref = outs
    width = x_ref.shape[1]
    half = width // 2
    place = lambda j: (j // 2, (j % 2) * width)

    attended = a_ref[cut, :]
    branch = jnp.concatenate(
        [mm(attended, wa[h, :, :half]) for h in range(2)], axis=1
    ) + vec_ref[2:3, :]
    yield
    resid = x_ref[cut, :].astype(f32) + branch
    center = resid - row_mean(resid)
    rstd = lax.rsqrt(row_mean(center * center) + EPS)
    z1 = center * rstd
    n1 = z1 * (1.0 + vec_ref[3:4, :]) + vec_ref[4:5, :]
    n1b = n1.astype(bf16)
    n1_ref[cut, :] = n1b
    yield

    def up(j):
        h, lo = place(j)
        return mm(n1b, wa[h, :, half + lo : half + lo + width]) + vec_ref[8 + j : 9 + j, :]

    hidden = [up(0)]
    yield
    feed = None
    for j in range(4):
        if j < 3:
            hidden.append(up(j + 1))
            yield
        active, tilt = gelu_parts(hidden[j])
        hidden[j] = None
        active = active.astype(bf16)
        at = slice(j * width, (j + 1) * width)
        g_ref[cut, at] = active
        slope[cut, at] = tilt
        yield
        h, lo = place(j)
        part = mm_nt(active, wb[h, :, lo : lo + width])
        feed = part if feed is None else feed + part
        yield
    resid2 = n1 + feed + vec_ref[7:8, :]
    center2 = resid2 - row_mean(resid2)
    rstd2 = lax.rsqrt(row_mean(center2 * center2) + EPS)
    z2 = center2 * rstd2
    gain2 = 1.0 + vec_ref[5:6, :]
    out_ref[cut, :] = (z2 * gain2 + vec_ref[6:7, :]).astype(bf16)
    dy = cot_ref[cut, :].astype(f32)
    s = dy * gain2
    dr2 = rstd2 * (s - row_mean(s) - z2 * row_mean(s * z2))
    df = dr2.astype(bf16)
    df_ref[cut, :] = df
    sums_ref[3] += fold_rows(dy * z2)
    sums_ref[4] += fold_rows(dy)
    sums_ref[5] += fold_rows(df.astype(f32))
    yield

    def back(j):
        h, lo = place(j)
        return mm(df, wb[h, :, lo : lo + width])

    d_active = [back(0)]
    yield
    dn1 = dr2
    for j in range(4):
        if j < 3:
            d_active.append(back(j + 1))
            yield
        at = slice(j * width, (j + 1) * width)
        du = (d_active[j] * slope[cut, at]).astype(bf16)
        d_active[j] = None
        du_ref[cut, at] = du
        sums_ref[6 + j] += fold_rows(du.astype(f32))
        yield
        h, lo = place(j)
        dn1 = dn1 + mm_nt(du, wa[h, :, half + lo : half + lo + width])
        yield
    sums_ref[0] += fold_rows(dn1 * z1)
    sums_ref[1] += fold_rows(dn1)
    s = dn1 * (1.0 + vec_ref[3:4, :])
    dr1 = rstd * (s - row_mean(s) - z1 * row_mean(s * z1))
    dr1_ref[cut, :] = dr1
    db = dr1.astype(bf16)
    db_ref[cut, :] = db
    sums_ref[2] += fold_rows(db.astype(f32))
    yield
    da = mm_nt(db[:, :half], wa[0, :, :half]) + mm_nt(db[:, half:], wa[1, :, :half])
    da_ref[cut, :] = da.astype(bf16)
    yield


def feed_both(n_a, n_b, sub, info, vec_ref, x_ref, a_ref, cot_ref, *refs):
    src_a = refs[:n_a]
    src_b = refs[n_a : n_a + n_b]
    refs = refs[n_a + n_b :]
    outs = refs[:8]
    sums_ref, slope, wa, wb, sems_a, sems_b = refs[8:]
    step = pl.program_id(0)
    copies_a = weight_copies(info, src_a, wa, sems_a)
    copies_b = weight_copies(info, src_b, wb, sems_b, Z_LAST)

    @pl.when(step == 0)
    def _():
        for copy in copies_a + copies_b:
            copy.start()
        sums_ref[...] = jnp.zeros_like(sums_ref)
        for copy in copies_a + copies_b:
            copy.wait()

    ins = (x_ref, a_ref, cot_ref)
    blocks = [
        feed_stages(slice(r, r + sub), vec_ref, ins, outs, sums_ref, slope, wa, wb)
        for r in range(0, x_ref.shape[0], sub)
    ]
    waiting, t = list(range(len(blocks))), 0
    while waiting:
        for i in list(waiting):
            if t >= i and next(blocks[i], True):
                waiting.remove(i)
        t += 1


def token_gradient(n_src, info, other_ref, mine_ref, dr1_ref, *refs):
    src = refs[:n_src]
    out_ref, w, sems = refs[n_src:]
    used = mine_ref.shape[2]

    @pl.when(pl.program_id(0) == 0)
    def _():
        copies = weight_copies(info, src, w, sems)
        for copy in copies:
            copy.start()
        for copy in copies:
            copy.wait()

    out_ref[...] = (
        dr1_ref[...]
        + mm_nt(other_ref[0], w[1 - info[0], :, :used])
        + mm_nt(mine_ref[0], w[info[0], :, :used])
    )


def vector_rows(info, sums_ref, other_ref, mine_ref):
    total = lambda v: jnp.sum(v, axis=0, keepdims=True)
    half = other_ref.shape[1] // 3
    rows = []
    for part in (0, 2):
        cut = slice(part * half, (part + 1) * half)
        other, mine = total(other_ref[:, cut]), total(mine_ref[:, cut])
        first = jnp.where(info[0] == 0, mine, other)
        second = jnp.where(info[0] == 0, other, mine)
        rows.append(jnp.concatenate([first, second], axis=1))
    return rows + [total(sums_ref[i]) for i in (2, 0, 1, 3, 4, 5, 6, 7, 8, 9)]


RELAYED = (
    [(0, k) for k in range(4)],
    [(3, 0), (3, 1), (1, 0), (1, 1)],
    [(3, 2), (3, 3), (2, 2), (2, 3)],
    [(1, 2), (1, 3)],
    [(2, 0), (2, 1)],
)


def store_parts(info, value, outs, acc, recv, buffers):
    size = value.shape[1]
    if buffers is None:
        outs[0][:, :size] = value.astype(outs[0].dtype)
        return
    acc[:, :size] = value
    for out, slots in zip(outs, buffers):
        for j, (a, k) in enumerate(slots):
            row = chip_row(info, a, k, True)
            mine = acc[pl.ds(row, 48), :size]
            if recv is not None:
                mine = mine + recv[pl.ds(row, 48), :size].astype(f32)
            out[j, :, :size] = mine.astype(bf16)


def attention_weight(pairs, crops, buffers, info, qkv_ref, da_ref, p_ref, x_ref, *refs):
    if buffers is not None:
        recv, all_sums_ref, other_ref, spread_ref, pick_ref, *refs = refs
    out_ref, sums_ref, *outs, keep, acc, left, sem = refs
    step = pl.program_id(0)
    tokens_copy = pltpu.make_async_copy(x_ref, left, sem)

    @pl.when(step == 0)
    def _():
        tokens_copy.start()

    @pl.when(step == crops)
    def _():
        tokens_copy.wait()

    @pl.when(step < crops)
    def _():
        attention_backward(pairs, info, qkv_ref, da_ref, p_ref, out_ref, sums_ref, keep)

    @pl.when((step >= crops) & (step < crops + 3))
    def _():
        value = mm_tn(left[...], keep[jnp.clip(step - crops, 0, 2)])
        store_parts(info, value, outs, acc, None if buffers is None else recv, buffers)

    if buffers is not None:

        @pl.when(step == crops + 3)
        def _():
            rows = vector_rows(info, all_sums_ref, other_ref, sums_ref)
            picked = jnp.concatenate([(r * pick_ref[...]).astype(bf16) for r in rows], axis=0)
            store_parts(info, mm_nt(picked, spread_ref[...]), outs, acc, None, buffers)


def weight_gradient(starts, sizes, has_recv, buffers, info, *refs):
    count = len(starts)
    lhs = refs[:count]
    rhs = refs[count : 2 * count]
    at = 2 * count
    recv = None
    if has_recv:
        recv = refs[at]
        at += 1
    (*outs, acc, left, sems) = refs[at:]
    step = pl.program_id(0)
    if recv is None:
        copies = [
            pltpu.make_async_copy(lhs[number], left.at[number], sems.at[number])
            for number in range(count)
        ]

        @pl.when(step == 0)
        def _():
            for copy in copies:
                copy.start()

        for number, start in enumerate(starts):

            @pl.when(step == start)
            def _(number=number):
                copies[number].wait()

    for number, start in enumerate(starts):
        here = step >= start
        if number + 1 < count:
            here = here & (step < starts[number + 1])

        @pl.when(here)
        def _(number=number):
            right = rhs[number]
            right = right[0] if len(right.shape) == 3 else right[...]
            value = mm_tn(left[number] if recv is None else lhs[number][...], right)
            store_parts(info, value, outs, acc, recv, buffers)


def params():
    return pltpu.CompilerParams(
        dimension_semantics=("arbitrary",), vmem_limit_bytes=VMEM_LIMIT
    )


def call(kernel, grid, in_specs, out_specs, out_shape, scratch, flops, nbytes, name, after=()):
    def body(info, *refs):
        kernel(info, *refs[len(after) :])

    run = pl.pallas_call(
        body,
        grid_spec=pltpu.PrefetchScalarGridSpec(
            num_scalar_prefetch=1,
            grid=grid,
            in_specs=[ANY] * len(after) + in_specs,
            out_specs=out_specs,
            scratch_shapes=scratch,
        ),
        out_shape=out_shape,
        compiler_params=params(),
        cost_estimate=pl.CostEstimate(
            flops=int(flops * COST), bytes_accessed=int(nbytes * COST), transcendentals=0
        ),
        name=name,
    )
    return lambda info, *operands: run(info, *after, *operands)


def struct(shape, dtype):
    return jax.ShapeDtypeStruct(shape, dtype)


def whole_block(shape):
    return pl.BlockSpec(shape, lambda i, info: (0,) * len(shape))


def rows_block(rows, columns):
    return pl.BlockSpec((rows, columns), lambda i, info: (i, 0))


def spread_tables(width):
    per = width // 64
    e = np.arange(width)
    spread = (np.arange(EXT)[:, None] == (e % per)[None, :]).astype(np.float32)
    pick = (np.arange(64)[:, None] == (e // per)[None, :]).astype(np.float32)
    return spread, pick


def run_attention_forward(info, x, weights, copies, pieces, vec, crops, after):
    rows, width = x.shape
    slots = rows // crops
    half = width // 2
    w_columns = pieces[0].shape[-1]
    has_ext = vec is None
    pairs = half // 128
    if has_ext:
        spread, pick = spread_tables(width)
        extra = [jnp.asarray(spread, bf16), jnp.asarray(pick, f32)]
    else:
        extra = [vec]
    extra_specs = [whole_block(e.shape) for e in extra]
    kernel = functools.partial(attention_forward, len(pieces), has_ext, pairs)
    return call(
        kernel,
        (crops,),
        [rows_block(slots, width)]
        + [whole_block(w.shape) for w in weights + copies]
        + [ANY] * len(pieces)
        + extra_specs,
        [
            whole_block((16, width)),
            pl.BlockSpec((2, slots, 3 * half), lambda i, info: (0, i, 0)),
            pl.BlockSpec((2, 1, H // 2, slots, slots), lambda i, info: (0, i, 0, 0, 0)),
            rows_block(slots, width),
        ]
        + [whole_block(w.shape) for w in weights],
        [
            struct((16, width), f32),
            struct((2, rows, 3 * half), bf16),
            struct((2, crops, H // 2, slots, slots), bf16),
            struct((rows, width), bf16),
        ]
        + [struct(w.shape, f32) for w in weights],
        [
            pltpu.VMEM((2, width, w_columns), bf16),
            pltpu.VMEM((2, 1, 3 * half), f32),
            pltpu.SemaphoreType.DMA((sem_count(pieces),)),
        ],
        2 * rows * width * 3 * width + 8 * rows * slots * width,
        30e6,
        "attention_forward",
        after,
    )(info, x, *weights, *copies, *pieces, *extra)


def run_attention_backward(info, qkv, da, probs, crops, which, after):
    _, rows, columns = qkv.shape
    slots = rows // crops
    half = columns // 3

    def pick(info):
        return info[0] if which else 1 - info[0]

    kernel = functools.partial(attention_backward, half // 128)
    return call(
        kernel,
        (crops,),
        [
            pl.BlockSpec((1, slots, columns), lambda i, info: (pick(info), i, 0)),
            pl.BlockSpec((slots, half), lambda i, info: (i, pick(info))),
            pl.BlockSpec(
                (1, 1, H // 2, slots, slots), lambda i, info: (pick(info), i, 0, 0, 0)
            ),
        ],
        [
            pl.BlockSpec((1, slots, columns), lambda i, info: (0, i, 0)),
            whole_block((8, columns)),
        ],
        [struct((1, rows, columns), bf16), struct((8, columns), f32)],
        [],
        16 * rows * slots * half,
        12e6,
        "attention_backward",
        after,
    )(info, qkv, da, probs)


def run_attention_weight(info, qkv, da, probs, x, crops, which, more, after):
    _, rows, columns = qkv.shape
    width = x.shape[1]
    slots = rows // crops
    half = columns // 3
    pick = lambda info: info[0] if which else 1 - info[0]
    crop = lambda i: jnp.minimum(i, crops - 1)
    part = lambda i, last: jnp.clip(i - crops, 0, last)
    in_specs = [
        pl.BlockSpec((1, slots, columns), lambda i, info: (pick(info), crop(i), 0)),
        pl.BlockSpec((slots, half), lambda i, info: (crop(i), pick(info))),
        pl.BlockSpec(
            (1, 1, H // 2, slots, slots), lambda i, info: (pick(info), crop(i), 0, 0, 0)
        ),
        ANY,
    ]
    operands = [qkv, da, probs, x]
    out_specs = [
        pl.BlockSpec((1, slots, columns), lambda i, info: (0, crop(i), 0)),
        whole_block((8, columns)),
    ]
    out_shape = [struct((1, rows, columns), bf16), struct((8, columns), f32)]
    if which:
        recv, sums, other = more
        spread, pick_rows = spread_tables(width)
        rest = [sums, other, jnp.asarray(spread, bf16), jnp.asarray(pick_rows, f32)]
        operands += [recv] + rest
        in_specs.append(pl.BlockSpec((width, half), lambda i, info: (0, part(i, 2))))
        in_specs += [whole_block(v.shape) for v in rest]
        out_specs += [
            pl.BlockSpec((len(b), 48, half), lambda i, info: (0, 0, part(i, 3))) for b in RELAYED
        ]
        out_shape += [struct((len(b), 48, columns + EXT), bf16) for b in RELAYED]
    else:
        out_specs.append(pl.BlockSpec((width, half), lambda i, info: (0, part(i, 2))))
        out_shape.append(struct((width, columns), bf16))
    kernel = functools.partial(attention_weight, half // 128, crops, RELAYED if which else None)
    out = call(
        kernel,
        (crops + 3 + which,),
        in_specs,
        out_specs,
        out_shape,
        [
            pltpu.VMEM((3, rows, half), bf16),
            pltpu.VMEM((width, half), f32),
            pltpu.VMEM((rows, width), bf16),
            pltpu.SemaphoreType.DMA,
        ],
        16 * rows * slots * half + 2 * rows * width * columns,
        20e6,
        "attention_weight",
        after,
    )(info, *operands)
    return out[0], out[1], out[2:]


def run_feed(info, vec, x, attended, cot, pieces_a, pieces_b, block, sub, after):
    rows, width = x.shape
    ff = 2 * pieces_b[0].shape[-1]
    kernel = functools.partial(feed_both, len(pieces_a), len(pieces_b), sub)
    narrow, wide = rows_block(block, width), rows_block(block, ff)
    return call(
        kernel,
        (rows // block,),
        [whole_block(vec.shape)] + [narrow] * 3 + [ANY] * (len(pieces_a) + len(pieces_b)),
        [narrow, wide, wide] + [narrow] * 5 + [whole_block((10, 8, width))],
        [struct((rows, width), bf16), struct((rows, ff), bf16), struct((rows, ff), bf16)]
        + [struct((rows, width), bf16)] * 4
        + [struct((rows, width), f32), struct((10, 8, width), f32)],
        [
            pltpu.VMEM((block, ff), f32),
            pltpu.VMEM((2, width, pieces_a[0].shape[-1]), bf16),
            pltpu.VMEM((2, width, pieces_b[0].shape[-1]), bf16),
            pltpu.SemaphoreType.DMA((sem_count(pieces_a),)),
            pltpu.SemaphoreType.DMA((sem_count(pieces_b),)),
        ],
        4 * rows * width * (width + 2 * ff),
        53e6,
        "feed_both",
        after,
    )(info, vec, x, attended, cot, *pieces_a, *pieces_b)


def run_token_gradient(info, dqkv_by, dr1, pieces, block, after):
    rows, width = dr1.shape
    columns = dqkv_by[0].shape[2]
    kernel = functools.partial(token_gradient, len(pieces))
    return call(
        kernel,
        (rows // block,),
        [
            pl.BlockSpec((1, block, columns), lambda i, info: (0, i, 0)),
            pl.BlockSpec((1, block, columns), lambda i, info: (0, i, 0)),
            rows_block(block, width),
        ]
        + [ANY] * len(pieces),
        rows_block(block, width),
        struct((rows, width), f32),
        [
            pltpu.VMEM((2, width, pieces[0].shape[-1]), bf16),
            pltpu.SemaphoreType.DMA((sem_count(pieces),)),
        ],
        4 * rows * width * columns,
        20e6,
        "token_gradient",
        after,
    )(info, *dqkv_by, dr1, *pieces)


def run_weight_gradient(info, pairs, columns, block, pick, recv, full, after, buffers=None):
    rows, width = pairs[0][0].shape
    once = pl.Buffered(1)
    starts, sizes, step = [], [], 0
    rhs_specs = []
    for _, rhs, total, size in pairs:
        count = total // size
        starts.append(step)
        sizes.append(size)
        near = lambda i, step=step, count=count: jnp.clip(i - step, 0, count - 1)
        if rhs.ndim == 3:
            rhs_specs.append(
                pl.BlockSpec((1, rows, size), lambda i, info, near=near: (0, 0, near(i)))
            )
        else:
            rhs_specs.append(
                pl.BlockSpec(
                    (rows, size),
                    lambda i, info, near=near, count=count: (0, pick(info) * count + near(i)),
                )
            )
        step += count
    operands = [p[0] for p in pairs] + [p[1] for p in pairs]
    left = pl.BlockSpec((rows, width), lambda i, info: (0, 0), pipeline_mode=once)
    specs = [ANY if recv is None else left for _ in pairs] + rhs_specs
    if recv is not None:
        recv, base = recv
        operands.append(recv)
        last = step - 1
        specs.append(
            pl.BlockSpec((width, block), lambda i, info: (0, base + jnp.minimum(i, last)))
        )
    if recv is None:
        out_specs = [pl.BlockSpec((width, block), lambda i, info: (0, i))]
        out_shape = [struct((width, columns), f32 if full else bf16)]
    else:
        out_specs = [
            pl.BlockSpec((len(b), 48, block), lambda i, info: (0, 0, i)) for b in buffers
        ]
        out_shape = [struct((len(b), 48, columns), bf16) for b in buffers]
    kernel = functools.partial(
        weight_gradient, tuple(starts), tuple(sizes), recv is not None, buffers
    )
    return call(
        kernel,
        (step,),
        specs,
        out_specs,
        out_shape,
        [
            pltpu.VMEM((width, block), f32),
            pltpu.VMEM((len(pairs), rows, width) if recv is None else (1, 16, width), bf16),
            pltpu.SemaphoreType.DMA((len(pairs),)),
        ],
        2 * rows * width * columns,
        12e6,
        "weight_gradient",
        after,
    )(info, *operands)


def neighbours(n):
    flip = lambda bits: [(i, i ^ bits) for i in range(n)]
    shift = lambda k: [(i, (i + 8 * k) % n) for i in range(n)]
    ways = {"core": 1, "x": 2, "y": 4, "xy": 6, "z": 8, "zz": 16, "zzz": 24}
    return {way: flip(bits) for way, bits in ways.items()}, shift


def send(value, pairs):
    return lax.ppermute(value, "dp", pairs)


def chip_piece(core, first, second, n):
    flips, _ = neighbours(n)
    keep = jnp.where(core == 0, first, second)
    give = jnp.where(core == 0, second, first)
    got = send(give, flips["core"])
    return jnp.where(core == 0, jnp.concatenate([keep, got]), jnp.concatenate([got, keep]))


def along_z(piece, n):
    _, shift = neighbours(n)
    return jnp.concatenate([piece] + [send(piece, shift(k)) for k in (1, 2, 3)])


def across_relayed(base, n, *gates):
    flips, _ = neighbours(n)
    by_x, by_y = send(base, flips["x"]), send(base, flips["y"])
    by_x, by_y = lax.optimization_barrier((by_x, by_y) + gates)[:2]
    mid = base.shape[0] // 2
    return [base, by_x, by_y, send(by_x[:mid], flips["y"]), send(by_y[mid:], flips["x"])]


def across_doubling(piece, n):
    flips, _ = neighbours(n)
    for way in ("x", "y"):
        piece = jnp.concatenate([piece, send(piece, flips[way])])
    return piece


def both_cores(own, n):
    flips, _ = neighbours(n)
    return own + [send(v, flips["core"]) for v in own]


def behind(value, *others):
    return lax.optimization_barrier((value,) + others)[0]


def sum_first(chunks, n, *gates):
    flips, _ = neighbours(n)
    got = [(send(parts[1], flips["x"]), send(parts[2], flips["y"])) for parts in chunks]
    got = lax.optimization_barrier((got,) + gates)[0]
    beside = lambda values: jnp.concatenate(values, axis=2).astype(bf16)
    to_x = beside(
        [p[3].astype(f32) + got_y[:2].astype(f32) for p, (_, got_y) in zip(chunks, got)]
    )
    to_y = beside(
        [p[4].astype(f32) + got_x[:2].astype(f32) for p, (got_x, _) in zip(chunks, got)]
    )
    return got, to_x, to_y


def sum_rest(chunks, first, n, *gates):
    flips, _ = neighbours(n)
    got, to_x, to_y = first
    rest_x, rest_y = send(to_x, flips["x"]), send(to_y, flips["y"])
    got, rest_x, rest_y = lax.optimization_barrier((got, rest_x, rest_y) + gates)[:3]
    beside = lambda values: jnp.concatenate(values, axis=2)
    low = beside(
        [p[0][:2].astype(f32) + got_x[2:].astype(f32) for p, (got_x, _) in zip(chunks, got)]
    ) + rest_y.astype(f32)
    high = beside(
        [p[0][2:].astype(f32) + got_y[2:].astype(f32) for p, (_, got_y) in zip(chunks, got)]
    ) + rest_x.astype(f32)
    return [low[0]] + [v.astype(bf16) for v in (low[1], high[0], high[1])], rest_x


def share_rows(core, done, n):
    flips, _ = neighbours(n)
    rows = done.shape[0] // 2
    keep = jnp.where(core == 0, done[:rows], done[rows:])
    give = jnp.where(core == 0, done[rows:], done[:rows])
    got = send(give, flips["core"])
    return jnp.where(core == 0, keep, got), jnp.where(core == 0, got, keep)


def sum_to_owner(total, ways, n, *gates):
    flips, _ = neighbours(n)
    got = [send(value, flips[way]) for value, way in zip(total[1:], ways)]
    got = lax.optimization_barrier((got,) + gates)[0]
    return total[0] + sum(v.astype(f32) for v in got)


def sum_by_halves(total, n):
    flips, _ = neighbours(n)
    got = send(jnp.stack([total[1], total[3]]), flips["z"]).astype(f32)
    give = (total[2].astype(f32) + got[1]).astype(bf16)
    far = send(give, flips["zz"])
    return total[0] + got[0] + far.astype(f32), give, far


def halves(matrix, groups):
    size = matrix.shape[1] // groups
    cut = size // 2
    return [
        jnp.concatenate(
            [matrix[:, g * size + h * cut : g * size + (h + 1) * cut] for g in range(groups)],
            axis=1,
        )
        for h in range(2)
    ]


def join(first, second, groups):
    rows, columns = first.shape
    if groups == 1:
        return jnp.concatenate([first, second], axis=1)
    shape = (rows, groups, 1, columns // groups)
    both = jnp.concatenate([first.reshape(shape), second.reshape(shape)], axis=2)
    return both.reshape(rows, 2 * columns)


def local(
    n,
    tokens,
    lengths,
    w_qkv,
    w_out,
    w_in,
    w_down,
    vector,
    key_qkv,
    key_out,
    key_in,
    key_down,
    key_vector,
    cotangent,
):
    width = tokens.shape[1]
    half = width // 2
    ff = w_in.shape[1]
    crops = lengths.shape[0]
    near = n == 32 and w_qkv.shape[0] == 24
    me = lax.axis_index("dp").astype(jnp.int32)
    core = me & 1
    place = jnp.stack([core, (me >> 1) & 1, (me >> 2) & 1, (me >> 3) & 3])
    info = jnp.concatenate([place, lengths.astype(jnp.int32)])

    qkv_halves = halves(w_qkv, 3)
    out_halves = halves(w_out, 1)
    in_halves = halves(w_in, 1)
    down_halves = halves(w_down, 1)
    mixed = [jnp.concatenate([out_halves[h], in_halves[h]], axis=1) for h in range(2)]
    if near:
        own_rows = w_qkv.shape[0]
        ext = jnp.pad(
            vector.reshape(own_rows, vector.shape[0] // own_rows),
            ((0, 0), (0, EXT - vector.shape[0] // own_rows)),
        )
        first = [jnp.concatenate([q, ext], axis=1) for q in qkv_halves]
        base = along_z(chip_piece(core, first[0], first[1], n), n)
        layer_down = across_doubling(chip_piece(core, down_halves[0], down_halves[1], n), n)
        p_qkv = across_relayed(base, n, info)
        piece = chip_piece(core, mixed[0], mixed[1], n)
        base_mixed = along_z(behind(piece, base, layer_down), n)
        layer_down = behind(layer_down, base_mixed)
        _, shift = neighbours(n)
        down_one, down_three = send(layer_down, shift(1)), send(layer_down, shift(3))
        base_late = behind(base_mixed, *p_qkv)
        p_qkv = both_cores(lax.optimization_barrier(p_qkv), n)
        order = [base_mixed]
        vec = None
    else:
        everywhere = lambda pair: [
            lax.all_gather(jnp.stack(pair), "dp", axis=1, tiled=True)
        ]
        p_qkv, p_mixed, p_down = map(everywhere, (qkv_halves, mixed, down_halves))
        vec = lax.all_gather(vector, "dp", axis=0, tiled=True).astype(f32)
        vec = jnp.pad(vec.reshape(-1, width), ((0, 16 - vec.shape[0] // width), (0, 0)))
        order = []

    vec, qkv, probs, attended, *deltas = run_attention_forward(
        info,
        tokens,
        [w_qkv, w_out, w_in, w_down],
        [key_qkv, key_out, key_in, key_down],
        p_qkv,
        vec,
        crops,
        order,
    )
    if near:
        p_mixed = across_relayed(base_late, n, attended)
        down_one, down_three = lax.optimization_barrier((down_one, down_three, attended))[:2]
        mid = layer_down.shape[0] // 2
        p_down = [layer_down, down_one, down_three]
        p_down += [send(down_one[:mid], shift(1)), send(down_three[mid:], shift(3))]
        p_mixed[3:], p_down[3:] = lax.optimization_barrier((p_mixed[3:], p_down[3:], attended))[:2]
        p_down[:3] = [behind(v, attended) for v in p_down[:3]]
        p_down = both_cores(p_down, n)
        p_mixed = both_cores(p_mixed, n)
    output, active, du, n1, df, db, da, dr1, sums = run_feed(
        info, vec, tokens, attended, cotangent, p_mixed, p_down, 512, 256, ()
    )
    down_pairs = [(df, active, ff // 2, width)]
    mixed_pairs = [(n1, du, ff // 2, width), (attended, db, half, half)]
    if near:
        flips, _ = neighbours(n)

        def mine(pairs, columns, base, after):
            return run_weight_gradient(
                info,
                pairs,
                columns,
                width,
                lambda info: info[0],
                (got_ff, base),
                False,
                after,
                RELAYED,
            )

        away_ff = run_weight_gradient(
            info,
            down_pairs + mixed_pairs,
            half + ff,
            width,
            lambda info: 1 - info[0],
            None,
            False,
            (),
        )[0]
        got_ff = send(away_ff, flips["core"])
        dqkv_other, sums_other, (away_qkv,) = run_attention_weight(
            info, qkv, da, probs, tokens, crops, 0, None, (away_ff,)
        )
        got_qkv = send(away_qkv, flips["core"])
        parts_down = mine(down_pairs, ff // 2, 0, (sums_other,))
        parts_mixed = mine(mixed_pairs, half + ff // 2, ff // 2 // width, (parts_down[0],))
        first_down = sum_first([parts_down], n, parts_mixed[0])
        dqkv_mine, sums_mine, parts_qkv = run_attention_weight(
            info,
            qkv,
            da,
            probs,
            tokens,
            crops,
            1,
            (got_qkv, sums, sums_other),
            (parts_mixed[0],) + first_down[1:],
        )
        first_mixed = sum_first([parts_mixed], n, sums_mine)
        total_down, _ = sum_rest([parts_down], first_down, n, sums_mine)
        total_mixed, arrived = sum_rest([parts_mixed], first_mixed, n)
        first_qkv = sum_first([parts_qkv], n, arrived)
        total_qkv, _ = sum_rest([parts_qkv], first_qkv, n)
        done_down, _, _ = sum_by_halves(total_down, n)
        done_mixed, give, last = sum_by_halves(total_mixed, n)
        grad_tokens = run_token_gradient(
            info, [dqkv_other, dqkv_mine], dr1, p_qkv, 256, (total_qkv[1], give)
        )
        done_qkv = sum_to_owner(total_qkv, ("z", "zz", "zzz"), n, last, grad_tokens)
        g_down = share_rows(core, done_down, n)
        g_mixed = share_rows(core, done_mixed, n)
        g_in = [v[:, : ff // 2] for v in g_mixed]
        g_out = [v[:, ff // 2 :] for v in g_mixed]
        g_qkv = share_rows(core, done_qkv, n)
        per = vector.shape[0] // w_qkv.shape[0]
        grad_down = join(g_down[0], g_down[1], 1)
        grad_vector = (g_qkv[0] + g_qkv[1])[:, 3 * half : 3 * half + per].reshape(-1)
        g_qkv = [v[:, : 3 * half] for v in g_qkv]
    else:

        def gradient(pairs_of, columns, block):
            return [
                run_weight_gradient(
                    info, pairs_of(h), columns, block, lambda info, h=h: h, None, True, ()
                )[0]
                for h in range(2)
            ]

        info_of = lambda h: info.at[0].set(h)
        results = [
            run_attention_backward(info_of(h), qkv, da, probs, crops, 1, ()) for h in range(2)
        ]
        dqkv_by = [r[0] for r in results]
        bias_sums = jnp.stack([jnp.sum(r[1], axis=0) for r in results]).reshape(2, 3, half)
        sums = jnp.sum(sums, axis=1)
        vec_grad = jnp.concatenate(
            [bias_sums[:, 0].reshape(-1), bias_sums[:, 2].reshape(-1)]
            + [sums[i] for i in (2, 0, 1, 3, 4, 5, 6, 7, 8, 9)]
        )
        g_down = gradient(lambda h: down_pairs, ff // 2, width)
        g_mixed = gradient(lambda h: mixed_pairs, half + ff // 2, width)
        g_in = [v[:, : ff // 2] for v in g_mixed]
        g_out = [v[:, ff // 2 :] for v in g_mixed]
        grad_down = join(g_down[0], g_down[1], 1)
        g_qkv = gradient(lambda h: [(tokens, dqkv_by[h], 3 * half, half)], 3 * half, half)
        grad_vector = lax.psum_scatter(vec_grad, "dp", scatter_dimension=0, tiled=True)
        grad_tokens = run_token_gradient(info_of(1), dqkv_by, dr1, p_qkv, 256, ())
    grad_qkv = join(g_qkv[0], g_qkv[1], 3)
    grad_out = join(g_out[0], g_out[1], 1)
    grad_in = join(g_in[0], g_in[1], 1)
    if not near:
        grad_qkv, grad_out, grad_in, grad_down = (
            lax.psum_scatter(g, "dp", scatter_dimension=0, tiled=True)
            for g in (grad_qkv, grad_out, grad_in, grad_down)
        )
    return (
        output,
        grad_tokens,
        grad_qkv,
        grad_out,
        grad_in,
        grad_down,
        grad_vector,
        *deltas,
        (vector.astype(f32) - key_vector) * 0.0005,
    )


def solution(mesh):
    n = mesh.shape["dp"]
    rows, flat = P("dp", None), P("dp")
    return jax.shard_map(
        functools.partial(local, n),
        mesh=mesh,
        in_specs=(rows, flat, rows, rows, rows, rows, flat, rows, rows, rows, rows, flat, rows),
        out_specs=(rows, rows, rows, rows, rows, rows, flat, rows, rows, rows, rows, flat),
        check_vma=False,
    )
```

```python
import functools

import jax
import jax.numpy as jnp
import numpy as np
from jax import lax
from jax.experimental import pallas as pl
from jax.experimental.pallas import tpu as pltpu
from jax.sharding import PartitionSpec as P

H = 12
EPS = 1e-12
EXT = 128
bf16 = jnp.bfloat16
f32 = jnp.float32
VMEM_LIMIT = 60 * 1024 * 1024
COST = 0.001
ANY = pl.BlockSpec(memory_space=pl.ANY)

NT = (((1,), (1,)), ((), ()))
TN = (((0,), (0,)), ((), ()))


def mm(a, b):
    return jnp.dot(a, b, preferred_element_type=f32)


def mm_nt(a, b):
    return lax.dot_general(a, b, NT, preferred_element_type=f32)


def mm_tn(a, b):
    return lax.dot_general(a, b, TN, preferred_element_type=f32)


def row_mean(v):
    return jnp.mean(v, axis=-1, keepdims=True)


def fold_rows(v):
    return jnp.sum(v.reshape(v.shape[0] // 8, 8, v.shape[1]), axis=0)


def chip_row(info, a, k, flip):
    x, y, z = info[1], info[2], info[3]
    xx = x ^ (a & 1)
    yy = y ^ (a >> 1)
    zz = z ^ k if flip else (z - k + 4) & 3
    return pl.multiple_of(((zz * 2 + yy) * 2 + xx) * 48, 16)


LAYER_LAST = tuple([(a, k) for k in range(4)] for a in range(3)) + (
    [(3, 0), (3, 1)],
    [(3, 2), (3, 3)],
)
Z_LAST = tuple([(a, k) for a in range(4)] for k in (0, 1, 3)) + (
    [(0, 2), (1, 2)],
    [(2, 2), (3, 2)],
)


def weight_copies(info, refs, w, sems, places=LAYER_LAST):
    if len(refs) == 1:
        return [pltpu.make_async_copy(refs[0], w, sems.at[0])]
    out = []
    for source in range(2):
        half = info[0] if source == 0 else 1 - info[0]
        for number, slots in enumerate(places):
            ref = refs[source * len(places) + number]
            for j, (a, k) in enumerate(slots):
                row = chip_row(info, a, k, False)
                out.append(
                    pltpu.make_async_copy(
                        ref.at[pl.ds(48 * j, 48)],
                        w.at[half, pl.ds(row, 48)],
                        sems.at[len(out)],
                    )
                )
    return out


def sem_count(pieces):
    return 1 if len(pieces) == 1 else 32


def attention_forward(n_src, has_ext, pairs, info, x_ref, *refs):
    weights, copies_in, deltas = refs[:4], refs[4:8], refs[-7:-3]
    refs = refs[8:-7] + refs[-3:]
    src = refs[:n_src]
    if has_ext:
        spread_ref, pick_ref = refs[n_src : n_src + 2]
        refs = refs[n_src + 2 :]
    else:
        vec_in = refs[n_src]
        refs = refs[n_src + 1 :]
    vec_ref, qkv_ref, p_ref, a_ref, w, bias, sems = refs
    crop = pl.program_id(0)
    half_width = pairs * 128

    @pl.when(crop == 0)
    def _():
        copies = weight_copies(info, src, w, sems)
        for copy in copies:
            copy.start()
        for copy in copies:
            copy.wait()
        if has_ext:
            spread = mm(w[0, :, 3 * half_width :], spread_ref[...])
            groups = spread.shape[0] // 64
            picked = spread.reshape(groups, 64, spread.shape[1]) * pick_ref[...][None]
            vec_ref[0:groups, :] = jnp.sum(picked, axis=1)
        else:
            vec_ref[...] = vec_in[...]
        for h in range(2):
            for part, row in ((0, 0), (2, 1)):
                bias[h, :, part * half_width : (part + 1) * half_width] = vec_ref[
                    row : row + 1, h * half_width : (h + 1) * half_width
                ]
            bias[h, :, half_width : 2 * half_width] = jnp.zeros((1, half_width), f32)

    @pl.when(crop == 1)
    def _():
        for weight, old, out in zip(weights, copies_in, deltas):
            out[...] = (weight[...].astype(f32) - old[...]) * 0.0005

    x = x_ref[...]
    slots = x.shape[0]
    length = info[4 + crop]
    usable = lax.broadcasted_iota(jnp.int32, (1, slots), 1) < length
    mask_row = jnp.where(usable, 0.0, -1e30).astype(f32)
    lane = lax.broadcasted_iota(jnp.int32, (1, 128), 1)
    sides = (
        jnp.where(lane < 64, 1.0, 0.0).astype(bf16),
        jnp.where(lane < 64, 0.0, 1.0).astype(bf16),
    )
    units = [(h, p, side) for h in range(2) for p in range(pairs) for side in range(2)]

    def project(h):
        qkv_ref[h] = (mm(x, w[h, :, : 3 * half_width]) + bias[h]).astype(bf16)

    def columns(h, part, p):
        lo = part * half_width + p * 128
        return qkv_ref[h, :, lo : lo + 128]

    scores, probs, first = {}, {}, None
    project(0)
    for t in range(len(units) + 4):
        if t == 3:
            project(1)
        if t < len(units):
            h, p, side = units[t]
            q2 = columns(h, 0, p) * jnp.asarray(0.125, bf16)
            scores[t] = mm_nt(q2, columns(h, 1, p) * sides[side]) + mask_row
        if 0 <= t - 3 < len(units):
            h, p, side = units[t - 3]
            value = scores.pop(t - 3)
            terms = jnp.exp(value - jnp.max(value, axis=1, keepdims=True))
            mass = jnp.sum(terms, axis=1, keepdims=True)
            rounded = (terms * (1.0 / mass)).astype(bf16)
            p_ref[h, 0, p * 2 + side] = rounded
            probs[t - 3] = rounded
        if 0 <= t - 4 < len(units):
            h, p, side = units[t - 4]
            part = mm(probs.pop(t - 4), columns(h, 2, p) * sides[side])
            if side == 0:
                first = part
            else:
                lo = h * half_width + p * 128
                a_ref[:, lo : lo + 128] = (first + part).astype(bf16)


def attention_backward(pairs, info, qkv_ref, da_ref, p_ref, out_ref, sums_ref, keep=None):
    half_width = pairs * 128
    lane = lax.broadcasted_iota(jnp.int32, (1, 128), 1)
    sides = (
        jnp.where(lane < 64, 1.0, 0.0).astype(bf16),
        jnp.where(lane < 64, 0.0, 1.0).astype(bf16),
    )

    @pl.when(pl.program_id(0) == 0)
    def _():
        sums_ref[...] = jnp.zeros_like(sums_ref)

    units = [(p, side) for p in range(pairs) for side in range(2)]

    def columns(part, p):
        lo = part * half_width + p * 128
        return qkv_ref[0, :, lo : lo + 128]

    d_probs, d_scores, total = {}, {}, None
    for t in range(len(units) + 4):
        if t < len(units):
            p, side = units[t]
            da2 = da_ref[:, p * 128 : (p + 1) * 128]
            d_probs[t] = mm_nt(da2, columns(2, p) * sides[side])
        if 0 <= t - 2 < len(units):
            p, side = units[t - 2]
            probs = p_ref[0, 0, p * 2 + side].astype(f32)
            value = d_probs.pop(t - 2)
            inner = jnp.sum(probs * value, axis=1, keepdims=True)
            d_scores[t - 2] = (probs * (value - inner)).astype(bf16)
        if 0 <= t - 4 < len(units):
            p, side = units[t - 4]
            value = d_scores.pop(t - 4)
            da2 = da_ref[:, p * 128 : (p + 1) * 128]
            parts = [
                mm(value, columns(1, p) * sides[side]) * 0.125,
                mm_tn(value, columns(0, p) * sides[side]) * 0.125,
                mm_tn(p_ref[0, 0, p * 2 + side], da2 * sides[side]),
            ]
            total = parts if side == 0 else [a + b for a, b in zip(total, parts)]
            if side == 1:
                for part in range(3):
                    lo = part * half_width + p * 128
                    rounded = total[part].astype(bf16)
                    out_ref[0, :, lo : lo + 128] = rounded
                    if keep is not None:
                        rows = pl.ds(pl.program_id(0) * rounded.shape[0], rounded.shape[0])
                        keep[part, rows, p * 128 : (p + 1) * 128] = rounded
                    if part != 1:
                        sums_ref[:, lo : lo + 128] += fold_rows(rounded.astype(f32))


def gelu_parts(u):
    size = jnp.abs(u)
    t = 1.0 / (1.0 + size * (0.3275911 * 0.7071067811865476))
    bell = jnp.exp(u * u * -0.5)
    poly = t * (
        0.127414796
        + t * (-0.142248368 + t * (0.7107068705 + t * (-0.7265760135 + t * 0.5307027145)))
    )
    tail = poly * bell
    cdf = jnp.where(u < 0.0, tail, 1.0 - tail)
    return u * cdf, cdf + u * (bell * 0.3989422804014327)


def feed_stages(cut, vec_ref, ins, outs, sums_ref, slope, wa, wb):
    x_ref, a_ref, cot_ref = ins
    out_ref, g_ref, du_ref, n1_ref, df_ref, db_ref, da_ref, dr1_ref = outs
    width = x_ref.shape[1]
    half = width // 2
    place = lambda j: (j // 2, (j % 2) * width)

    attended = a_ref[cut, :]
    branch = jnp.concatenate(
        [mm(attended, wa[h, :, :half]) for h in range(2)], axis=1
    ) + vec_ref[2:3, :]
    yield
    resid = x_ref[cut, :].astype(f32) + branch
    center = resid - row_mean(resid)
    rstd = lax.rsqrt(row_mean(center * center) + EPS)
    z1 = center * rstd
    n1 = z1 * (1.0 + vec_ref[3:4, :]) + vec_ref[4:5, :]
    n1b = n1.astype(bf16)
    n1_ref[cut, :] = n1b
    yield

    def up(j):
        h, lo = place(j)
        return mm(n1b, wa[h, :, half + lo : half + lo + width]) + vec_ref[8 + j : 9 + j, :]

    hidden = [up(0)]
    yield
    feed = None
    for j in range(4):
        if j < 3:
            hidden.append(up(j + 1))
            yield
        active, tilt = gelu_parts(hidden[j])
        hidden[j] = None
        active = active.astype(bf16)
        at = slice(j * width, (j + 1) * width)
        g_ref[cut, at] = active
        slope[cut, at] = tilt
        yield
        h, lo = place(j)
        part = mm_nt(active, wb[h, :, lo : lo + width])
        feed = part if feed is None else feed + part
        yield
    resid2 = n1 + feed + vec_ref[7:8, :]
    center2 = resid2 - row_mean(resid2)
    rstd2 = lax.rsqrt(row_mean(center2 * center2) + EPS)
    z2 = center2 * rstd2
    gain2 = 1.0 + vec_ref[5:6, :]
    out_ref[cut, :] = (z2 * gain2 + vec_ref[6:7, :]).astype(bf16)
    dy = cot_ref[cut, :].astype(f32)
    s = dy * gain2
    dr2 = rstd2 * (s - row_mean(s) - z2 * row_mean(s * z2))
    df = dr2.astype(bf16)
    df_ref[cut, :] = df
    sums_ref[3] += fold_rows(dy * z2)
    sums_ref[4] += fold_rows(dy)
    sums_ref[5] += fold_rows(df.astype(f32))
    yield

    def back(j):
        h, lo = place(j)
        return mm(df, wb[h, :, lo : lo + width])

    d_active = [back(0)]
    yield
    dn1 = dr2
    for j in range(4):
        if j < 3:
            d_active.append(back(j + 1))
            yield
        at = slice(j * width, (j + 1) * width)
        du = (d_active[j] * slope[cut, at]).astype(bf16)
        d_active[j] = None
        du_ref[cut, at] = du
        sums_ref[6 + j] += fold_rows(du.astype(f32))
        yield
        h, lo = place(j)
        dn1 = dn1 + mm_nt(du, wa[h, :, half + lo : half + lo + width])
        yield
    sums_ref[0] += fold_rows(dn1 * z1)
    sums_ref[1] += fold_rows(dn1)
    s = dn1 * (1.0 + vec_ref[3:4, :])
    dr1 = rstd * (s - row_mean(s) - z1 * row_mean(s * z1))
    dr1_ref[cut, :] = dr1
    db = dr1.astype(bf16)
    db_ref[cut, :] = db
    sums_ref[2] += fold_rows(db.astype(f32))
    yield
    da = mm_nt(db[:, :half], wa[0, :, :half]) + mm_nt(db[:, half:], wa[1, :, :half])
    da_ref[cut, :] = da.astype(bf16)
    yield


def feed_both(n_a, n_b, sub, info, vec_ref, x_ref, a_ref, cot_ref, *refs):
    src_a = refs[:n_a]
    src_b = refs[n_a : n_a + n_b]
    refs = refs[n_a + n_b :]
    outs = refs[:8]
    sums_ref, slope, wa, wb, sems_a, sems_b = refs[8:]
    step = pl.program_id(0)
    copies_a = weight_copies(info, src_a, wa, sems_a)
    copies_b = weight_copies(info, src_b, wb, sems_b, Z_LAST)

    @pl.when(step == 0)
    def _():
        for copy in copies_a + copies_b:
            copy.start()
        sums_ref[...] = jnp.zeros_like(sums_ref)
        for copy in copies_a + copies_b:
            copy.wait()

    ins = (x_ref, a_ref, cot_ref)
    blocks = [
        feed_stages(slice(r, r + sub), vec_ref, ins, outs, sums_ref, slope, wa, wb)
        for r in range(0, x_ref.shape[0], sub)
    ]
    waiting, t = list(range(len(blocks))), 0
    while waiting:
        for i in list(waiting):
            if t >= i and next(blocks[i], True):
                waiting.remove(i)
        t += 1


def token_gradient(n_src, info, other_ref, mine_ref, dr1_ref, *refs):
    src = refs[:n_src]
    out_ref, w, sems = refs[n_src:]
    used = mine_ref.shape[2]

    @pl.when(pl.program_id(0) == 0)
    def _():
        copies = weight_copies(info, src, w, sems)
        for copy in copies:
            copy.start()
        for copy in copies:
            copy.wait()

    out_ref[...] = (
        dr1_ref[...]
        + mm_nt(other_ref[0], w[1 - info[0], :, :used])
        + mm_nt(mine_ref[0], w[info[0], :, :used])
    )


def vector_rows(info, sums_ref, other_ref, mine_ref):
    total = lambda v: jnp.sum(v, axis=0, keepdims=True)
    half = other_ref.shape[1] // 3
    rows = []
    for part in (0, 2):
        cut = slice(part * half, (part + 1) * half)
        other, mine = total(other_ref[:, cut]), total(mine_ref[:, cut])
        first = jnp.where(info[0] == 0, mine, other)
        second = jnp.where(info[0] == 0, other, mine)
        rows.append(jnp.concatenate([first, second], axis=1))
    return rows + [total(sums_ref[i]) for i in (2, 0, 1, 3, 4, 5, 6, 7, 8, 9)]


RELAYED = (
    [(0, k) for k in range(4)],
    [(3, 0), (3, 1), (1, 0), (1, 1)],
    [(3, 2), (3, 3), (2, 2), (2, 3)],
    [(1, 2), (1, 3)],
    [(2, 0), (2, 1)],
)


def store_parts(info, value, outs, acc, recv, buffers):
    size = value.shape[1]
    if buffers is None:
        outs[0][:, :size] = value.astype(outs[0].dtype)
        return
    acc[:, :size] = value
    for out, slots in zip(outs, buffers):
        for j, (a, k) in enumerate(slots):
            row = chip_row(info, a, k, True)
            mine = acc[pl.ds(row, 48), :size]
            if recv is not None:
                mine = mine + recv[pl.ds(row, 48), :size].astype(f32)
            out[j, :, :size] = mine.astype(bf16)


def attention_weight(pairs, crops, buffers, info, qkv_ref, da_ref, p_ref, x_ref, *refs):
    if buffers is not None:
        recv, all_sums_ref, other_ref, spread_ref, pick_ref, *refs = refs
    out_ref, sums_ref, *outs, keep, acc, left, sem = refs
    step = pl.program_id(0)
    tokens_copy = pltpu.make_async_copy(x_ref, left, sem)

    @pl.when(step == 0)
    def _():
        tokens_copy.start()

    @pl.when(step == crops)
    def _():
        tokens_copy.wait()

    @pl.when(step < crops)
    def _():
        attention_backward(pairs, info, qkv_ref, da_ref, p_ref, out_ref, sums_ref, keep)

    @pl.when((step >= crops) & (step < crops + 3))
    def _():
        value = mm_tn(left[...], keep[jnp.clip(step - crops, 0, 2)])
        store_parts(info, value, outs, acc, None if buffers is None else recv, buffers)

    if buffers is not None:

        @pl.when(step == crops + 3)
        def _():
            rows = vector_rows(info, all_sums_ref, other_ref, sums_ref)
            picked = jnp.concatenate([(r * pick_ref[...]).astype(bf16) for r in rows], axis=0)
            store_parts(info, mm_nt(picked, spread_ref[...]), outs, acc, None, buffers)


def weight_gradient(starts, sizes, has_recv, buffers, info, *refs):
    count = len(starts)
    lhs = refs[:count]
    rhs = refs[count : 2 * count]
    at = 2 * count
    recv = None
    if has_recv:
        recv = refs[at]
        at += 1
    (*outs, acc, left, sems) = refs[at:]
    step = pl.program_id(0)
    if recv is None:
        copies = [
            pltpu.make_async_copy(lhs[number], left.at[number], sems.at[number])
            for number in range(count)
        ]

        @pl.when(step == 0)
        def _():
            for copy in copies:
                copy.start()

        for number, start in enumerate(starts):

            @pl.when(step == start)
            def _(number=number):
                copies[number].wait()

    for number, start in enumerate(starts):
        here = step >= start
        if number + 1 < count:
            here = here & (step < starts[number + 1])

        @pl.when(here)
        def _(number=number):
            right = rhs[number]
            right = right[0] if len(right.shape) == 3 else right[...]
            value = mm_tn(left[number] if recv is None else lhs[number][...], right)
            store_parts(info, value, outs, acc, recv, buffers)


def params():
    return pltpu.CompilerParams(
        dimension_semantics=("arbitrary",), vmem_limit_bytes=VMEM_LIMIT
    )


def call(kernel, grid, in_specs, out_specs, out_shape, scratch, flops, nbytes, name, after=()):
    def body(info, *refs):
        kernel(info, *refs[len(after) :])

    run = pl.pallas_call(
        body,
        grid_spec=pltpu.PrefetchScalarGridSpec(
            num_scalar_prefetch=1,
            grid=grid,
            in_specs=[ANY] * len(after) + in_specs,
            out_specs=out_specs,
            scratch_shapes=scratch,
        ),
        out_shape=out_shape,
        compiler_params=params(),
        cost_estimate=pl.CostEstimate(
            flops=int(flops * COST), bytes_accessed=int(nbytes * COST), transcendentals=0
        ),
        name=name,
    )
    return lambda info, *operands: run(info, *after, *operands)


def struct(shape, dtype):
    return jax.ShapeDtypeStruct(shape, dtype)


def whole_block(shape):
    return pl.BlockSpec(shape, lambda i, info: (0,) * len(shape))


def rows_block(rows, columns):
    return pl.BlockSpec((rows, columns), lambda i, info: (i, 0))


def spread_tables(width):
    per = width // 64
    e = np.arange(width)
    spread = (np.arange(EXT)[:, None] == (e % per)[None, :]).astype(np.float32)
    pick = (np.arange(64)[:, None] == (e // per)[None, :]).astype(np.float32)
    return spread, pick


def run_attention_forward(info, x, weights, copies, pieces, vec, crops, after):
    rows, width = x.shape
    slots = rows // crops
    half = width // 2
    w_columns = pieces[0].shape[-1]
    has_ext = vec is None
    pairs = half // 128
    if has_ext:
        spread, pick = spread_tables(width)
        extra = [jnp.asarray(spread, bf16), jnp.asarray(pick, f32)]
    else:
        extra = [vec]
    extra_specs = [whole_block(e.shape) for e in extra]
    kernel = functools.partial(attention_forward, len(pieces), has_ext, pairs)
    return call(
        kernel,
        (crops,),
        [rows_block(slots, width)]
        + [whole_block(w.shape) for w in weights + copies]
        + [ANY] * len(pieces)
        + extra_specs,
        [
            whole_block((16, width)),
            pl.BlockSpec((2, slots, 3 * half), lambda i, info: (0, i, 0)),
            pl.BlockSpec((2, 1, H // 2, slots, slots), lambda i, info: (0, i, 0, 0, 0)),
            rows_block(slots, width),
        ]
        + [whole_block(w.shape) for w in weights],
        [
            struct((16, width), f32),
            struct((2, rows, 3 * half), bf16),
            struct((2, crops, H // 2, slots, slots), bf16),
            struct((rows, width), bf16),
        ]
        + [struct(w.shape, f32) for w in weights],
        [
            pltpu.VMEM((2, width, w_columns), bf16),
            pltpu.VMEM((2, 1, 3 * half), f32),
            pltpu.SemaphoreType.DMA((sem_count(pieces),)),
        ],
        2 * rows * width * 3 * width + 8 * rows * slots * width,
        30e6,
        "attention_forward",
        after,
    )(info, x, *weights, *copies, *pieces, *extra)


def run_attention_backward(info, qkv, da, probs, crops, which, after):
    _, rows, columns = qkv.shape
    slots = rows // crops
    half = columns // 3

    def pick(info):
        return info[0] if which else 1 - info[0]

    kernel = functools.partial(attention_backward, half // 128)
    return call(
        kernel,
        (crops,),
        [
            pl.BlockSpec((1, slots, columns), lambda i, info: (pick(info), i, 0)),
            pl.BlockSpec((slots, half), lambda i, info: (i, pick(info))),
            pl.BlockSpec(
                (1, 1, H // 2, slots, slots), lambda i, info: (pick(info), i, 0, 0, 0)
            ),
        ],
        [
            pl.BlockSpec((1, slots, columns), lambda i, info: (0, i, 0)),
            whole_block((8, columns)),
        ],
        [struct((1, rows, columns), bf16), struct((8, columns), f32)],
        [],
        16 * rows * slots * half,
        12e6,
        "attention_backward",
        after,
    )(info, qkv, da, probs)


def run_attention_weight(info, qkv, da, probs, x, crops, which, more, after):
    _, rows, columns = qkv.shape
    width = x.shape[1]
    slots = rows // crops
    half = columns // 3
    pick = lambda info: info[0] if which else 1 - info[0]
    crop = lambda i: jnp.minimum(i, crops - 1)
    part = lambda i, last: jnp.clip(i - crops, 0, last)
    in_specs = [
        pl.BlockSpec((1, slots, columns), lambda i, info: (pick(info), crop(i), 0)),
        pl.BlockSpec((slots, half), lambda i, info: (crop(i), pick(info))),
        pl.BlockSpec(
            (1, 1, H // 2, slots, slots), lambda i, info: (pick(info), crop(i), 0, 0, 0)
        ),
        ANY,
    ]
    operands = [qkv, da, probs, x]
    out_specs = [
        pl.BlockSpec((1, slots, columns), lambda i, info: (0, crop(i), 0)),
        whole_block((8, columns)),
    ]
    out_shape = [struct((1, rows, columns), bf16), struct((8, columns), f32)]
    if which:
        recv, sums, other = more
        spread, pick_rows = spread_tables(width)
        rest = [sums, other, jnp.asarray(spread, bf16), jnp.asarray(pick_rows, f32)]
        operands += [recv] + rest
        in_specs.append(pl.BlockSpec((width, half), lambda i, info: (0, part(i, 2))))
        in_specs += [whole_block(v.shape) for v in rest]
        out_specs += [
            pl.BlockSpec((len(b), 48, half), lambda i, info: (0, 0, part(i, 3))) for b in RELAYED
        ]
        out_shape += [struct((len(b), 48, columns + EXT), bf16) for b in RELAYED]
    else:
        out_specs.append(pl.BlockSpec((width, half), lambda i, info: (0, part(i, 2))))
        out_shape.append(struct((width, columns), bf16))
    kernel = functools.partial(attention_weight, half // 128, crops, RELAYED if which else None)
    out = call(
        kernel,
        (crops + 3 + which,),
        in_specs,
        out_specs,
        out_shape,
        [
            pltpu.VMEM((3, rows, half), bf16),
            pltpu.VMEM((width, half), f32),
            pltpu.VMEM((rows, width), bf16),
            pltpu.SemaphoreType.DMA,
        ],
        16 * rows * slots * half + 2 * rows * width * columns,
        20e6,
        "attention_weight",
        after,
    )(info, *operands)
    return out[0], out[1], out[2:]


def run_feed(info, vec, x, attended, cot, pieces_a, pieces_b, block, sub, after):
    rows, width = x.shape
    ff = 2 * pieces_b[0].shape[-1]
    kernel = functools.partial(feed_both, len(pieces_a), len(pieces_b), sub)
    narrow, wide = rows_block(block, width), rows_block(block, ff)
    return call(
        kernel,
        (rows // block,),
        [whole_block(vec.shape)] + [narrow] * 3 + [ANY] * (len(pieces_a) + len(pieces_b)),
        [narrow, wide, wide] + [narrow] * 5 + [whole_block((10, 8, width))],
        [struct((rows, width), bf16), struct((rows, ff), bf16), struct((rows, ff), bf16)]
        + [struct((rows, width), bf16)] * 4
        + [struct((rows, width), f32), struct((10, 8, width), f32)],
        [
            pltpu.VMEM((block, ff), f32),
            pltpu.VMEM((2, width, pieces_a[0].shape[-1]), bf16),
            pltpu.VMEM((2, width, pieces_b[0].shape[-1]), bf16),
            pltpu.SemaphoreType.DMA((sem_count(pieces_a),)),
            pltpu.SemaphoreType.DMA((sem_count(pieces_b),)),
        ],
        4 * rows * width * (width + 2 * ff),
        53e6,
        "feed_both",
        after,
    )(info, vec, x, attended, cot, *pieces_a, *pieces_b)


def run_token_gradient(info, dqkv_by, dr1, pieces, block, after):
    rows, width = dr1.shape
    columns = dqkv_by[0].shape[2]
    kernel = functools.partial(token_gradient, len(pieces))
    return call(
        kernel,
        (rows // block,),
        [
            pl.BlockSpec((1, block, columns), lambda i, info: (0, i, 0)),
            pl.BlockSpec((1, block, columns), lambda i, info: (0, i, 0)),
            rows_block(block, width),
        ]
        + [ANY] * len(pieces),
        rows_block(block, width),
        struct((rows, width), f32),
        [
            pltpu.VMEM((2, width, pieces[0].shape[-1]), bf16),
            pltpu.SemaphoreType.DMA((sem_count(pieces),)),
        ],
        4 * rows * width * columns,
        20e6,
        "token_gradient",
        after,
    )(info, *dqkv_by, dr1, *pieces)


def run_weight_gradient(info, pairs, columns, block, pick, recv, full, after, buffers=None):
    rows, width = pairs[0][0].shape
    once = pl.Buffered(1)
    starts, sizes, step = [], [], 0
    rhs_specs = []
    for _, rhs, total, size in pairs:
        count = total // size
        starts.append(step)
        sizes.append(size)
        near = lambda i, step=step, count=count: jnp.clip(i - step, 0, count - 1)
        if rhs.ndim == 3:
            rhs_specs.append(
                pl.BlockSpec((1, rows, size), lambda i, info, near=near: (0, 0, near(i)))
            )
        else:
            rhs_specs.append(
                pl.BlockSpec(
                    (rows, size),
                    lambda i, info, near=near, count=count: (0, pick(info) * count + near(i)),
                )
            )
        step += count
    operands = [p[0] for p in pairs] + [p[1] for p in pairs]
    left = pl.BlockSpec((rows, width), lambda i, info: (0, 0), pipeline_mode=once)
    specs = [ANY if recv is None else left for _ in pairs] + rhs_specs
    if recv is not None:
        recv, base = recv
        operands.append(recv)
        last = step - 1
        specs.append(
            pl.BlockSpec((width, block), lambda i, info: (0, base + jnp.minimum(i, last)))
        )
    if recv is None:
        out_specs = [pl.BlockSpec((width, block), lambda i, info: (0, i))]
        out_shape = [struct((width, columns), f32 if full else bf16)]
    else:
        out_specs = [
            pl.BlockSpec((len(b), 48, block), lambda i, info: (0, 0, i)) for b in buffers
        ]
        out_shape = [struct((len(b), 48, columns), bf16) for b in buffers]
    kernel = functools.partial(
        weight_gradient, tuple(starts), tuple(sizes), recv is not None, buffers
    )
    return call(
        kernel,
        (step,),
        specs,
        out_specs,
        out_shape,
        [
            pltpu.VMEM((width, block), f32),
            pltpu.VMEM((len(pairs), rows, width) if recv is None else (1, 16, width), bf16),
            pltpu.SemaphoreType.DMA((len(pairs),)),
        ],
        2 * rows * width * columns,
        12e6,
        "weight_gradient",
        after,
    )(info, *operands)


def neighbours(n):
    flip = lambda bits: [(i, i ^ bits) for i in range(n)]
    shift = lambda k: [(i, (i + 8 * k) % n) for i in range(n)]
    ways = {"core": 1, "x": 2, "y": 4, "xy": 6, "z": 8, "zz": 16, "zzz": 24}
    return {way: flip(bits) for way, bits in ways.items()}, shift


def send(value, pairs):
    return lax.ppermute(value, "dp", pairs)


def chip_piece(core, first, second, n):
    flips, _ = neighbours(n)
    keep = jnp.where(core == 0, first, second)
    give = jnp.where(core == 0, second, first)
    got = send(give, flips["core"])
    return jnp.where(core == 0, jnp.concatenate([keep, got]), jnp.concatenate([got, keep]))


def along_z(piece, n):
    _, shift = neighbours(n)
    return jnp.concatenate([piece] + [send(piece, shift(k)) for k in (1, 2, 3)])


def across_relayed(base, n, *gates):
    flips, _ = neighbours(n)
    by_x, by_y = send(base, flips["x"]), send(base, flips["y"])
    by_x, by_y = lax.optimization_barrier((by_x, by_y) + gates)[:2]
    mid = base.shape[0] // 2
    return [base, by_x, by_y, send(by_x[:mid], flips["y"]), send(by_y[mid:], flips["x"])]


def across_doubling(piece, n):
    flips, _ = neighbours(n)
    for way in ("x", "y"):
        piece = jnp.concatenate([piece, send(piece, flips[way])])
    return piece


def copy_halves(info, *refs):
    count = len(refs) // 2
    sems = refs[-1]
    copies = []
    for number in range(count):
        source, out = refs[number], refs[count + number]
        rows = out.shape[0]
        lo = (number % 2) * rows
        copies.append(
            pltpu.make_async_copy(source.at[pl.ds(lo, rows)], out, sems.at[number])
        )
    for copy in copies:
        copy.start()
    for copy in copies:
        copy.wait()


def take_halves(info, values):
    shapes = [struct((v.shape[0] // 2, v.shape[1]), v.dtype) for v in values]
    return call(
        copy_halves,
        (1,),
        [ANY] * len(values),
        [ANY] * len(values),
        shapes,
        [pltpu.SemaphoreType.DMA((len(values),))],
        0,
        3e6,
        "take_halves",
    )(info, *values)


def both_cores(own, n):
    flips, _ = neighbours(n)
    return own + [send(v, flips["core"]) for v in own]


def behind(value, *others):
    return lax.optimization_barrier((value,) + others)[0]


def sum_first(chunks, n, *gates):
    flips, _ = neighbours(n)
    got = [(send(parts[1], flips["x"]), send(parts[2], flips["y"])) for parts in chunks]
    got = lax.optimization_barrier((got,) + gates)[0]
    beside = lambda values: jnp.concatenate(values, axis=2).astype(bf16)
    to_x = beside(
        [p[3].astype(f32) + got_y[:2].astype(f32) for p, (_, got_y) in zip(chunks, got)]
    )
    to_y = beside(
        [p[4].astype(f32) + got_x[:2].astype(f32) for p, (got_x, _) in zip(chunks, got)]
    )
    return got, to_x, to_y


def sum_rest(chunks, first, n, *gates):
    flips, _ = neighbours(n)
    got, to_x, to_y = first
    rest_x, rest_y = send(to_x, flips["x"]), send(to_y, flips["y"])
    got, rest_x, rest_y = lax.optimization_barrier((got, rest_x, rest_y) + gates)[:3]
    beside = lambda values: jnp.concatenate(values, axis=2)
    low = beside(
        [p[0][:2].astype(f32) + got_x[2:].astype(f32) for p, (got_x, _) in zip(chunks, got)]
    ) + rest_y.astype(f32)
    high = beside(
        [p[0][2:].astype(f32) + got_y[2:].astype(f32) for p, (_, got_y) in zip(chunks, got)]
    ) + rest_x.astype(f32)
    return [low[0]] + [v.astype(bf16) for v in (low[1], high[0], high[1])], rest_x


def share_rows(core, done, n):
    flips, _ = neighbours(n)
    rows = done.shape[0] // 2
    keep = jnp.where(core == 0, done[:rows], done[rows:])
    give = jnp.where(core == 0, done[rows:], done[:rows])
    got = send(give, flips["core"])
    return jnp.where(core == 0, keep, got), jnp.where(core == 0, got, keep)


def sum_to_owner(total, ways, n, *gates):
    flips, _ = neighbours(n)
    got = [send(value, flips[way]) for value, way in zip(total[1:], ways)]
    got = lax.optimization_barrier((got,) + gates)[0]
    return total[0] + sum(v.astype(f32) for v in got)


def sum_by_halves(total, n):
    flips, _ = neighbours(n)
    got = send(jnp.stack([total[1], total[3]]), flips["z"]).astype(f32)
    give = (total[2].astype(f32) + got[1]).astype(bf16)
    far = send(give, flips["zz"])
    return total[0] + got[0] + far.astype(f32), give, far


def halves(matrix, groups):
    size = matrix.shape[1] // groups
    cut = size // 2
    return [
        jnp.concatenate(
            [matrix[:, g * size + h * cut : g * size + (h + 1) * cut] for g in range(groups)],
            axis=1,
        )
        for h in range(2)
    ]


def join(first, second, groups):
    rows, columns = first.shape
    if groups == 1:
        return jnp.concatenate([first, second], axis=1)
    shape = (rows, groups, 1, columns // groups)
    both = jnp.concatenate([first.reshape(shape), second.reshape(shape)], axis=2)
    return both.reshape(rows, 2 * columns)


def local(
    n,
    tokens,
    lengths,
    w_qkv,
    w_out,
    w_in,
    w_down,
    vector,
    key_qkv,
    key_out,
    key_in,
    key_down,
    key_vector,
    cotangent,
):
    width = tokens.shape[1]
    half = width // 2
    ff = w_in.shape[1]
    crops = lengths.shape[0]
    near = n == 32 and w_qkv.shape[0] == 24
    me = lax.axis_index("dp").astype(jnp.int32)
    core = me & 1
    place = jnp.stack([core, (me >> 1) & 1, (me >> 2) & 1, (me >> 3) & 3])
    info = jnp.concatenate([place, lengths.astype(jnp.int32)])

    qkv_halves = halves(w_qkv, 3)
    out_halves = halves(w_out, 1)
    in_halves = halves(w_in, 1)
    down_halves = halves(w_down, 1)
    mixed = [jnp.concatenate([out_halves[h], in_halves[h]], axis=1) for h in range(2)]
    if near:
        own_rows = w_qkv.shape[0]
        ext = jnp.pad(
            vector.reshape(own_rows, vector.shape[0] // own_rows),
            ((0, 0), (0, EXT - vector.shape[0] // own_rows)),
        )
        first = [jnp.concatenate([q, ext], axis=1) for q in qkv_halves]
        base = along_z(chip_piece(core, first[0], first[1], n), n)
        layer_down = across_doubling(chip_piece(core, down_halves[0], down_halves[1], n), n)
        p_qkv = across_relayed(base, n, info)
        piece = chip_piece(core, mixed[0], mixed[1], n)
        base_mixed = along_z(behind(piece, base, layer_down), n)
        layer_down = behind(layer_down, base_mixed)
        _, shift = neighbours(n)
        down_one, down_three = send(layer_down, shift(1)), send(layer_down, shift(3))
        base_late = behind(base_mixed, *p_qkv)
        p_qkv = both_cores(lax.optimization_barrier(p_qkv), n)
        order = [base_mixed]
        vec = None
    else:
        everywhere = lambda pair: [
            lax.all_gather(jnp.stack(pair), "dp", axis=1, tiled=True)
        ]
        p_qkv, p_mixed, p_down = map(everywhere, (qkv_halves, mixed, down_halves))
        vec = lax.all_gather(vector, "dp", axis=0, tiled=True).astype(f32)
        vec = jnp.pad(vec.reshape(-1, width), ((0, 16 - vec.shape[0] // width), (0, 0)))
        order = []

    vec, qkv, probs, attended, *deltas = run_attention_forward(
        info,
        tokens,
        [w_qkv, w_out, w_in, w_down],
        [key_qkv, key_out, key_in, key_down],
        p_qkv,
        vec,
        crops,
        order,
    )
    if near:
        flips, _ = neighbours(n)
        near_x, near_y = send(base_late, flips["x"]), send(base_late, flips["y"])
        near_x, near_y, down_one, down_three = lax.optimization_barrier(
            (near_x, near_y, down_one, down_three, attended)
        )[:4]
        cuts = take_halves(info, [near_x, near_y, down_one, down_three])
        p_mixed = [base_late, near_x, near_y, send(cuts[0], flips["y"]), send(cuts[1], flips["x"])]
        p_down = [layer_down, down_one, down_three]
        p_down += [send(cuts[2], shift(1)), send(cuts[3], shift(3))]
        p_mixed[3:], p_down[3:] = lax.optimization_barrier((p_mixed[3:], p_down[3:], attended))[:2]
        p_down[:3] = [behind(v, attended) for v in p_down[:3]]
        p_down = both_cores(p_down, n)
        p_mixed = both_cores(p_mixed, n)
    output, active, du, n1, df, db, da, dr1, sums = run_feed(
        info, vec, tokens, attended, cotangent, p_mixed, p_down, 512, 256, ()
    )
    down_pairs = [(df, active, ff // 2, width)]
    mixed_pairs = [(n1, du, ff // 2, width), (attended, db, half, half)]
    if near:
        flips, _ = neighbours(n)

        def mine(pairs, columns, base, after):
            return run_weight_gradient(
                info,
                pairs,
                columns,
                width,
                lambda info: info[0],
                (got_ff, base),
                False,
                after,
                RELAYED,
            )

        away_ff = run_weight_gradient(
            info,
            down_pairs + mixed_pairs,
            half + ff,
            width,
            lambda info: 1 - info[0],
            None,
            False,
            (),
        )[0]
        got_ff = send(away_ff, flips["core"])
        dqkv_other, sums_other, (away_qkv,) = run_attention_weight(
            info, qkv, da, probs, tokens, crops, 0, None, (away_ff,)
        )
        got_qkv = send(away_qkv, flips["core"])
        parts_down = mine(down_pairs, ff // 2, 0, (sums_other,))
        parts_mixed = mine(mixed_pairs, half + ff // 2, ff // 2 // width, (parts_down[0],))
        first_down = sum_first([parts_down], n, parts_mixed[0])
        dqkv_mine, sums_mine, parts_qkv = run_attention_weight(
            info,
            qkv,
            da,
            probs,
            tokens,
            crops,
            1,
            (got_qkv, sums, sums_other),
            (parts_mixed[0],) + first_down[1:],
        )
        first_mixed = sum_first([parts_mixed], n, sums_mine)
        total_down, _ = sum_rest([parts_down], first_down, n, sums_mine)
        total_mixed, arrived = sum_rest([parts_mixed], first_mixed, n)
        first_qkv = sum_first([parts_qkv], n, arrived)
        total_qkv, _ = sum_rest([parts_qkv], first_qkv, n)
        done_down, _, _ = sum_by_halves(total_down, n)
        done_mixed, give, last = sum_by_halves(total_mixed, n)
        grad_tokens = run_token_gradient(
            info, [dqkv_other, dqkv_mine], dr1, p_qkv, 256, (total_qkv[1], give)
        )
        done_qkv = sum_to_owner(total_qkv, ("z", "zz", "zzz"), n, last, grad_tokens)
        g_down = share_rows(core, done_down, n)
        g_mixed = share_rows(core, done_mixed, n)
        g_in = [v[:, : ff // 2] for v in g_mixed]
        g_out = [v[:, ff // 2 :] for v in g_mixed]
        g_qkv = share_rows(core, done_qkv, n)
        per = vector.shape[0] // w_qkv.shape[0]
        grad_down = join(g_down[0], g_down[1], 1)
        grad_vector = (g_qkv[0] + g_qkv[1])[:, 3 * half : 3 * half + per].reshape(-1)
        g_qkv = [v[:, : 3 * half] for v in g_qkv]
    else:

        def gradient(pairs_of, columns, block):
            return [
                run_weight_gradient(
                    info, pairs_of(h), columns, block, lambda info, h=h: h, None, True, ()
                )[0]
                for h in range(2)
            ]

        info_of = lambda h: info.at[0].set(h)
        results = [
            run_attention_backward(info_of(h), qkv, da, probs, crops, 1, ()) for h in range(2)
        ]
        dqkv_by = [r[0] for r in results]
        bias_sums = jnp.stack([jnp.sum(r[1], axis=0) for r in results]).reshape(2, 3, half)
        sums = jnp.sum(sums, axis=1)
        vec_grad = jnp.concatenate(
            [bias_sums[:, 0].reshape(-1), bias_sums[:, 2].reshape(-1)]
            + [sums[i] for i in (2, 0, 1, 3, 4, 5, 6, 7, 8, 9)]
        )
        g_down = gradient(lambda h: down_pairs, ff // 2, width)
        g_mixed = gradient(lambda h: mixed_pairs, half + ff // 2, width)
        g_in = [v[:, : ff // 2] for v in g_mixed]
        g_out = [v[:, ff // 2 :] for v in g_mixed]
        grad_down = join(g_down[0], g_down[1], 1)
        g_qkv = gradient(lambda h: [(tokens, dqkv_by[h], 3 * half, half)], 3 * half, half)
        grad_vector = lax.psum_scatter(vec_grad, "dp", scatter_dimension=0, tiled=True)
        grad_tokens = run_token_gradient(info_of(1), dqkv_by, dr1, p_qkv, 256, ())
    grad_qkv = join(g_qkv[0], g_qkv[1], 3)
    grad_out = join(g_out[0], g_out[1], 1)
    grad_in = join(g_in[0], g_in[1], 1)
    if not near:
        grad_qkv, grad_out, grad_in, grad_down = (
            lax.psum_scatter(g, "dp", scatter_dimension=0, tiled=True)
            for g in (grad_qkv, grad_out, grad_in, grad_down)
        )
    return (
        output,
        grad_tokens,
        grad_qkv,
        grad_out,
        grad_in,
        grad_down,
        grad_vector,
        *deltas,
        (vector.astype(f32) - key_vector) * 0.0005,
    )


def solution(mesh):
    n = mesh.shape["dp"]
    rows, flat = P("dp", None), P("dp")
    return jax.shard_map(
        functools.partial(local, n),
        mesh=mesh,
        in_specs=(rows, flat, rows, rows, rows, rows, flat, rows, rows, rows, rows, flat, rows),
        out_specs=(rows, rows, rows, rows, rows, rows, flat, rows, rows, rows, rows, flat),
        check_vma=False,
    )
```
